128 devices in a mesh: dp: 8 (over x, core), mem: 16 (over z, y).
Axes of the slice: x: 4, y: 4, z: 4, core: 2. Of those that a mesh axis runs over, the one named last changes fastest.
Arguments:
- tokens: bfloat16 [256, 256, 1024], P(('dp', 'mem')), may hold values from -6 to 6
- memory: bfloat16 [256, 384, 1024], P('dp', 'mem'), may hold values from -6 to 6
- cotangent: bfloat16 [256, 256, 1024], P(('dp', 'mem')), may hold values from -24 to 24
- tgt_len: int32 [256], P(('dp', 'mem')), may hold values from 128 to 256, as said below
- src_len: int32 [256], P('dp'), may hold values from 24 to 384, as said below
- self_qkv: bfloat16 [1024, 3072], P('dp'), may hold values from -0.1875 to 0.1875
- self_out: bfloat16 [1024, 1024], P('dp'), may hold values from -0.75 to 0.75
- cross_q: bfloat16 [1024, 1024], P('dp'), may hold values from -0.1875 to 0.1875
- cross_kv: bfloat16 [1024, 2048], P('dp'), may hold values from -0.1875 to 0.1875
- cross_out: bfloat16 [1024, 1024], P('dp'), may hold values from -1 to 1
- ffn_in: bfloat16 [1024, 4096], P('dp'), may hold values from -0.1875 to 0.1875
- ffn_out: bfloat16 [4096, 1024], P('dp'), may hold values from -0.09375 to 0.09375
- first_gain: bfloat16 [1024], P('dp'), may hold values from 0.5 to 1.5
- first_bias: bfloat16 [1024], P('dp'), may hold values from -1 to 1
- second_gain: bfloat16 [1024], P('dp'), may hold values from 0.5 to 1.5
- second_bias: bfloat16 [1024], P('dp'), may hold values from -1 to 1
- third_gain: bfloat16 [1024], P('dp'), may hold values from 0.5 to 1.5
- third_bias: bfloat16 [1024], P('dp'), may hold values from -1 to 1
- prefix_key: bfloat16 [30, 1024], replicated, may hold values from -6 to 6
- prefix_value: bfloat16 [30, 1024], replicated, may hold values from -6 to 6
- down_weight: bfloat16 [1024, 512], replicated, may hold values from -0.1875 to 0.1875
- down_bias: bfloat16 [512], replicated, may hold values from -3 to 3
- up_weight: bfloat16 [512, 1024], replicated, may hold values from -0.0625 to 0.0625
- up_bias: bfloat16 [1024], replicated, may hold values from -0.59765625 to 0.59765625
Outputs:
- output: bfloat16 [256, 256, 1024], P(('dp', 'mem'))
- input_grad: bfloat16 [256, 256, 1024], P(('dp', 'mem'))
- memory_grad: bfloat16 [256, 384, 1024], P('dp', 'mem')
- keyprefix_grad: float32 [30, 1024], P(None, ('dp', 'mem'))
- valueprefix_grad: float32 [30, 1024], P(None, ('dp', 'mem'))
- downweight_grad: float32 [1024, 512], P(('dp', 'mem'))
- downbias_grad: float32 [512], P(('dp', 'mem'))
- upweight_grad: float32 [512, 1024], P(None, ('dp', 'mem'))
- upbias_grad: float32 [1024], P(('dp', 'mem'))
The draws below stay inside these ranges and needn't reach their ends.
Inputs may be any that keep to these rules, and one draw needn't show every extreme that they name: `tgt_len`: sequences n with equal n // 32 and equal (n) % 2 form a group; each group holds one sequence of length 256 and another of half of 256. `src_len`: in each group as for tgt_len one sequence has 384 source positions and another has 24; short ones are more common.
All inputs are finite; a program needn't handle non-finite values.
Results may differ from the reference program's by a relative error of at most 0.023.
Values may be sent and summed in bfloat16 or wider, within the bound.
No kernel may reach another device: no remote copies, remote signals or barrier semaphores. Data moves between devices by JAX's collectives and lax.ppermute only.
A program may use at most 256 MiB of HBM per device.

```python
import jax
import jax.numpy as jnp
from jax import lax

D = 1024
HEADS = 16
HEAD_DIM = 64
FF = 4096
ADAPT = 512
PREFIX = 30
TGT = 256
SRC = 384
MICRO = 2
SEQ_DEV = 1
SEQS = 256
GROUP_SEQS = 16


def spread_lengths(key, lowest, highest, tilted):
    group_count = SEQS // (GROUP_SEQS * MICRO)
    members = GROUP_SEQS // SEQ_DEV
    shape_all = (group_count, members, MICRO, SEQ_DEV)
    first_draw = jax.random.randint(jax.random.fold_in(key, 1), shape_all, 0, highest - lowest + 1)
    second_draw = jax.random.randint(jax.random.fold_in(key, 2), shape_all, 0, highest - lowest + 1)
    offsets = jnp.minimum(first_draw, second_draw) if tilted else first_draw
    pick_shape = (group_count, 1, MICRO, 1)
    top_pick = jax.random.randint(jax.random.fold_in(key, 3), pick_shape, 0, GROUP_SEQS)
    low_pick = (top_pick + 1 + jax.random.randint(jax.random.fold_in(key, 4), pick_shape, 0, GROUP_SEQS - 1)) % GROUP_SEQS
    slot_index = jnp.arange(members)[None, :, None, None] * SEQ_DEV + jnp.arange(SEQ_DEV)[None, None, None, :]
    lengths = jnp.where(slot_index == top_pick, highest, jnp.where(slot_index == low_pick, lowest, lowest + offsets))
    return lengths.reshape(SEQS).astype(jnp.int32)


def draw_tgt_len(key, part):
    key = jax.random.fold_in(key, 17)
    return spread_lengths(key, TGT // 2, TGT, False)


def draw_src_len(key, part):
    key = jax.random.fold_in(key, 29)
    return spread_lengths(key, SRC // 16, SRC, True)


def strengthened(drawn, stream_key, source, target, blocks, factor):
    owner, partner = [(jnp.arange(drawn.shape[dim]) // (drawn.shape[dim] // blocks)).reshape([-1 if axis == dim else 1 for axis in range(drawn.ndim)]) for dim in (source, target)]
    chosen = jax.random.permutation(stream_key, blocks)[partner]
    strong = (owner == chosen) | (owner == (partner + blocks // 2) % blocks)
    return jnp.where(strong, factor * drawn, drawn)


def shard_levels(key, extent, cuts, least, largest):
    level = 1.0
    for dim, shards_of in cuts:
        heights = jax.random.uniform(jax.random.fold_in(jax.random.fold_in(key, 6), dim), (shards_of,), jnp.float32, least / len(cuts), largest / len(cuts))
        level = level * jnp.repeat(jnp.exp(heights), extent[dim] // shards_of).reshape((-1,) + (1,) * (len(extent) - 1 - dim))
    return level


def noise(rng, shape, width, bound, split=(), dtype=jnp.bfloat16):
    array = width * jax.random.normal(rng, shape, jnp.float32)
    if split:
        array = array * shard_levels(rng, shape, split, -0.22, 0.18)
    return jnp.clip(array, -bound, bound).astype(dtype)


def noise_with(stream_key, extent, scale, reach, cuts, heavy, dtype=jnp.bfloat16):
    entries = scale * jax.random.normal(stream_key, extent, jnp.float32)
    if cuts:
        entries = entries * shard_levels(stream_key, extent, cuts, -0.22, 0.18)
    return jnp.clip(strengthened(entries, jax.random.fold_in(stream_key, 3), *heavy), -reach, reach).astype(dtype)


def setup_inputs(seed: int = 0) -> dict:
    key_list = jax.random.split(jax.random.key(seed), 25)
    return {
        "tokens": noise(key_list[0], (SEQS, TGT, D), 1.0, 6.0, ((0, 128),)),
        "memory": noise(key_list[1], (SEQS, SRC, D), 1.0, 6.0, ((0, 8), (1, 16))),
        "cotangent": noise_with(key_list[2], (SEQS, TGT, D), 1.0, 24.0, ((0, 128),), (0, 2, 128, 5.5)),
        "tgt_len": draw_tgt_len(jax.random.fold_in(key_list[24], 71), 0),
        "src_len": draw_src_len(jax.random.fold_in(key_list[24], 71), 0),
        "self_qkv": noise(key_list[5], (D, 3 * D), D ** -0.5, 0.1875, ((0, 8),)),
        "self_out": noise(key_list[6], (D, D), (D // 16) ** -0.5, 0.75, ((0, 8),)),
        "cross_q": noise(key_list[7], (D, D), D ** -0.5, 0.1875, ((0, 8),)),
        "cross_kv": noise(key_list[8], (D, 2 * D), D ** -0.5, 0.1875, ((0, 8),)),
        "cross_out": noise(key_list[9], (D, D), (D // 32) ** -0.5, 1.0, ((0, 8),)),
        "ffn_in": noise(key_list[10], (D, FF), D ** -0.5, 0.1875, ((0, 8),)),
        "ffn_out": noise(key_list[11], (FF, D), FF ** -0.5, 0.09375, ((0, 8),)),
        "first_gain": jnp.clip(1.0 + 0.1 * jax.random.normal(key_list[12], (D,), jnp.float32), 0.5, 1.5).astype(jnp.bfloat16),
        "first_bias": noise(key_list[13], (D,), 0.2, 1.0, ((0, 8),)),
        "second_gain": jnp.clip(1.0 + 0.1 * jax.random.normal(key_list[14], (D,), jnp.float32), 0.5, 1.5).astype(jnp.bfloat16),
        "second_bias": noise(key_list[15], (D,), 0.2, 1.0, ((0, 8),)),
        "third_gain": jnp.clip(1.0 + 0.1 * jax.random.normal(key_list[16], (D,), jnp.float32), 0.5, 1.5).astype(jnp.bfloat16),
        "third_bias": noise(key_list[17], (D,), 0.2, 1.0, ((0, 8),)),
        "prefix_key": noise(key_list[18], (PREFIX, D), 1.0, 6.0),
        "prefix_value": noise(key_list[19], (PREFIX, D), 1.0, 6.0),
        "down_weight": noise(key_list[20], (D, ADAPT), D ** -0.5, 0.1875),
        "down_bias": noise(key_list[21], (ADAPT,), 0.5, 3.0),
        "up_weight": noise(key_list[22], (ADAPT, D), (16 * ADAPT) ** -0.5, 0.0625),
        "up_bias": noise(key_list[23], (D,), 0.1, 0.59765625),
    }


NEGATIVE = -1e+30
EPSILON = 1e-05
PRECISE = lax.Precision.HIGHEST

@jax.custom_vjp
def low(v):
    return lax.optimization_barrier(v.astype(jnp.bfloat16)).astype(jnp.float32)

@jax.custom_vjp
def low_back(v):
    return v

def low_keep(v):
    return (low(v), None)

def low_pass(kept, grad):
    return (grad,)

def back_keep(v):
    return (v, None)

def back_low(kept, grad):
    return (low(grad),)
low.defvjp(low_keep, low_pass)
low_back.defvjp(back_keep, back_low)

def round_both(value_in):
    return low(low_back(value_in))

def product(left, right):
    return jnp.matmul(left, right, precision=PRECISE)

def normalize(hidden, gain, offset):
    centred = hidden - lax.optimization_barrier(jnp.mean(hidden, axis=-1, keepdims=True))
    inverse = lax.rsqrt(lax.optimization_barrier(jnp.mean(centred * centred, axis=-1, keepdims=True)) + EPSILON)
    return centred * inverse * gain + offset

def split_heads(array_in):
    return array_in.reshape(array_in.shape[:-1] + (array_in.shape[-1] // HEAD_DIM, HEAD_DIM))

def forward(tok_in, mem_in, prefix_key, prefix_value, down_weight, down_bias, up_weight, up_bias, frozen, tgt_len, src_len, fixed_shift):
    w_qkv, w_out, w_cq, w_ckv, w_cout, w_in, w_ffout, gain_one, bias_one, gain_two, bias_two, gain_three, bias_three = frozen
    seq_count, tgt_size, model_width = tok_in.shape
    prefix_size = prefix_key.shape[0]
    factor = HEAD_DIM ** (-0.5)
    positions = jnp.arange(tgt_size)
    row_valid = positions[None, :] < tgt_len[:, None]
    causal = (positions[None, :] <= positions[:, None])[None] & row_valid[:, None, :]
    visible = jnp.concatenate([jnp.ones((seq_count, tgt_size, prefix_size), jnp.bool_), causal], axis=2)
    projected = product(tok_in, w_qkv)
    self_query = split_heads(round_both(projected[..., :model_width]))
    self_key = round_both(projected[..., model_width:2 * model_width])
    self_value = round_both(projected[..., 2 * model_width:])
    key_all = split_heads(jnp.concatenate([jnp.broadcast_to(prefix_key[None], (seq_count, prefix_size, model_width)), self_key], axis=1))
    value_all = split_heads(jnp.concatenate([jnp.broadcast_to(prefix_value[None], (seq_count, prefix_size, model_width)), self_value], axis=1))
    scores = low_back(jnp.einsum('bqhd,bkhd->bhqk', self_query, key_all, precision=PRECISE) * factor)
    probs_self = jax.nn.softmax(jnp.where(visible[:, None], scores, NEGATIVE), axis=-1)
    attended = jnp.einsum('bhqk,bkhd->bqhd', low(probs_self), value_all, precision=PRECISE)
    attended = round_both(attended.reshape(seq_count, tgt_size, model_width))
    first_out = normalize(tok_in + low_back(product(attended, w_out)), gain_one, bias_one)
    cross_query = split_heads(round_both(product(low(first_out), w_cq)))
    mem_proj = product(mem_in, w_ckv)
    mem_key = split_heads(round_both(mem_proj[..., :model_width]))
    mem_value = split_heads(round_both(mem_proj[..., model_width:]))
    src_valid = (jnp.arange(mem_in.shape[1])[None, :] < src_len[:, None])[:, None, :, None]
    cross_scores = low_back(jnp.einsum('bkhd,bqhd->bhkq', mem_key, cross_query, precision=PRECISE) * factor)
    row_max = lax.optimization_barrier(jnp.max(jnp.where(src_valid, cross_scores, NEGATIVE), axis=2))
    cross_weights = jnp.exp(jnp.where(src_valid, cross_scores - fixed_shift[:, :, None, :], NEGATIVE))
    row_total = lax.optimization_barrier(jnp.sum(cross_weights, axis=2))
    numerator = low_back(jnp.einsum('bhkq,bkhd->bqhd', low(cross_weights), mem_value, precision=PRECISE))
    merged = round_both((numerator / jnp.transpose(row_total, (0, 2, 1))[..., None]).reshape(seq_count, tgt_size, model_width))
    second_out = normalize(first_out + low_back(product(merged, w_cout)), gain_two, bias_two)
    second_low = low(second_out)
    ffn_act = low(jax.nn.gelu(low_back(product(second_low, w_in)), approximate=False))
    adapt_act = low(jax.nn.gelu(low_back(product(second_low, down_weight) + down_bias), approximate=False))
    hidden_three = second_out + low_back(product(ffn_act, w_ffout)) + 4.0 * low_back(product(adapt_act, up_weight) + up_bias)
    return (normalize(hidden_three, gain_three, bias_three), row_max)

def reference(tokens, memory, cotangent, tgt_len, src_len, self_qkv, self_out, cross_q, cross_kv, cross_out, ffn_in, ffn_out, first_gain, first_bias, second_gain, second_bias, third_gain, third_bias, prefix_key, prefix_value, down_weight, down_bias, up_weight, up_bias):
    frozen = tuple((weight_in.astype(jnp.float32) for weight_in in (self_qkv, self_out, cross_q, cross_kv, cross_out, ffn_in, ffn_out, first_gain, first_bias, second_gain, second_bias, third_gain, third_bias)))
    trainable = tuple((weight_in.astype(jnp.float32) for weight_in in (prefix_key, prefix_value, down_weight, down_bias, up_weight, up_bias)))
    group_size = GROUP_SEQS
    group_count = tokens.shape[0] // group_size

    def split_groups(array_in):
        return array_in.reshape((group_count, group_size) + array_in.shape[1:])

    def scan_step(carried, batch_in):
        tok_in, mem_in, cot_in, tgt_in, src_in = batch_in
        primals = (tok_in.astype(jnp.float32), mem_in.astype(jnp.float32)) + trainable

        def run_layer(row_shift):

            def layer_fn(*inputs):
                return forward(*inputs, frozen, tgt_in, src_in, row_shift)
            return layer_fn
        zero_shift = jnp.zeros((tok_in.shape[0], HEADS, TGT), jnp.float32)
        first_pass = run_layer(zero_shift)(*primals)[1]
        result, pullback, unused_max = jax.vjp(run_layer(first_pass), *primals, has_aux=True)
        live_rows = (jnp.arange(TGT)[None, :] < tgt_in[:, None]).astype(jnp.float32)
        gradients = pullback(cot_in.astype(jnp.float32) * live_rows[..., None])
        carried = tuple((left + right for left, right in zip(carried, gradients[2:])))
        return (carried, (result.astype(jnp.bfloat16), gradients[0].astype(jnp.bfloat16), gradients[1].astype(jnp.bfloat16)))
    initial = tuple((jnp.zeros_like(weight_in) for weight_in in trainable))
    totals, (outputs, input_grads, memory_grads) = lax.scan(scan_step, initial, (split_groups(tokens), split_groups(memory), split_groups(cotangent), split_groups(tgt_len), split_groups(src_len)))
    return (outputs.reshape(tokens.shape), input_grads.reshape(tokens.shape), memory_grads.reshape(memory.shape), totals[0], totals[1], totals[2], totals[3], totals[4], totals[5])
```

```python
import functools

import jax
import jax.numpy as jnp
from jax import lax
from jax.experimental import pallas as pl
from jax.experimental.pallas import tpu as pltpu
from jax.sharding import Mesh
from jax.sharding import PartitionSpec as P

HEAD_DIM = 64
PAIR = 128
GROUP = 256
PREFIX_PAD = 32
MEM = ("mem_0", "mem_1")
DP = ("dp_0", "dp_1")
DP_MEM = ("dp_0", "dp_1", "mem_0", "mem_1")

NEGATIVE = -1e30
EPSILON = 1e-05
SCALE = HEAD_DIM ** (-0.5)
BF = jnp.bfloat16
F32 = jnp.float32
VMEM_BYTES = 60 * 1024 * 1024


def dot_nn(left, right):
    return lax.dot_general(left, right, (((1,), (0,)), ((), ())), preferred_element_type=F32)


def dot_nt(left, right):
    return lax.dot_general(left, right, (((1,), (1,)), ((), ())), preferred_element_type=F32)


def dot_tn(left, right):
    return lax.dot_general(left, right, (((0,), (0,)), ((), ())), preferred_element_type=F32)


def head_masks():
    lane = lax.broadcasted_iota(jnp.int32, (1, PAIR), 1)
    return [jnp.where((lane >= HEAD_DIM) == bool(h), 1.0, 0.0).astype(BF) for h in range(2)]


def norm_stats(hidden):
    centred = hidden - jnp.mean(hidden, axis=-1, keepdims=True)
    inverse = lax.rsqrt(jnp.mean(centred * centred, axis=-1, keepdims=True) + EPSILON)
    return centred * inverse, inverse


def norm_back(grad_in, normed, inverse, gain):
    scaled = grad_in * gain
    return inverse * (
        scaled
        - jnp.mean(scaled, axis=-1, keepdims=True)
        - normed * jnp.mean(scaled * normed, axis=-1, keepdims=True)
    )


def gelu_both(pre):
    cdf = 0.5 * (1.0 + lax.erf(pre * (0.5**0.5)))
    density = jnp.exp(-0.5 * pre * pre) * 0.3989422804014327
    return pre * cdf, cdf + pre * density


def self_forward_kernel(
    len_ref, tok_ref, wq_ref, wk_ref, wv_ref, pk_ref, pv_ref, wo_ref, wcq_ref, norm_ref,
    q_ref, k_ref, v_ref, nrm_ref, inv_ref, cq_ref, att_ref,
):
    step = pl.program_id(0)
    seqs = len_ref.shape[0]
    rows_all = tok_ref.shape[0]
    tgt = rows_all // seqs
    tok = tok_ref[...]
    q_ref[...] = dot_nn(tok, wq_ref[...]).astype(BF)
    k_ref[...] = dot_nn(tok, wk_ref[...]).astype(BF)
    v_ref[...] = dot_nn(tok, wv_ref[...]).astype(BF)
    masks = head_masks()
    row = lax.broadcasted_iota(jnp.int32, (tgt, tgt), 0)
    col = lax.broadcasted_iota(jnp.int32, (tgt, tgt), 1)
    slot = lax.broadcasted_iota(jnp.int32, (tgt, PREFIX_PAD), 1)
    for s in range(seqs):
        visible = (col <= row) & (col < len_ref[s])
        for p in range(GROUP // PAIR):
            at = pl.ds(p * PAIR, PAIR)
            here = pl.ds(s * tgt, tgt)
            q = q_ref[here, at] * SCALE
            k = k_ref[here, at]
            v = v_ref[here, at]
            pk = pk_ref[:, at]
            pv = pv_ref[:, at]
            total = jnp.zeros((tgt, PAIR), F32)
            for mask in masks:
                s1 = jnp.where(visible, dot_nt(q, k * mask), NEGATIVE)
                s0 = jnp.where(slot < 30, dot_nt(q, pk * mask), NEGATIVE)
                top = jnp.maximum(
                    jnp.max(s1, axis=1, keepdims=True), jnp.max(s0, axis=1, keepdims=True)
                )
                e1 = jnp.exp(s1 - top)
                e0 = jnp.exp(s0 - top)
                inv = 1.0 / (
                    jnp.sum(e1, axis=1, keepdims=True) + jnp.sum(e0, axis=1, keepdims=True)
                )
                out = dot_nn((e1 * inv).astype(BF), v * mask) + dot_nn(
                    (e0 * inv).astype(BF), pv * mask
                )
                total = total + out
            att_ref[here, pl.ds(pl.multiple_of(step * GROUP + p * PAIR, PAIR), PAIR)] = (
                total.astype(BF)
            )

    @pl.when(step == pl.num_programs(0) - 1)
    def _():
        hidden = tok.astype(F32) + dot_nn(att_ref[...], wo_ref[...])
        nrm, inv = norm_stats(hidden)
        nrm_ref[...] = nrm
        inv_ref[...] = inv
        first = nrm * norm_ref[0:1, :] + norm_ref[1:2, :]
        cq_ref[...] = dot_nn(first.astype(BF), wcq_ref[...]).astype(BF)


def cross_forward_kernel(
    len_ref, mem_ref, wk_ref, wv_ref, cq_ref, wco_ref, nrm1_ref, norm_ref,
    mk_ref, mv_ref, nrm_ref, inv_ref, att_ref,
):
    step = pl.program_id(0)
    seqs = len_ref.shape[0]
    tgt = cq_ref.shape[0] // seqs
    src = mem_ref.shape[0] // seqs
    mem = mem_ref[...]
    mk_ref[...] = dot_nn(mem, wk_ref[...]).astype(BF)
    mv_ref[...] = dot_nn(mem, wv_ref[...]).astype(BF)
    masks = head_masks()
    slot = lax.broadcasted_iota(jnp.int32, (tgt, src), 1)
    for s in range(seqs):
        valid = slot < len_ref[s]
        for p in range(GROUP // PAIR):
            at = pl.ds(p * PAIR, PAIR)
            here = pl.ds(s * tgt, tgt)
            there = pl.ds(s * src, src)
            q = cq_ref[here, at] * SCALE
            k = mk_ref[there, at]
            v = mv_ref[there, at]
            total = jnp.zeros((tgt, PAIR), F32)
            for mask in masks:
                sc = jnp.where(valid, dot_nt(q, k * mask), NEGATIVE)
                e = jnp.exp(sc - jnp.max(sc, axis=1, keepdims=True))
                inv = 1.0 / jnp.sum(e, axis=1, keepdims=True)
                total = total + dot_nn(e.astype(BF), v * mask) * inv
            att_ref[here, pl.ds(pl.multiple_of(step * GROUP + p * PAIR, PAIR), PAIR)] = (
                total.astype(BF)
            )

    @pl.when(step == pl.num_programs(0) - 1)
    def _():
        first = nrm1_ref[...] * norm_ref[0:1, :] + norm_ref[1:2, :]
        nrm, inv = norm_stats(first + dot_nn(att_ref[...], wco_ref[...]))
        nrm_ref[...] = nrm
        inv_ref[...] = inv


def ffn_kernel(
    len_ref, nrm2_ref, inv2_ref, cot_ref, win_ref, wff_ref, down_ref, db_ref, up_ref, ub_ref,
    norm_ref,
    out_ref, gtwo_ref, dw_ref, db_out_ref, uw_ref, ub_out_ref,
    acc_ref, low_ref, slope_ref, aact_ref, aslope_ref, g_ref,
):
    phase = pl.program_id(0)
    j = pl.program_id(1)
    last = pl.num_programs(1) - 1
    seqs = len_ref.shape[0]
    rows_all = nrm2_ref.shape[0]
    tgt = rows_all // seqs
    half = rows_all // 2

    @pl.when((phase == 0) & (j == 0))
    def _():
        for b in range(2):
            r = pl.ds(b * half, half)
            second = nrm2_ref[r, :] * norm_ref[2:3, :] + norm_ref[3:4, :]
            low = second.astype(BF)
            low_ref[r, :] = low
            act, slope = gelu_both(dot_nn(low, down_ref[...]) + db_ref[...])
            act = act.astype(BF)
            aact_ref[r, :] = act
            aslope_ref[r, :] = slope.astype(BF)
            acc_ref[r, :] = second + 4.0 * (dot_nn(act, up_ref[...]) + ub_ref[...])

    @pl.when(phase == 0)
    def _():
        for b in range(2):
            r = pl.ds(b * half, half)
            act, slope = gelu_both(dot_nn(low_ref[r, :], win_ref[...]))
            slope_ref[j, r, :] = slope.astype(BF)
            acc_ref[r, :] += dot_nn(act.astype(BF), wff_ref[...])

    @pl.when((phase == 1) & (j == 0))
    def _():
        for s in range(seqs):
            r = pl.ds(s * tgt, tgt)
            nrm, inv = norm_stats(acc_ref[r, :])
            out_ref[r, :] = (nrm * norm_ref[4:5, :] + norm_ref[5:6, :]).astype(BF)
            live = lax.broadcasted_iota(jnp.int32, (tgt, 1), 0) < len_ref[s]
            go = jnp.where(live, cot_ref[r, :].astype(F32), 0.0)
            gthree = norm_back(go, nrm, inv, norm_ref[4:5, :])
            g_ref[r, :] = gthree.astype(BF)
            acc_ref[r, :] = gthree
        agrad = g_ref[...] * 4.0
        ub_out_ref[...] = jnp.sum(agrad.astype(F32), axis=0, keepdims=True)
        uw_ref[...] = dot_tn(agrad, aact_ref[...]).astype(BF)
        apg = (dot_nt(agrad, up_ref[...]) * aslope_ref[...].astype(F32)).astype(BF)
        db_out_ref[...] = jnp.sum(apg.astype(F32), axis=0, keepdims=True)
        dw_ref[...] = dot_tn(low_ref[...], apg).astype(BF)
        acc_ref[...] += dot_nt(apg, down_ref[...])

    @pl.when(phase == 1)
    def _():
        for b in range(2):
            r = pl.ds(b * half, half)
            grad = (dot_nt(g_ref[r, :], wff_ref[...]) * slope_ref[j, r, :].astype(F32)).astype(BF)
            acc_ref[r, :] += dot_nt(grad, win_ref[...])

    @pl.when((phase == 1) & (j == last))
    def _():
        gtwo_ref[...] = norm_back(acc_ref[...], nrm2_ref[...], inv2_ref[...], norm_ref[2:3, :])


def cross_backward_kernel(
    len_ref, gtwo_ref, wco_ref, cq_ref, mk_ref, mv_ref, wk_ref, wv_ref,
    dq_ref, dmem_ref, low_ref, acc_ref, dk_ref, dv_ref,
):
    step = pl.program_id(0)
    seqs = len_ref.shape[0]
    tgt = cq_ref.shape[0] // seqs
    src = mk_ref.shape[0] // seqs

    @pl.when(step == 0)
    def _():
        low_ref[...] = gtwo_ref[...].astype(BF)
        acc_ref[...] = jnp.zeros_like(acc_ref)

    mg_all = dot_nt(low_ref[...], wco_ref[...]).astype(BF)
    masks = head_masks()
    slot = lax.broadcasted_iota(jnp.int32, (src, tgt), 0)
    for s in range(seqs):
        valid = slot < len_ref[s]
        for p in range(GROUP // PAIR):
            at = pl.ds(p * PAIR, PAIR)
            here = pl.ds(s * tgt, tgt)
            there = pl.ds(s * src, src)
            q = cq_ref[here, at] * SCALE
            k = mk_ref[there, at]
            v = mv_ref[there, at]
            mg = mg_all[s * tgt : (s + 1) * tgt, p * PAIR : (p + 1) * PAIR]
            dq = jnp.zeros((tgt, PAIR), F32)
            dk = jnp.zeros((src, PAIR), F32)
            dv = jnp.zeros((src, PAIR), F32)
            for mask in masks:
                km = k * mask
                sc = jnp.where(valid, dot_nt(km, q), NEGATIVE)
                e = jnp.exp(sc - jnp.max(sc, axis=0, keepdims=True))
                prob = e * (1.0 / jnp.sum(e, axis=0, keepdims=True))
                dprob = dot_nt(v * mask, mg)
                delta = jnp.sum(prob * dprob, axis=0, keepdims=True)
                ds = (prob * (dprob - delta)).astype(BF)
                dq = dq + dot_tn(ds, km)
                dk = dk + dot_nn(ds, q * mask)
                dv = dv + dot_nn(prob.astype(BF), mg * mask)
            dq_ref[here, at] = (dq * SCALE).astype(BF)
            dk_ref[there, at] = dk.astype(BF)
            dv_ref[there, at] = dv.astype(BF)
    acc_ref[...] += dot_nt(dk_ref[...], wk_ref[...]) + dot_nt(dv_ref[...], wv_ref[...])

    @pl.when(step == pl.num_programs(0) - 1)
    def _():
        dmem_ref[...] = acc_ref[...].astype(BF)


def self_backward_kernel(
    len_ref, gtwo_ref, cdq_ref, wcq_ref, nrm1_ref, inv1_ref, norm_ref,
    wo_ref, q_ref, k_ref, v_ref, pk_ref, pv_ref, wq_ref, wk_ref, wv_ref,
    din_ref, dpk_ref, dpv_ref, low_ref, acc_ref, dq_ref, dk_ref, dv_ref,
):
    step = pl.program_id(0)
    seqs = len_ref.shape[0]
    tgt = gtwo_ref.shape[0] // seqs

    @pl.when(step == 0)
    def _():
        grad_first = gtwo_ref[...] + dot_nt(cdq_ref[...], wcq_ref[...])
        grad_one = norm_back(grad_first, nrm1_ref[...], inv1_ref[...], norm_ref[0:1, :])
        acc_ref[...] = grad_one
        low_ref[...] = grad_one.astype(BF)

    ag_all = dot_nt(low_ref[...], wo_ref[...]).astype(BF)
    masks = head_masks()
    row = lax.broadcasted_iota(jnp.int32, (tgt, tgt), 1)
    col = lax.broadcasted_iota(jnp.int32, (tgt, tgt), 0)
    slot = lax.broadcasted_iota(jnp.int32, (PREFIX_PAD, tgt), 0)
    for p in range(GROUP // PAIR):
        at = pl.ds(p * PAIR, PAIR)
        pk = pk_ref[:, at]
        pv = pv_ref[:, at]
        dpk = jnp.zeros((PREFIX_PAD, PAIR), F32)
        dpv = jnp.zeros((PREFIX_PAD, PAIR), F32)
        for s in range(seqs):
            visible = (col <= row) & (col < len_ref[s])
            here = pl.ds(s * tgt, tgt)
            q = q_ref[here, at] * SCALE
            k = k_ref[here, at]
            v = v_ref[here, at]
            ag = ag_all[s * tgt : (s + 1) * tgt, p * PAIR : (p + 1) * PAIR]
            dq = jnp.zeros((tgt, PAIR), F32)
            dk = jnp.zeros((tgt, PAIR), F32)
            dv = jnp.zeros((tgt, PAIR), F32)
            for mask in masks:
                km = k * mask
                pkm = pk * mask
                qm = q * mask
                agm = ag * mask
                s1 = jnp.where(visible, dot_nt(km, q), NEGATIVE)
                s0 = jnp.where(slot < 30, dot_nt(pkm, q), NEGATIVE)
                top = jnp.maximum(
                    jnp.max(s1, axis=0, keepdims=True), jnp.max(s0, axis=0, keepdims=True)
                )
                e1 = jnp.exp(s1 - top)
                e0 = jnp.exp(s0 - top)
                inv = 1.0 / (
                    jnp.sum(e1, axis=0, keepdims=True) + jnp.sum(e0, axis=0, keepdims=True)
                )
                p1 = e1 * inv
                p0 = e0 * inv
                d1 = dot_nt(v * mask, ag)
                d0 = dot_nt(pv * mask, ag)
                delta = jnp.sum(p1 * d1, axis=0, keepdims=True) + jnp.sum(
                    p0 * d0, axis=0, keepdims=True
                )
                g1 = (p1 * (d1 - delta)).astype(BF)
                g0 = (p0 * (d0 - delta)).astype(BF)
                dq = dq + dot_tn(g1, km) + dot_tn(g0, pkm)
                dk = dk + dot_nn(g1, qm)
                dv = dv + dot_nn(p1.astype(BF), agm)
                dpk = dpk + dot_nn(g0, qm)
                dpv = dpv + dot_nn(p0.astype(BF), agm)
            dq_ref[here, at] = (dq * SCALE).astype(BF)
            dk_ref[here, at] = dk.astype(BF)
            dv_ref[here, at] = dv.astype(BF)
        dpk_ref[:, at] = dpk
        dpv_ref[:, at] = dpv
    acc_ref[...] += (
        dot_nt(dq_ref[...], wq_ref[...])
        + dot_nt(dk_ref[...], wk_ref[...])
        + dot_nt(dv_ref[...], wv_ref[...])
    )

    @pl.when(step == pl.num_programs(0) - 1)
    def _():
        din_ref[...] = acc_ref[...].astype(BF)


def whole(shape):
    return pl.BlockSpec(shape, lambda *_: (0,) * len(shape))


def columns(rows, width, offset=0):
    return pl.BlockSpec((rows, width), lambda i, *_: (0, i + offset))


def rows_of(height, width):
    return pl.BlockSpec((height, width), lambda i, *_: (i, 0))


def shaped(shape, dtype):
    return jax.ShapeDtypeStruct(shape, dtype)


def call(kernel, grid, in_specs, out_specs, outs, scratch, flops, moved, *args):
    return pl.pallas_call(
        kernel,
        grid_spec=pltpu.PrefetchScalarGridSpec(
            num_scalar_prefetch=1,
            grid=grid,
            in_specs=in_specs,
            out_specs=out_specs,
            scratch_shapes=scratch,
        ),
        out_shape=outs,
        compiler_params=pltpu.CompilerParams(
            vmem_limit_bytes=VMEM_BYTES,
            dimension_semantics=("arbitrary",) * len(grid),
        ),
        cost_estimate=pl.CostEstimate(flops=flops, bytes_accessed=moved, transcendentals=0),
    )(*args)


def self_forward(lens, tok, w_qkv, pk, pv, w_out, w_cq, norms):
    rows, width = tok.shape
    steps = width // GROUP
    return call(
        self_forward_kernel,
        (steps,),
        [
            whole((rows, width)),
            columns(width, GROUP),
            columns(width, GROUP, steps),
            columns(width, GROUP, 2 * steps),
            columns(PREFIX_PAD, GROUP),
            columns(PREFIX_PAD, GROUP),
            whole((width, width)),
            whole((width, width)),
            whole(norms.shape),
        ],
        [columns(rows, GROUP)] * 3
        + [whole((rows, width)), whole((rows, 1)), whole((rows, width))],
        [shaped((rows, width), BF)] * 3
        + [shaped((rows, width), F32), shaped((rows, 1), F32), shaped((rows, width), BF)],
        [pltpu.VMEM((rows, width), BF)],
        2 * rows * width * width * 5,
        20 * width * width,
        lens, tok, w_qkv, w_qkv, w_qkv, pk, pv, w_out, w_cq, norms,
    )


def cross_forward(lens, mem, w_ckv, cq, w_cout, nrm1, norms):
    rows, width = cq.shape
    steps = width // GROUP
    places = mem.shape[0]
    return call(
        cross_forward_kernel,
        (steps,),
        [
            whole((places, width)),
            columns(width, GROUP),
            columns(width, GROUP, steps),
            columns(rows, GROUP),
            whole((width, width)),
            whole((rows, width)),
            whole(norms.shape),
        ],
        [columns(places, GROUP)] * 2 + [whole((rows, width)), whole((rows, 1))],
        [shaped((places, width), BF)] * 2 + [shaped((rows, width), F32), shaped((rows, 1), F32)],
        [pltpu.VMEM((rows, width), BF)],
        2 * width * width * (rows + 2 * places),
        14 * width * width,
        lens, mem, w_ckv, w_ckv, cq, w_cout, nrm1, norms,
    )


def ffn(lens, nrm2, inv2, cot, w_in, w_ff, down, db, up, ub, norms):
    rows, width = nrm2.shape
    hidden = w_in.shape[1]
    adapt = down.shape[1]
    block = 512
    steps = hidden // block
    return call(
        ffn_kernel,
        (2, steps),
        [
            whole((rows, width)),
            whole((rows, 1)),
            whole((rows, width)),
            pl.BlockSpec((width, block), lambda p, j, *_: (0, j)),
            pl.BlockSpec((block, width), lambda p, j, *_: (j, 0)),
            whole((width, adapt)),
            whole((1, adapt)),
            whole((adapt, width)),
            whole((1, width)),
            whole(norms.shape),
        ],
        [
            whole((rows, width)),
            whole((rows, width)),
            whole((width, adapt)),
            whole((1, adapt)),
            whole((width, adapt)),
            whole((1, width)),
        ],
        [
            shaped((rows, width), BF),
            shaped((rows, width), F32),
            shaped((width, adapt), BF),
            shaped((1, adapt), F32),
            shaped((width, adapt), BF),
            shaped((1, width), F32),
        ],
        [
            pltpu.VMEM((rows, width), F32),
            pltpu.VMEM((rows, width), BF),
            pltpu.VMEM((steps, rows, block), BF),
            pltpu.VMEM((rows, adapt), BF),
            pltpu.VMEM((rows, adapt), BF),
            pltpu.VMEM((rows, width), BF),
        ],
        2 * rows * width * (4 * hidden + 6 * adapt),
        8 * width * hidden,
        lens, nrm2, inv2, cot, w_in, w_ff, down, db, up, ub, norms,
    )


def cross_backward(lens, gtwo, w_cout, cq, mk, mv, w_ckv):
    rows, width = cq.shape
    steps = width // GROUP
    places = mk.shape[0]
    return call(
        cross_backward_kernel,
        (steps,),
        [
            whole((rows, width)),
            rows_of(GROUP, width),
            columns(rows, GROUP),
            columns(places, GROUP),
            columns(places, GROUP),
            columns(width, GROUP),
            columns(width, GROUP, steps),
        ],
        [columns(rows, GROUP), whole((places, width))],
        [shaped((rows, width), BF), shaped((places, width), BF)],
        [
            pltpu.VMEM((rows, width), BF),
            pltpu.VMEM((places, width), F32),
            pltpu.VMEM((places, GROUP), BF),
            pltpu.VMEM((places, GROUP), BF),
        ],
        2 * width * width * (rows + 2 * places),
        14 * width * width,
        lens, gtwo, w_cout, cq, mk, mv, w_ckv, w_ckv,
    )


def self_backward(
    lens, gtwo, cdq, w_cq, nrm1, inv1, norms, w_out, q, k, v, pk, pv, w_qkv
):
    rows, width = q.shape
    steps = width // GROUP
    return call(
        self_backward_kernel,
        (steps,),
        [
            whole((rows, width)),
            whole((rows, width)),
            whole((width, width)),
            whole((rows, width)),
            whole((rows, 1)),
            whole(norms.shape),
            rows_of(GROUP, width),
            columns(rows, GROUP),
            columns(rows, GROUP),
            columns(rows, GROUP),
            columns(PREFIX_PAD, GROUP),
            columns(PREFIX_PAD, GROUP),
            columns(width, GROUP),
            columns(width, GROUP, steps),
            columns(width, GROUP, 2 * steps),
        ],
        [whole((rows, width)), columns(PREFIX_PAD, GROUP), columns(PREFIX_PAD, GROUP)],
        [
            shaped((rows, width), BF),
            shaped((PREFIX_PAD, width), F32),
            shaped((PREFIX_PAD, width), F32),
        ],
        [
            pltpu.VMEM((rows, width), BF),
            pltpu.VMEM((rows, width), F32),
            pltpu.VMEM((rows, GROUP), BF),
            pltpu.VMEM((rows, GROUP), BF),
            pltpu.VMEM((rows, GROUP), BF),
        ],
        2 * rows * width * width * 5,
        20 * width * width,
        lens, gtwo, cdq, w_cq, nrm1, inv1, norms, w_out, q, k, v, pk, pv, w_qkv, w_qkv, w_qkv,
    )


def local(
    tokens, memory, cotangent, tgt_len, src_len,
    self_qkv, self_out, cross_q, cross_kv, cross_out, ffn_in, ffn_out,
    first_gain, first_bias, second_gain, second_bias, third_gain, third_bias,
    prefix_key, prefix_value, down_weight, down_bias, up_weight, up_bias,
):
    mem_groups = lax.axis_size(MEM)
    mem_place = lax.axis_index(MEM)
    seqs, tgt, width = tokens.shape
    src_block = memory.shape[1]
    prefix = prefix_key.shape[0]

    def gathered(w):
        return lax.all_gather(w, DP, axis=0, tiled=True)

    vectors = jnp.stack(
        [first_gain, first_bias, second_gain, second_bias, third_gain, third_bias]
        + [third_bias] * 2
    )
    norms = lax.all_gather(vectors, DP, axis=1, tiled=True).astype(F32)
    w_qkv = gathered(self_qkv)
    w_oq = gathered(jnp.concatenate([self_out, cross_q], axis=1))
    w_out, w_cq = w_oq[:, :width], w_oq[:, width:]
    w_ckv = gathered(cross_kv)
    w_cout = gathered(cross_out)
    w_in = gathered(ffn_in)
    w_ff = gathered(ffn_out)

    mem_rows = lax.all_to_all(memory, MEM, split_axis=0, concat_axis=1, tiled=True)
    mem_rows = mem_rows.reshape(-1, width)
    own_src = lax.dynamic_slice_in_dim(src_len, mem_place * seqs, seqs, 0)

    tok = tokens.reshape(seqs * tgt, width)
    cot = cotangent.reshape(seqs * tgt, width)
    pk = jnp.pad(prefix_key, ((0, PREFIX_PAD - prefix), (0, 0)))
    pv = jnp.pad(prefix_value, ((0, PREFIX_PAD - prefix), (0, 0)))

    q, k, v, nrm1, inv1, cq = self_forward(tgt_len, tok, w_qkv, pk, pv, w_out, w_cq, norms)
    mk, mv, nrm2, inv2 = cross_forward(own_src, mem_rows, w_ckv, cq, w_cout, nrm1, norms)
    output, gtwo, dw, db, uw, ub = ffn(
        tgt_len, nrm2, inv2, cot, w_in, w_ff,
        down_weight, down_bias.astype(F32)[None], up_weight, up_bias.astype(F32)[None], norms,
    )
    cdq, dmem = cross_backward(own_src, gtwo, w_cout, cq, mk, mv, w_ckv)
    memory_grad = lax.all_to_all(
        dmem.reshape(seqs, mem_groups * src_block, width),
        MEM, split_axis=1, concat_axis=0, tiled=True,
    )
    din, dpk, dpv = self_backward(
        tgt_len, gtwo, cdq, w_cq, nrm1, inv1, norms, w_out, q, k, v, pk, pv, w_qkv
    )

    ranks = mem_groups * lax.axis_size(DP)

    def summed(x):
        arrived = lax.all_to_all(x, DP_MEM, split_axis=0, concat_axis=0, tiled=True)
        return jnp.sum(arrived.astype(F32), axis=0)

    def blocks(x):
        return jnp.moveaxis(x.reshape(x.shape[0], ranks, -1), 1, 0)

    adapter = summed(
        jnp.concatenate(
            [dw.reshape(ranks, -1, dw.shape[1]), uw.reshape(ranks, -1, uw.shape[1])], axis=1
        )
    )
    high = dw.shape[0] // ranks
    small = [blocks(x) for x in (dpk[:prefix], dpv[:prefix], db, ub)]
    total = summed(jnp.concatenate([x.reshape(ranks, -1) for x in small], axis=1))
    parts = []
    start = 0
    for x in small:
        size = x.shape[1] * x.shape[2]
        parts.append(total[start : start + size].reshape(x.shape[1:]))
        start += size
    return (
        output.reshape(tokens.shape),
        din.reshape(tokens.shape),
        memory_grad,
        parts[0],
        parts[1],
        adapter[:high],
        parts[2][0],
        adapter[high:].T,
        parts[3][0],
    )


def solution(mesh):
    torus = Mesh(mesh.devices.reshape(4, 2, 4, 4), ("dp_0", "dp_1", "mem_0", "mem_1"))
    by_dp = P(DP, None)
    copied = P(None)
    return jax.shard_map(
        local,
        mesh=torus,
        in_specs=(
            P(DP_MEM, None, None), P(DP, MEM, None), P(DP_MEM, None, None), P(DP_MEM), P(DP),
            by_dp, by_dp, by_dp, by_dp, by_dp, by_dp, by_dp,
            P(DP), P(DP), P(DP), P(DP), P(DP), P(DP),
            copied, copied, copied, copied, copied, copied,
        ),
        out_specs=(
            P(DP_MEM, None, None),
            P(DP_MEM, None, None),
            P(DP, MEM, None),
            P(None, DP_MEM),
            P(None, DP_MEM),
            P(DP_MEM, None),
            P(DP_MEM),
            P(None, DP_MEM),
            P(DP_MEM),
        ),
        check_vma=False,
    )
```

```python
import functools

import jax
import jax.numpy as jnp
from jax import lax
from jax.experimental import pallas as pl
from jax.experimental.pallas import tpu as pltpu
from jax.sharding import Mesh
from jax.sharding import PartitionSpec as P

HEAD_DIM = 64
PAIR = 128
GROUP = 256
PREFIX_PAD = 32
BIAS_ROWS = 4
MEM = ("mem_0", "mem_1")
DP = ("dp_0", "dp_1")
DP_MEM = ("dp_0", "dp_1", "mem_0", "mem_1")

NEGATIVE = -1e30
EPSILON = 1e-05
SCALE = HEAD_DIM ** (-0.5)
BF = jnp.bfloat16
F32 = jnp.float32
SPREAD = 4
FF_AT = 0
IN_AT = 4096
KV_AT = 8192
OUT_AT = 10240
SOUT_AT = 11264
CQ_AT = 12288
VMEM_BYTES = 60 * 1024 * 1024


def dot_nn(left, right):
    return lax.dot_general(left, right, (((1,), (0,)), ((), ())), preferred_element_type=F32)


def dot_nt(left, right):
    return lax.dot_general(left, right, (((1,), (1,)), ((), ())), preferred_element_type=F32)


def dot_tn(left, right):
    return lax.dot_general(left, right, (((0,), (0,)), ((), ())), preferred_element_type=F32)


def head_masks():
    lane = lax.broadcasted_iota(jnp.int32, (1, PAIR), 1)
    return [jnp.where((lane >= HEAD_DIM) == bool(h), 1.0, 0.0).astype(BF) for h in range(2)]


def norm_stats(hidden):
    centred = hidden - jnp.mean(hidden, axis=-1, keepdims=True)
    inverse = lax.rsqrt(jnp.mean(centred * centred, axis=-1, keepdims=True) + EPSILON)
    return centred * inverse, inverse


def norm_back(grad_in, normed, inverse, gain):
    scaled = grad_in * gain
    return inverse * (
        scaled
        - jnp.mean(scaled, axis=-1, keepdims=True)
        - normed * jnp.mean(scaled * normed, axis=-1, keepdims=True)
    )


def gelu_both(pre):
    cdf = 0.5 * (1.0 + lax.erf(pre * (0.5**0.5)))
    density = jnp.exp(-0.5 * pre * pre) * 0.3989422804014327
    return pre * cdf, cdf + pre * density


def self_forward_kernel(
    len_ref, tok_ref, wq_ref, wk_ref, wv_ref, pk_ref, pv_ref,
    q_ref, k_ref, v_ref, att_ref,
):
    seqs = len_ref.shape[0]
    rows_all = tok_ref.shape[0]
    tgt = rows_all // seqs
    tok = tok_ref[...]
    q_ref[...] = dot_nn(tok, wq_ref[...]).astype(BF)
    k_ref[...] = dot_nn(tok, wk_ref[...]).astype(BF)
    v_ref[...] = dot_nn(tok, wv_ref[...]).astype(BF)
    masks = head_masks()
    row = lax.broadcasted_iota(jnp.int32, (tgt, tgt), 0)
    col = lax.broadcasted_iota(jnp.int32, (tgt, tgt), 1)
    slot = lax.broadcasted_iota(jnp.int32, (tgt, PREFIX_PAD), 1)
    for s in range(seqs):
        visible = (col <= row) & (col < len_ref[s])
        for p in range(GROUP // PAIR):
            at = pl.ds(p * PAIR, PAIR)
            here = pl.ds(s * tgt, tgt)
            q = q_ref[here, at] * SCALE
            k = k_ref[here, at]
            v = v_ref[here, at]
            pk = pk_ref[:, at]
            pv = pv_ref[:, at]
            total = jnp.zeros((tgt, PAIR), F32)
            for mask in masks:
                s1 = jnp.where(visible, dot_nt(q, k * mask), NEGATIVE)
                s0 = jnp.where(slot < 30, dot_nt(q, pk * mask), NEGATIVE)
                top = jnp.maximum(
                    jnp.max(s1, axis=1, keepdims=True), jnp.max(s0, axis=1, keepdims=True)
                )
                e1 = jnp.exp(s1 - top)
                e0 = jnp.exp(s0 - top)
                inv = 1.0 / (
                    jnp.sum(e1, axis=1, keepdims=True) + jnp.sum(e0, axis=1, keepdims=True)
                )
                out = dot_nn((e1 * inv).astype(BF), v * mask) + dot_nn(
                    (e0 * inv).astype(BF), pv * mask
                )
                total = total + out
            att_ref[here, at] = total.astype(BF)


def cross_forward_kernel(
    len_ref, mem_ref, wk_ref, wv_ref, tok_ref, self_ref, wo_ref, wcq_ref, wco_ref, norm_ref,
    mk_ref, mv_ref, cq_ref, nrm1_ref, inv1_ref, nrm_ref, inv_ref, att_ref,
):
    step = pl.program_id(0)
    seqs = len_ref.shape[0]
    tgt = tok_ref.shape[0] // seqs
    src = mem_ref.shape[0] // seqs

    @pl.when(step == 0)
    def _():
        for s in range(seqs):
            r = pl.ds(s * tgt, tgt)
            nrm, inv = norm_stats(
                tok_ref[r, :].astype(F32) + dot_nn(self_ref[r, :], wo_ref[...])
            )
            nrm1_ref[r, :] = nrm
            inv1_ref[r, :] = inv
            first = nrm * norm_ref[0:1, :] + norm_ref[1:2, :]
            cq_ref[r, :] = dot_nn(first.astype(BF), wcq_ref[...]).astype(BF)

    mem = mem_ref[...]
    mk_ref[...] = dot_nn(mem, wk_ref[...]).astype(BF)
    mv_ref[...] = dot_nn(mem, wv_ref[...]).astype(BF)
    masks = head_masks()
    slot = lax.broadcasted_iota(jnp.int32, (tgt, src), 1)
    for s in range(seqs):
        valid = slot < len_ref[s]
        for p in range(GROUP // PAIR):
            at = pl.ds(p * PAIR, PAIR)
            here = pl.ds(s * tgt, tgt)
            there = pl.ds(s * src, src)
            lanes = pl.ds(pl.multiple_of(step * GROUP + p * PAIR, PAIR), PAIR)
            q = cq_ref[here, lanes] * SCALE
            k = mk_ref[there, at]
            v = mv_ref[there, at]
            total = jnp.zeros((tgt, PAIR), F32)
            for mask in masks:
                sc = jnp.where(valid, dot_nt(q, k * mask), NEGATIVE)
                e = jnp.exp(sc - jnp.max(sc, axis=1, keepdims=True))
                inv = 1.0 / jnp.sum(e, axis=1, keepdims=True)
                total = total + dot_nn(e.astype(BF), v * mask) * inv
            att_ref[here, lanes] = total.astype(BF)

    @pl.when(step == pl.num_programs(0) - 1)
    def _():
        first = nrm1_ref[...] * norm_ref[0:1, :] + norm_ref[1:2, :]
        nrm, inv = norm_stats(first + dot_nn(att_ref[...], wco_ref[...]))
        nrm_ref[...] = nrm
        inv_ref[...] = inv


def ffn_kernel(
    len_ref, nrm2_ref, inv2_ref, cot_ref, win_ref, wff_ref, down_ref, db_ref, up_ref, ub_ref,
    norm_ref,
    out_ref, gtwo_ref, adapt_ref,
    acc_ref, low_ref, slope_ref, aact_ref, aslope_ref, g_ref,
):
    phase = pl.program_id(0)
    j = pl.program_id(1)
    last = pl.num_programs(1) - 1
    seqs = len_ref.shape[0]
    rows_all = nrm2_ref.shape[0]
    tgt = rows_all // seqs
    half = rows_all // 2
    width = nrm2_ref.shape[1]
    wff = jnp.concatenate(
        [wff_ref[:, b * width : (b + 1) * width] for b in range(wff_ref.shape[1] // width)], axis=0
    )

    @pl.when((phase == 0) & (j == 0))
    def _():
        for b in range(2):
            r = pl.ds(b * half, half)
            second = nrm2_ref[r, :] * norm_ref[2:3, :] + norm_ref[3:4, :]
            low = second.astype(BF)
            low_ref[r, :] = low
            act, slope = gelu_both(dot_nn(low, down_ref[...]) + db_ref[...])
            act = act.astype(BF)
            aact_ref[r, :] = act
            aslope_ref[r, :] = slope.astype(BF)
            acc_ref[r, :] = second + 4.0 * (dot_nn(act, up_ref[...]) + ub_ref[...])

    @pl.when(phase == 0)
    def _():
        for b in range(2):
            r = pl.ds(b * half, half)
            act, slope = gelu_both(dot_nn(low_ref[r, :], win_ref[...]))
            slope_ref[j, r, :] = slope.astype(BF)
            acc_ref[r, :] += dot_nn(act.astype(BF), wff)

    @pl.when((phase == 1) & (j == 0))
    def _():
        for s in range(seqs):
            r = pl.ds(s * tgt, tgt)
            nrm, inv = norm_stats(acc_ref[r, :])
            out_ref[r, :] = (nrm * norm_ref[4:5, :] + norm_ref[5:6, :]).astype(BF)
            live = lax.broadcasted_iota(jnp.int32, (tgt, 1), 0) < len_ref[s]
            go = jnp.where(live, cot_ref[r, :].astype(F32), 0.0)
            gthree = norm_back(go, nrm, inv, norm_ref[4:5, :])
            g_ref[r, :] = gthree.astype(BF)
            acc_ref[r, :] = gthree
        agrad = g_ref[...] * 4.0
        adapt = aact_ref.shape[1]
        apg = (dot_nt(agrad, up_ref[...]) * aslope_ref[...].astype(F32)).astype(BF)
        adapt_ref[:, :adapt] = dot_tn(low_ref[...], apg).astype(BF)
        adapt_ref[:, adapt : 2 * adapt] = dot_tn(agrad, aact_ref[...]).astype(BF)
        ones = jnp.ones((rows_all, PAIR), BF)
        down_sum = dot_tn(apg, ones).astype(BF)
        high = width // adapt
        row = lax.broadcasted_iota(jnp.int32, (width, adapt), 0)
        col = lax.broadcasted_iota(jnp.int32, (width, adapt), 1)
        block = BIAS_ROWS * high
        entry = lax.div(row, block) * BIAS_ROWS + lax.rem(row, block)
        chosen = (entry == col) & (lax.rem(row, block) < BIAS_ROWS)
        placed = dot_nn(jnp.where(chosen, 1.0, 0.0).astype(BF), down_sum)
        lane = lax.broadcasted_iota(jnp.int32, (width, PAIR), 1)
        sums = jnp.where(lane == 2 * PREFIX_PAD, dot_tn(agrad, ones), placed)
        sums = jnp.where((lane >= 2 * PREFIX_PAD) & (lane < 2 * PREFIX_PAD + 2), sums, 0.0)
        adapt_ref[:, 2 * adapt :] = sums.astype(BF)
        acc_ref[...] += dot_nt(apg, down_ref[...])

    @pl.when(phase == 1)
    def _():
        for b in range(2):
            r = pl.ds(b * half, half)
            grad = (dot_nt(g_ref[r, :], wff) * slope_ref[j, r, :].astype(F32)).astype(BF)
            acc_ref[r, :] += dot_nt(grad, win_ref[...])

    @pl.when((phase == 1) & (j == last))
    def _():
        gtwo_ref[...] = norm_back(acc_ref[...], nrm2_ref[...], inv2_ref[...], norm_ref[2:3, :])


def cross_backward_kernel(
    len_ref, gtwo_ref, wco_ref, cq_ref, mk_ref, mv_ref, wk_ref, wv_ref,
    dq_ref, dmem_ref, low_ref, acc_ref, dk_ref, dv_ref,
):
    step = pl.program_id(0)
    seqs = len_ref.shape[0]
    tgt = cq_ref.shape[0] // seqs
    src = mk_ref.shape[0] // seqs

    @pl.when(step == 0)
    def _():
        low_ref[...] = gtwo_ref[...].astype(BF)
        acc_ref[...] = jnp.zeros_like(acc_ref)

    mg_all = dot_nt(low_ref[...], wco_ref[...]).astype(BF)
    masks = head_masks()
    slot = lax.broadcasted_iota(jnp.int32, (src, tgt), 0)
    for s in range(seqs):
        valid = slot < len_ref[s]
        for p in range(GROUP // PAIR):
            at = pl.ds(p * PAIR, PAIR)
            here = pl.ds(s * tgt, tgt)
            there = pl.ds(s * src, src)
            q = cq_ref[here, at] * SCALE
            k = mk_ref[there, at]
            v = mv_ref[there, at]
            mg = mg_all[s * tgt : (s + 1) * tgt, p * PAIR : (p + 1) * PAIR]
            dq = jnp.zeros((tgt, PAIR), F32)
            dk = jnp.zeros((src, PAIR), F32)
            dv = jnp.zeros((src, PAIR), F32)
            for mask in masks:
                km = k * mask
                sc = jnp.where(valid, dot_nt(km, q), NEGATIVE)
                e = jnp.exp(sc - jnp.max(sc, axis=0, keepdims=True))
                prob = e * (1.0 / jnp.sum(e, axis=0, keepdims=True))
                dprob = dot_nt(v * mask, mg)
                delta = jnp.sum(prob * dprob, axis=0, keepdims=True)
                ds = (prob * (dprob - delta)).astype(BF)
                dq = dq + dot_tn(ds, km)
                dk = dk + dot_nn(ds, q * mask)
                dv = dv + dot_nn(prob.astype(BF), mg * mask)
            dq_ref[here, at] = (dq * SCALE).astype(BF)
            dk_ref[there, at] = dk.astype(BF)
            dv_ref[there, at] = dv.astype(BF)
    acc_ref[...] += dot_nt(dk_ref[...], wk_ref[...]) + dot_nt(dv_ref[...], wv_ref[...])

    @pl.when(step == pl.num_programs(0) - 1)
    def _():
        parts, _, high, width = dmem_ref.shape
        for s in range(seqs):
            block = acc_ref[s * src : (s + 1) * src, :]
            dmem_ref[:, s] = block.reshape(parts, high, width).astype(BF)


def self_backward_kernel(
    len_ref, gtwo_ref, cdq_ref, wcq_ref, nrm1_ref, inv1_ref, norm_ref,
    wo_ref, q_ref, k_ref, v_ref, pk_ref, pv_ref,
    gone_ref, dq_ref, dk_ref, dv_ref, small_ref, low_ref,
):
    step = pl.program_id(0)
    seqs = len_ref.shape[0]
    tgt = gtwo_ref.shape[0] // seqs

    @pl.when(step == 0)
    def _():
        grad_first = gtwo_ref[...] + dot_nt(cdq_ref[...], wcq_ref[...])
        grad_one = norm_back(grad_first, nrm1_ref[...], inv1_ref[...], norm_ref[0:1, :])
        gone_ref[...] = grad_one
        low_ref[...] = grad_one.astype(BF)

    ag_all = dot_nt(low_ref[...], wo_ref[...]).astype(BF)
    masks = head_masks()
    row = lax.broadcasted_iota(jnp.int32, (tgt, tgt), 1)
    col = lax.broadcasted_iota(jnp.int32, (tgt, tgt), 0)
    slot = lax.broadcasted_iota(jnp.int32, (PREFIX_PAD, tgt), 0)
    for p in range(GROUP // PAIR):
        at = pl.ds(p * PAIR, PAIR)
        pk = pk_ref[:, at]
        pv = pv_ref[:, at]
        dpk = jnp.zeros((PREFIX_PAD, PAIR), F32)
        dpv = jnp.zeros((PREFIX_PAD, PAIR), F32)
        for s in range(seqs):
            visible = (col <= row) & (col < len_ref[s])
            here = pl.ds(s * tgt, tgt)
            q = q_ref[here, at] * SCALE
            k = k_ref[here, at]
            v = v_ref[here, at]
            ag = ag_all[s * tgt : (s + 1) * tgt, p * PAIR : (p + 1) * PAIR]
            dq = jnp.zeros((tgt, PAIR), F32)
            dk = jnp.zeros((tgt, PAIR), F32)
            dv = jnp.zeros((tgt, PAIR), F32)
            for mask in masks:
                km = k * mask
                pkm = pk * mask
                qm = q * mask
                agm = ag * mask
                s1 = jnp.where(visible, dot_nt(km, q), NEGATIVE)
                s0 = jnp.where(slot < 30, dot_nt(pkm, q), NEGATIVE)
                top = jnp.maximum(
                    jnp.max(s1, axis=0, keepdims=True), jnp.max(s0, axis=0, keepdims=True)
                )
                e1 = jnp.exp(s1 - top)
                e0 = jnp.exp(s0 - top)
                inv = 1.0 / (
                    jnp.sum(e1, axis=0, keepdims=True) + jnp.sum(e0, axis=0, keepdims=True)
                )
                p1 = e1 * inv
                p0 = e0 * inv
                d1 = dot_nt(v * mask, ag)
                d0 = dot_nt(pv * mask, ag)
                delta = jnp.sum(p1 * d1, axis=0, keepdims=True) + jnp.sum(
                    p0 * d0, axis=0, keepdims=True
                )
                g1 = (p1 * (d1 - delta)).astype(BF)
                g0 = (p0 * (d0 - delta)).astype(BF)
                dq = dq + dot_tn(g1, km) + dot_tn(g0, pkm)
                dk = dk + dot_nn(g1, qm)
                dv = dv + dot_nn(p1.astype(BF), agm)
                dpk = dpk + dot_nn(g0, qm)
                dpv = dpv + dot_nn(p0.astype(BF), agm)
            dq_ref[here, at] = (dq * SCALE).astype(BF)
            dk_ref[here, at] = dk.astype(BF)
            dv_ref[here, at] = dv.astype(BF)
        both = jnp.concatenate(
            [dpk, dpv, jnp.zeros((PAIR - 2 * PREFIX_PAD, PAIR), F32)], axis=0
        )
        small_ref[p * PAIR : (p + 1) * PAIR, :] = both.T


def input_grad_kernel(gone_ref, dq_ref, dk_ref, dv_ref, wq_ref, wk_ref, wv_ref, din_ref):
    din_ref[...] = (
        gone_ref[...]
        + dot_nt(dq_ref[...], wq_ref[...])
        + dot_nt(dk_ref[...], wk_ref[...])
        + dot_nt(dv_ref[...], wv_ref[...])
    ).astype(BF)


def square(width, at):
    return pl.BlockSpec((width, width), lambda *_: (0, at // width))


def whole(shape):
    return pl.BlockSpec(shape, lambda *_: (0,) * len(shape))


def columns(rows, width, offset=0):
    return pl.BlockSpec((rows, width), lambda i, *_: (0, i + offset))


def rows_of(height, width, at):
    return pl.BlockSpec((height, width), lambda i, *_: (i, at // width))


def shaped(shape, dtype):
    return jax.ShapeDtypeStruct(shape, dtype)


def call(kernel, grid, in_specs, out_specs, outs, scratch, flops, moved, *args):
    return pl.pallas_call(
        kernel,
        grid_spec=pltpu.PrefetchScalarGridSpec(
            num_scalar_prefetch=1,
            grid=grid,
            in_specs=in_specs,
            out_specs=out_specs,
            scratch_shapes=scratch,
        ),
        out_shape=outs,
        compiler_params=pltpu.CompilerParams(
            vmem_limit_bytes=VMEM_BYTES,
            dimension_semantics=("arbitrary",) * len(grid),
        ),
        cost_estimate=pl.CostEstimate(flops=flops, bytes_accessed=moved, transcendentals=0),
    )(*args)


def self_forward(lens, tok, early, pk, pv):
    rows, width = tok.shape
    steps = width // GROUP
    return call(
        self_forward_kernel,
        (steps,),
        [
            whole((rows, width)),
            columns(width, GROUP),
            columns(width, GROUP, steps),
            columns(width, GROUP, 2 * steps),
            columns(PREFIX_PAD, GROUP),
            columns(PREFIX_PAD, GROUP),
        ],
        [columns(rows, GROUP)] * 4,
        [shaped((rows, width), BF)] * 4,
        [],
        2 * rows * width * width * 3,
        14 * width * width,
        lens, tok, early, early, early, pk, pv,
    )


def cross_forward(lens, mem, late, tok, att, norms):
    rows, width = tok.shape
    steps = width // GROUP
    places = mem.shape[0]
    return call(
        cross_forward_kernel,
        (steps,),
        [
            whole((places, width)),
            columns(width, GROUP, KV_AT // GROUP),
            columns(width, GROUP, KV_AT // GROUP + steps),
            whole((rows, width)),
            whole((rows, width)),
            square(width, SOUT_AT),
            square(width, CQ_AT),
            square(width, OUT_AT),
            whole(norms.shape),
        ],
        [columns(places, GROUP)] * 2
        + [whole((rows, width)), whole((rows, width)), whole((rows, 1))]
        + [whole((rows, width)), whole((rows, 1))],
        [shaped((places, width), BF)] * 2
        + [shaped((rows, width), BF), shaped((rows, width), F32), shaped((rows, 1), F32)]
        + [shaped((rows, width), F32), shaped((rows, 1), F32)],
        [pltpu.VMEM((rows, width), BF)],
        2 * width * width * (3 * rows + 2 * places),
        20 * width * width,
        lens, mem, late, late, tok, att, late, late, late, norms,
    )


def ffn(lens, nrm2, inv2, cot, late, down, db, up, ub, norms):
    rows, width = nrm2.shape
    hidden = SPREAD * width
    adapt = down.shape[1]
    block = 512
    steps = hidden // block
    return call(
        ffn_kernel,
        (2, steps),
        [
            whole((rows, width)),
            whole((rows, 1)),
            whole((rows, width)),
            pl.BlockSpec((width, block), lambda p, j, *_: (0, j + IN_AT // block)),
            pl.BlockSpec((block // SPREAD, SPREAD * width), lambda p, j, *_: (j, FF_AT)),
            whole((width, adapt)),
            whole((1, adapt)),
            whole((adapt, width)),
            whole((1, width)),
            whole(norms.shape),
        ],
        [
            whole((rows, width)),
            whole((rows, width)),
            whole((width, 2 * adapt + PAIR)),
        ],
        [
            shaped((rows, width), BF),
            shaped((rows, width), F32),
            shaped((width, 2 * adapt + PAIR), BF),
        ],
        [
            pltpu.VMEM((rows, width), F32),
            pltpu.VMEM((rows, width), BF),
            pltpu.VMEM((steps, rows, block), BF),
            pltpu.VMEM((rows, adapt), BF),
            pltpu.VMEM((rows, adapt), BF),
            pltpu.VMEM((rows, width), BF),
        ],
        2 * rows * width * (4 * hidden + 6 * adapt),
        8 * width * hidden,
        lens, nrm2, inv2, cot, late, late, down, db, up, ub, norms,
    )


def cross_backward(lens, gtwo, late, cq, mk, mv, parts):
    rows, width = cq.shape
    steps = width // GROUP
    places = mk.shape[0]
    seqs = lens.shape[0]
    sent = (parts, seqs, places // seqs // parts, width)
    return call(
        cross_backward_kernel,
        (steps,),
        [
            whole((rows, width)),
            rows_of(GROUP, width, OUT_AT),
            columns(rows, GROUP),
            columns(places, GROUP),
            columns(places, GROUP),
            columns(width, GROUP, KV_AT // GROUP),
            columns(width, GROUP, KV_AT // GROUP + steps),
        ],
        [columns(rows, GROUP), whole(sent)],
        [shaped((rows, width), BF), shaped(sent, BF)],
        [
            pltpu.VMEM((rows, width), BF),
            pltpu.VMEM((places, width), F32),
            pltpu.VMEM((places, GROUP), BF),
            pltpu.VMEM((places, GROUP), BF),
        ],
        2 * width * width * (rows + 2 * places),
        14 * width * width,
        lens, gtwo, late, cq, mk, mv, late, late,
    )


def self_backward(lens, gtwo, cdq, late, nrm1, inv1, norms, q, k, v, pk, pv):
    rows, width = q.shape
    steps = width // GROUP
    return call(
        self_backward_kernel,
        (steps,),
        [
            whole((rows, width)),
            whole((rows, width)),
            square(width, CQ_AT),
            whole((rows, width)),
            whole((rows, 1)),
            whole(norms.shape),
            rows_of(GROUP, width, SOUT_AT),
            columns(rows, GROUP),
            columns(rows, GROUP),
            columns(rows, GROUP),
            columns(PREFIX_PAD, GROUP),
            columns(PREFIX_PAD, GROUP),
        ],
        [whole((rows, width))]
        + [columns(rows, GROUP)] * 3
        + [pl.BlockSpec((GROUP, PAIR), lambda i, *_: (i, 0))],
        [shaped((rows, width), F32)]
        + [shaped((rows, width), BF)] * 3
        + [shaped((width, PAIR), F32)],
        [pltpu.VMEM((rows, width), BF)],
        2 * rows * width * width * 4,
        20 * width * width,
        lens, gtwo, cdq, late, nrm1, inv1, norms, late, q, k, v, pk, pv,
    )


def input_gradient(gone, dq, dk, dv, early):
    rows, width = gone.shape

    def part(index):
        return pl.BlockSpec((GROUP, width), lambda i: (i, index))

    return pl.pallas_call(
        input_grad_kernel,
        grid=(width // GROUP,),
        in_specs=[pl.BlockSpec((rows, GROUP), lambda i: (0, i))]
        + [whole((rows, width))] * 3
        + [part(0), part(1), part(2)],
        out_specs=pl.BlockSpec((rows, GROUP), lambda i: (0, i)),
        out_shape=shaped((rows, width), BF),
        compiler_params=pltpu.CompilerParams(
            vmem_limit_bytes=VMEM_BYTES, dimension_semantics=("arbitrary",)
        ),
        cost_estimate=pl.CostEstimate(
            flops=6 * rows * width * width, bytes_accessed=12 * width * width, transcendentals=0
        ),
    )(gone, dq, dk, dv, early, early, early)


def ring_gather(shard, other):
    rows = shard.shape[0]
    half = rows // 2
    count = lax.axis_size("dp_0")
    x, core = lax.axis_index("dp_0"), lax.axis_index("dp_1")
    up = [(i, (i + 1) % count) for i in range(count)]
    down = [(i, (i - 1) % count) for i in range(count)]
    below = lax.ppermute(shard, "dp_0", up)
    above = lax.ppermute(shard, "dp_0", down)
    filled = jnp.zeros((count * 2 * rows, shard.shape[1]), shard.dtype)
    filled, other = lax.optimization_barrier((filled, other))
    far_low = lax.ppermute(below[:half], "dp_0", up)
    far_high = lax.ppermute(above[half:], "dp_0", down)
    for piece, offset, start in (
        (shard, 0, 0), (below, -1, 0), (above, 1, 0), (far_low, 2, 0), (far_high, 2, half),
    ):
        swapped = lax.ppermute(piece, "dp_1", [(0, 1), (1, 0)])
        chip = (x + offset + count) % count
        for part, place in ((piece, core), (swapped, 1 - core)):
            at = (chip * 2 + place) * rows + start
            filled = lax.dynamic_update_slice_in_dim(filled, part, at, 0)
    return filled, other


def local(
    tokens, memory, cotangent, tgt_len, src_len,
    self_qkv, self_out, cross_q, cross_kv, cross_out, ffn_in, ffn_out,
    first_gain, first_bias, second_gain, second_bias, third_gain, third_bias,
    prefix_key, prefix_value, down_weight, down_bias, up_weight, up_bias,
):
    mem_groups = lax.axis_size(MEM)
    mem_place = lax.axis_index(MEM)
    seqs, tgt, width = tokens.shape
    src_block = memory.shape[1]
    prefix = prefix_key.shape[0]

    high = cross_out.shape[0] // mem_groups
    mine = functools.partial(
        lax.dynamic_slice_in_dim, start_index=mem_place * high, slice_size=high
    )
    spread = mine(ffn_out.reshape(SPREAD, -1, width), axis=1)
    late = lax.all_gather(
        jnp.concatenate(
            [jnp.moveaxis(spread, 0, 1).reshape(high, SPREAD * width)]
            + [mine(w, axis=0) for w in (ffn_in, cross_kv, cross_out, self_out, cross_q)],
            axis=1,
        ),
        DP_MEM, axis=0, tiled=True,
    )
    early, memory = ring_gather(self_qkv, memory)
    mem_rows = lax.all_to_all(memory, MEM, split_axis=0, concat_axis=1, tiled=True)
    mem_rows = mem_rows.reshape(-1, width)
    own_src = lax.dynamic_slice_in_dim(src_len, mem_place * seqs, seqs, 0)

    tok = tokens.reshape(seqs * tgt, width)
    cot = cotangent.reshape(seqs * tgt, width)
    pk = jnp.pad(prefix_key, ((0, PREFIX_PAD - prefix), (0, 0)))
    pv = jnp.pad(prefix_value, ((0, PREFIX_PAD - prefix), (0, 0)))

    q, k, v, att = self_forward(tgt_len, tok, early, pk, pv)
    vectors = jnp.stack(
        [first_gain, first_bias, second_gain, second_bias, third_gain, third_bias]
        + [third_bias] * 2
    )
    vectors, att = lax.optimization_barrier((vectors, att))
    norms = lax.all_gather(vectors, DP, axis=1, tiled=True).astype(F32)
    mk, mv, cq, nrm1, inv1, nrm2, inv2 = cross_forward(own_src, mem_rows, late, tok, att, norms)
    output, gtwo, adapter = ffn(
        tgt_len, nrm2, inv2, cot, late,
        down_weight, down_bias.astype(F32)[None], up_weight, up_bias.astype(F32)[None], norms,
    )
    adapter = lax.psum_scatter(adapter, DP, scatter_dimension=0, tiled=True)

    def summed(x, axes):
        arrived = lax.all_to_all(x, axes, split_axis=0, concat_axis=0, tiled=True)
        return jnp.sum(arrived.astype(F32), axis=0)

    cdq, dmem = cross_backward(own_src, gtwo, late, cq, mk, mv, mem_groups)
    memory_grad = lax.all_to_all(dmem, MEM, split_axis=0, concat_axis=0, tiled=True)
    gone, dq, dk, dv, small = self_backward(
        tgt_len, gtwo, cdq, late, nrm1, inv1, norms, q, k, v, pk, pv
    )
    dq, small, memory_grad = lax.optimization_barrier((dq, small, memory_grad))
    small = summed(small.reshape(lax.axis_size(DP), -1, PAIR), DP)
    din = input_gradient(gone, dq, dk, dv, early)
    adapt = down_weight.shape[1]
    tail = (adapter[:, 2 * adapt :].astype(F32) + small).astype(BF)
    joined = jnp.concatenate([adapter[:, : 2 * adapt], tail], axis=1)
    total = summed(joined.reshape(mem_groups, -1, joined.shape[1]), MEM)
    last = total[:, 2 * adapt :]
    return (
        output.reshape(tokens.shape),
        din.reshape(tokens.shape),
        memory_grad.reshape(memory.shape),
        last[:, :prefix].T,
        last[:, PREFIX_PAD : PREFIX_PAD + prefix].T,
        total[:, :adapt],
        last[:BIAS_ROWS, 2 * PREFIX_PAD + 1],
        total[:, adapt : 2 * adapt].T,
        last[:, 2 * PREFIX_PAD],
    )


def solution(mesh):
    torus = Mesh(mesh.devices.reshape(4, 2, 4, 4), ("dp_0", "dp_1", "mem_0", "mem_1"))
    by_dp = P(DP, None)
    copied = P(None)
    return jax.shard_map(
        local,
        mesh=torus,
        in_specs=(
            P(DP_MEM, None, None), P(DP, MEM, None), P(DP_MEM, None, None), P(DP_MEM), P(DP),
            by_dp, by_dp, by_dp, by_dp, by_dp, by_dp, by_dp,
            P(DP), P(DP), P(DP), P(DP), P(DP), P(DP),
            copied, copied, copied, copied, copied, copied,
        ),
        out_specs=(
            P(DP_MEM, None, None),
            P(DP_MEM, None, None),
            P(DP, MEM, None),
            P(None, DP_MEM),
            P(None, DP_MEM),
            P(DP_MEM, None),
            P(DP_MEM),
            P(None, DP_MEM),
            P(DP_MEM),
        ),
        check_vma=False,
    )
```

```python
import functools

import jax
import jax.numpy as jnp
from jax import lax
from jax.experimental import pallas as pl
from jax.experimental.pallas import tpu as pltpu
from jax.sharding import Mesh
from jax.sharding import PartitionSpec as P

HEAD_DIM = 64
PAIR = 128
GROUP = 256
PREFIX = 30
PREFIX_PAD = 32
BIAS_ROWS = 4
MEM = ("mem_0", "mem_1")
DP = ("dp_0", "dp_1")
DP_MEM = ("dp_0", "dp_1", "mem_0", "mem_1")

NEGATIVE = -1e30
EPSILON = 1e-05
SCALE = HEAD_DIM ** (-0.5)
BF = jnp.bfloat16
F32 = jnp.float32
SPREAD = 4
STRIP = 128
FFN_BLOCK = 1024
FF_AT = 0
IN_AT = 4096
OUT_AT = 8192
SOUT_AT = 9216
CQ_AT = 10240
KV_AT = 11264
VMEM_BYTES = 60 * 1024 * 1024


def dot_nn(left, right):
    return lax.dot_general(left, right, (((1,), (0,)), ((), ())), preferred_element_type=F32)


def dot_nt(left, right):
    return lax.dot_general(left, right, (((1,), (1,)), ((), ())), preferred_element_type=F32)


def dot_tn(left, right):
    return lax.dot_general(left, right, (((0,), (0,)), ((), ())), preferred_element_type=F32)


def per_head(x):
    lane = lax.broadcasted_iota(jnp.int32, (1, GROUP), 1)
    return [
        x * jnp.where(lane // HEAD_DIM == h, 1.0, 0.0).astype(BF)
        for h in range(GROUP // HEAD_DIM)
    ]


def stacked(parts):
    return jnp.concatenate(parts, axis=0)


def beside(parts):
    return jnp.concatenate(parts, axis=1)


def cut(x, count, axis):
    size = x.shape[axis] // count
    return [lax.slice_in_dim(x, i * size, (i + 1) * size, axis=axis) for i in range(count)]


def norm_stats(hidden):
    centred = hidden - jnp.mean(hidden, axis=-1, keepdims=True)
    inverse = lax.rsqrt(jnp.mean(centred * centred, axis=-1, keepdims=True) + EPSILON)
    return centred * inverse, inverse


def norm_back(grad_in, normed, inverse, gain):
    scaled = grad_in * gain
    return inverse * (
        scaled
        - jnp.mean(scaled, axis=-1, keepdims=True)
        - normed * jnp.mean(scaled * normed, axis=-1, keepdims=True)
    )


def gelu_both(pre):
    cdf = 0.5 * (1.0 + lax.erf(pre * (0.5**0.5)))
    density = jnp.exp(-0.5 * pre * pre) * 0.3989422804014327
    return pre * cdf, cdf + pre * density


def self_forward_kernel(
    len_ref, tok_ref, wq_ref, wk_ref, wv_ref, pk_ref, pv_ref,
    q_ref, k_ref, v_ref, att_ref,
):
    seqs = len_ref.shape[0]
    rows_all = tok_ref.shape[0]
    tgt = rows_all // seqs
    projected = dot_nn(tok_ref[...], beside([wq_ref[...], wk_ref[...], wv_ref[...]])).astype(BF)
    q_ref[...] = projected[:, :GROUP]
    k_ref[...] = projected[:, GROUP : 2 * GROUP]
    v_ref[...] = projected[:, 2 * GROUP :]
    heads = GROUP // HEAD_DIM
    row = lax.broadcasted_iota(jnp.int32, (tgt, tgt), 0)
    col = lax.broadcasted_iota(jnp.int32, (tgt, tgt), 1)
    prefix_bias = jnp.where(
        lax.broadcasted_iota(jnp.int32, (1, PREFIX_PAD), 1) < PREFIX, 0.0, NEGATIVE
    )
    pk = per_head(pk_ref[...])
    pv = per_head(pv_ref[...])
    ones = stacked(
        per_head(jnp.ones((PREFIX_PAD, GROUP), BF)) + per_head(jnp.ones((tgt, GROUP), BF))
    )
    scores = []
    for s in range(seqs):
        here = pl.ds(s * tgt, tgt)
        scores.append(dot_nt(q_ref[here, :] * SCALE, stacked(pk + per_head(k_ref[here, :]))))
    for s in range(seqs):
        here = pl.ds(s * tgt, tgt)
        bias = jnp.where((col <= row) & (col < len_ref[s]), 0.0, NEGATIVE)
        pre = cut(scores[s][:, : heads * PREFIX_PAD], heads, 1)
        own = cut(scores[s][:, heads * PREFIX_PAD :], heads, 1)
        own_probs, pre_probs = [], []
        for x, y in zip(own, pre):
            x = x + bias
            y = y + prefix_bias
            top = jnp.maximum(jnp.max(x, axis=1, keepdims=True), jnp.max(y, axis=1, keepdims=True))
            own_probs.append(jnp.exp(x - top).astype(BF))
            pre_probs.append(jnp.exp(y - top).astype(BF))
        probs = beside(pre_probs + own_probs)
        total = dot_nn(probs, stacked(pv + per_head(v_ref[here, :])))
        att_ref[here, :] = (total / dot_nn(probs, ones)).astype(BF)


def cross_forward_kernel(
    len_ref, mem_ref, wk_ref, wv_ref, tok_ref, self_ref, wo_ref, wcq_ref, norm_ref,
    mk_ref, mv_ref, cq_ref, nrm1_ref, inv1_ref, att_ref,
):
    step = pl.program_id(0)
    seqs = len_ref.shape[0]
    tgt = tok_ref.shape[0] // seqs
    src = mem_ref.shape[0] // seqs

    @pl.when(step == 0)
    def _():
        for s in range(seqs):
            r = pl.ds(s * tgt, tgt)
            nrm, inv = norm_stats(
                tok_ref[r, :].astype(F32) + dot_nn(self_ref[r, :], wo_ref[...])
            )
            nrm1_ref[r, :] = nrm
            inv1_ref[r, :] = inv
            first = nrm * norm_ref[0:1, :] + norm_ref[1:2, :]
            cq_ref[r, :] = dot_nn(first.astype(BF), wcq_ref[...]).astype(BF)

    mem = mem_ref[...]
    projected = dot_nn(mem, beside([wk_ref[...], wv_ref[...]])).astype(BF)
    mk_ref[...] = projected[:, :GROUP]
    mv_ref[...] = projected[:, GROUP:]
    heads = GROUP // HEAD_DIM
    lanes = pl.ds(pl.multiple_of(step * GROUP, GROUP), GROUP)
    slot = lax.broadcasted_iota(jnp.int32, (1, src), 1)
    ones = stacked(per_head(jnp.ones((src, GROUP), BF)))
    scores = []
    for s in range(seqs):
        q = cq_ref[s * tgt : (s + 1) * tgt, lanes] * SCALE
        scores.append(dot_nt(q, stacked(per_head(mk_ref[s * src : (s + 1) * src, :]))))
    for s in range(seqs):
        bias = jnp.where(slot < len_ref[s], 0.0, NEGATIVE)
        probs = []
        for x in cut(scores[s], heads, 1):
            x = x + bias
            probs.append(jnp.exp(x - jnp.max(x, axis=1, keepdims=True)).astype(BF))
        probs = beside(probs)
        total = dot_nn(probs, stacked(per_head(mv_ref[s * src : (s + 1) * src, :])))
        att_ref[s * tgt : (s + 1) * tgt, :] = (total / dot_nn(probs, ones)).astype(BF)


def ffn_kernel(
    len_ref, nrm1_ref, att_ref, wco_ref, cot_ref, win_ref, wff_ref, down_ref, db_ref, up_ref, ub_ref,
    norm_ref,
    out_ref, gtwo_ref, adapt_ref,
    nrm2_ref, inv2_ref, acc_ref, low_ref, slope_ref, aact_ref, aslope_ref, g_ref,
    cot_here, down_here, up_here, out_here, adapt_here, sems,
):
    phase = pl.program_id(0)
    j = pl.program_id(1)
    last = pl.num_programs(1) - 1
    seqs = len_ref.shape[0]
    rows_all = nrm1_ref.shape[0]
    tgt = rows_all // seqs
    half = rows_all // 2
    width = nrm1_ref.shape[1]
    strip = wff_ref.shape[0] // (win_ref.shape[1] // (SPREAD * STRIP))
    wff = stacked(
        [
            wff_ref[c : c + strip, b * width : (b + 1) * width]
            for c in range(0, wff_ref.shape[0], strip)
            for b in range(SPREAD)
        ]
    )

    cot_in = pltpu.make_async_copy(cot_ref, cot_here, sems.at[0])
    down_in = pltpu.make_async_copy(down_ref, down_here, sems.at[1])
    up_in = pltpu.make_async_copy(up_ref, up_here, sems.at[2])
    out_back = pltpu.make_async_copy(out_here, out_ref, sems.at[3])
    adapt_back = pltpu.make_async_copy(adapt_here, adapt_ref, sems.at[4])

    @pl.when((phase == 0) & (j == 0))
    def _():
        down_in.start()
        up_in.start()
        cot_in.start()
        for b in range(2):
            r = pl.ds(b * half, half)
            first = nrm1_ref[r, :] * norm_ref[0:1, :] + norm_ref[1:2, :]
            nrm, inv = norm_stats(first + dot_nn(att_ref[r, :], wco_ref[...]))
            nrm2_ref[r, :] = nrm
            inv2_ref[r, :] = inv
            second = nrm * norm_ref[2:3, :] + norm_ref[3:4, :]
            low_ref[r, :] = second.astype(BF)
            acc_ref[r, :] = second

    @pl.when(phase == 0)
    def _():
        act, slope = gelu_both(dot_nn(low_ref[...], win_ref[...]))
        slope_ref[j] = slope.astype(BF)
        acc_ref[...] += dot_nn(act.astype(BF), wff)

    @pl.when((phase == 1) & (j == 0))
    def _():
        down_in.wait()
        up_in.wait()
        cot_in.wait()
        act, slope = gelu_both(dot_nn(low_ref[...], down_here[...]) + db_ref[...])
        aact_ref[...] = act.astype(BF)
        aslope_ref[...] = slope.astype(BF)
        for s in range(seqs):
            r = pl.ds(s * tgt, tgt)
            adapted = dot_nn(aact_ref[r, :], up_here[...]) + ub_ref[...]
            nrm, inv = norm_stats(acc_ref[r, :] + 4.0 * adapted)
            out_here[r, :] = (nrm * norm_ref[4:5, :] + norm_ref[5:6, :]).astype(BF)
            live = lax.broadcasted_iota(jnp.int32, (tgt, 1), 0) < len_ref[s]
            go = jnp.where(live, cot_here[r, :].astype(F32), 0.0)
            gthree = norm_back(go, nrm, inv, norm_ref[4:5, :])
            g_ref[r, :] = gthree.astype(BF)
            acc_ref[r, :] = gthree
        out_back.start()
        agrad = g_ref[...] * 4.0
        adapt = aact_ref.shape[1]
        apg = (dot_nt(agrad, up_here[...]) * aslope_ref[...].astype(F32)).astype(BF)
        adapt_here[:, :adapt] = dot_tn(low_ref[...], apg).astype(BF)
        adapt_here[:, adapt : 2 * adapt] = dot_tn(agrad, aact_ref[...]).astype(BF)
        ones = jnp.ones((rows_all, PAIR), BF)
        down_sum = dot_tn(apg, ones).astype(BF)
        high = width // adapt
        row = lax.broadcasted_iota(jnp.int32, (width, adapt), 0)
        col = lax.broadcasted_iota(jnp.int32, (width, adapt), 1)
        block = BIAS_ROWS * high
        entry = lax.div(row, block) * BIAS_ROWS + lax.rem(row, block)
        chosen = (entry == col) & (lax.rem(row, block) < BIAS_ROWS)
        placed = dot_nn(jnp.where(chosen, 1.0, 0.0).astype(BF), down_sum)
        lane = lax.broadcasted_iota(jnp.int32, (width, PAIR), 1)
        sums = jnp.where(lane == 2 * PREFIX_PAD, dot_tn(agrad, ones), placed)
        sums = jnp.where((lane >= 2 * PREFIX_PAD) & (lane < 2 * PREFIX_PAD + 2), sums, 0.0)
        adapt_here[:, 2 * adapt :] = sums.astype(BF)
        adapt_back.start()
        acc_ref[...] += dot_nt(apg, down_here[...])

    @pl.when(phase == 1)
    def _():
        grad = (dot_nt(g_ref[...], wff) * slope_ref[j].astype(F32)).astype(BF)
        acc_ref[...] += dot_nt(grad, win_ref[...])

    @pl.when((phase == 1) & (j == last))
    def _():
        gtwo_ref[...] = norm_back(acc_ref[...], nrm2_ref[...], inv2_ref[...], norm_ref[2:3, :])
        out_back.wait()
        adapt_back.wait()


def cross_backward_kernel(
    len_ref, gtwo_ref, wco_ref, cq_ref, mk_ref, mv_ref, wk_ref, wv_ref,
    dq_ref, dmem_ref, low_ref, acc_ref, dk_ref, dv_ref,
):
    step = pl.program_id(0)
    seqs = len_ref.shape[0]
    tgt = cq_ref.shape[0] // seqs
    src = mk_ref.shape[0] // seqs

    @pl.when(step == 0)
    def _():
        low_ref[...] = gtwo_ref[...].astype(BF)
        acc_ref[...] = jnp.zeros_like(acc_ref)

    mg_all = dot_nt(low_ref[...], wco_ref[...]).astype(BF)
    heads = GROUP // HEAD_DIM
    slot = lax.broadcasted_iota(jnp.int32, (src, tgt), 0)
    for s in range(seqs):
        bias = jnp.where(slot < len_ref[s], 0.0, NEGATIVE)
        here = pl.ds(s * tgt, tgt)
        there = pl.ds(s * src, src)
        q = cq_ref[here, :] * SCALE
        mg = mg_all[s * tgt : (s + 1) * tgt]
        k = mk_ref[there, :]
        scores = cut(dot_nt(stacked(per_head(k)), q), heads, 0)
        dprobs = cut(dot_nt(stacked(per_head(mv_ref[there, :])), mg), heads, 0)
        probs, grads = [], []
        for x, d in zip(scores, dprobs):
            x = x + bias
            x = jnp.exp(x - jnp.max(x, axis=0, keepdims=True))
            x = x * (1.0 / jnp.sum(x, axis=0, keepdims=True))
            grads.append((x * (d - jnp.sum(x * d, axis=0, keepdims=True))).astype(BF))
            probs.append(x.astype(BF))
        dq = dot_tn(stacked(grads), stacked(per_head(k)))
        dq_ref[here, :] = (dq * SCALE).astype(BF)
        dk_ref[there, :] = dot_nn(beside(grads), stacked(per_head(q))).astype(BF)
        dv_ref[there, :] = dot_nn(beside(probs), stacked(per_head(mg))).astype(BF)
    acc_ref[...] += dot_nt(
        beside([dk_ref[...], dv_ref[...]]), beside([wk_ref[...], wv_ref[...]])
    )

    @pl.when(step == pl.num_programs(0) - 1)
    def _():
        parts, _, high, width = dmem_ref.shape
        for s in range(seqs):
            block = acc_ref[s * src : (s + 1) * src, :]
            dmem_ref[:, s] = block.reshape(parts, high, width).astype(BF)


def self_backward_kernel(
    len_ref, gtwo_ref, cdq_ref, wcq_ref, nrm1_ref, inv1_ref, norm_ref,
    wo_ref, q_ref, k_ref, v_ref, pk_ref, pv_ref,
    gone_ref, dq_ref, dk_ref, dv_ref, small_ref, low_ref,
):
    step = pl.program_id(0)
    seqs = len_ref.shape[0]
    tgt = gtwo_ref.shape[0] // seqs

    @pl.when(step == 0)
    def _():
        grad_first = gtwo_ref[...] + dot_nt(cdq_ref[...], wcq_ref[...])
        grad_one = norm_back(grad_first, nrm1_ref[...], inv1_ref[...], norm_ref[0:1, :])
        gone_ref[...] = grad_one
        low_ref[...] = grad_one.astype(BF)

    ag_all = dot_nt(low_ref[...], wo_ref[...]).astype(BF)
    heads = GROUP // HEAD_DIM
    row = lax.broadcasted_iota(jnp.int32, (tgt, tgt), 1)
    col = lax.broadcasted_iota(jnp.int32, (tgt, tgt), 0)
    prefix_bias = jnp.where(
        lax.broadcasted_iota(jnp.int32, (PREFIX_PAD, tgt), 0) < PREFIX, 0.0, NEGATIVE
    )
    pk = per_head(pk_ref[...])
    pv = per_head(pv_ref[...])
    dpk = jnp.zeros((PREFIX_PAD, GROUP), F32)
    dpv = jnp.zeros((PREFIX_PAD, GROUP), F32)
    split = heads * PREFIX_PAD
    for s in range(seqs):
        bias = jnp.where((col <= row) & (col < len_ref[s]), 0.0, NEGATIVE)
        here = pl.ds(s * tgt, tgt)
        q = q_ref[here, :] * SCALE
        ag = ag_all[s * tgt : (s + 1) * tgt]
        keys = stacked(pk + per_head(k_ref[here, :]))
        scores = dot_nt(keys, q)
        dprobs = dot_nt(stacked(pv + per_head(v_ref[here, :])), ag)
        probs, grads = [], []
        for x, d, y, e in zip(
            cut(scores[split:], heads, 0),
            cut(dprobs[split:], heads, 0),
            cut(scores[:split], heads, 0),
            cut(dprobs[:split], heads, 0),
        ):
            x = x + bias
            y = y + prefix_bias
            top = jnp.maximum(jnp.max(x, axis=0, keepdims=True), jnp.max(y, axis=0, keepdims=True))
            x = jnp.exp(x - top)
            y = jnp.exp(y - top)
            inv = 1.0 / (jnp.sum(x, axis=0, keepdims=True) + jnp.sum(y, axis=0, keepdims=True))
            x = x * inv
            y = y * inv
            delta = jnp.sum(x * d, axis=0, keepdims=True) + jnp.sum(y * e, axis=0, keepdims=True)
            grads.append([(y * (e - delta)).astype(BF), (x * (d - delta)).astype(BF)])
            probs.append(stacked([y.astype(BF), x.astype(BF)]))
        dq = dot_tn(stacked([g[0] for g in grads] + [g[1] for g in grads]), keys)
        dk = dot_nn(beside([stacked(g) for g in grads]), stacked(per_head(q)))
        dv = dot_nn(beside(probs), stacked(per_head(ag)))
        dq_ref[here, :] = (dq * SCALE).astype(BF)
        dk_ref[here, :] = dk[PREFIX_PAD:].astype(BF)
        dv_ref[here, :] = dv[PREFIX_PAD:].astype(BF)
        dpk = dpk + dk[:PREFIX_PAD]
        dpv = dpv + dv[:PREFIX_PAD]
    for p in range(GROUP // PAIR):
        at = slice(p * PAIR, (p + 1) * PAIR)
        both = stacked(
            [dpk[:, at], dpv[:, at], jnp.zeros((PAIR - 2 * PREFIX_PAD, PAIR), F32)]
        )
        small_ref[at, :] = both.T


def input_grad_kernel(gone_ref, dq_ref, dk_ref, dv_ref, wq_ref, wk_ref, wv_ref, din_ref):
    din_ref[...] = (
        gone_ref[...]
        + dot_nt(
            beside([dq_ref[...], dk_ref[...], dv_ref[...]]),
            beside([wq_ref[...], wk_ref[...], wv_ref[...]]),
        )
    ).astype(BF)


ANYWHERE = pl.BlockSpec(memory_space=pl.ANY)


def square(width, at):
    return pl.BlockSpec((width, width), lambda *_: (0, at // width))


def whole(shape):
    return pl.BlockSpec(shape, lambda *_: (0,) * len(shape))


def columns(rows, width, offset=0):
    return pl.BlockSpec((rows, width), lambda i, *_: (0, i + offset))


def rows_of(height, width, at):
    return pl.BlockSpec((height, width), lambda i, *_: (i, at // width))


def shaped(shape, dtype):
    return jax.ShapeDtypeStruct(shape, dtype)


def call(kernel, grid, in_specs, out_specs, outs, scratch, flops, moved, *args):
    return pl.pallas_call(
        kernel,
        grid_spec=pltpu.PrefetchScalarGridSpec(
            num_scalar_prefetch=1,
            grid=grid,
            in_specs=in_specs,
            out_specs=out_specs,
            scratch_shapes=scratch,
        ),
        out_shape=outs,
        compiler_params=pltpu.CompilerParams(
            vmem_limit_bytes=VMEM_BYTES,
            dimension_semantics=("arbitrary",) * len(grid),
        ),
        cost_estimate=pl.CostEstimate(flops=flops, bytes_accessed=moved, transcendentals=0),
    )(*args)


def self_forward(lens, tok, early, pk, pv):
    rows, width = tok.shape
    steps = width // GROUP
    return call(
        self_forward_kernel,
        (steps,),
        [
            whole((rows, width)),
            columns(width, GROUP),
            columns(width, GROUP, steps),
            columns(width, GROUP, 2 * steps),
            columns(PREFIX_PAD, GROUP),
            columns(PREFIX_PAD, GROUP),
        ],
        [columns(rows, GROUP)] * 4,
        [shaped((rows, width), BF)] * 4,
        [],
        2 * rows * width * width * 3,
        14 * width * width,
        lens, tok, early, early, early, pk, pv,
    )


def cross_forward(lens, mem, late, tok, att, norms):
    rows, width = tok.shape
    steps = width // GROUP
    places = mem.shape[0]
    return call(
        cross_forward_kernel,
        (steps,),
        [
            whole((places, width)),
            columns(width, GROUP, KV_AT // GROUP),
            columns(width, GROUP, KV_AT // GROUP + steps),
            whole((rows, width)),
            whole((rows, width)),
            square(width, SOUT_AT),
            square(width, CQ_AT),
            whole(norms.shape),
        ],
        [columns(places, GROUP)] * 2
        + [whole((rows, width)), whole((rows, width)), whole((rows, 1)), columns(rows, GROUP)],
        [shaped((places, width), BF)] * 2
        + [shaped((rows, width), BF), shaped((rows, width), F32), shaped((rows, 1), F32)]
        + [shaped((rows, width), BF)],
        [],
        2 * width * width * (2 * rows + 2 * places),
        16 * width * width,
        lens, mem, late, late, tok, att, late, late, norms,
    )


def ffn(lens, nrm1, att, cot, late, down, db, up, ub, norms):
    rows, width = nrm1.shape
    hidden = SPREAD * width
    adapt = down.shape[1]
    block = FFN_BLOCK
    steps = hidden // block
    return call(
        ffn_kernel,
        (2, steps),
        [
            whole((rows, width)),
            whole((rows, width)),
            square(width, OUT_AT),
            ANYWHERE,
            pl.BlockSpec((width, block), lambda p, j, *_: (0, j + IN_AT // block)),
            pl.BlockSpec((block // SPREAD, SPREAD * width), lambda p, j, *_: (j, FF_AT)),
            ANYWHERE,
            whole((1, adapt)),
            ANYWHERE,
            whole((1, width)),
            whole(norms.shape),
        ],
        [ANYWHERE, whole((rows, width)), ANYWHERE],
        [
            shaped((rows, width), BF),
            shaped((rows, width), F32),
            shaped((width, 2 * adapt + PAIR), BF),
        ],
        [
            pltpu.VMEM((rows, width), F32),
            pltpu.VMEM((rows, 1), F32),
            pltpu.VMEM((rows, width), F32),
            pltpu.VMEM((rows, width), BF),
            pltpu.VMEM((steps, rows, block), BF),
            pltpu.VMEM((rows, adapt), BF),
            pltpu.VMEM((rows, adapt), BF),
            pltpu.VMEM((rows, width), BF),
            pltpu.VMEM((rows, width), BF),
            pltpu.VMEM((width, adapt), BF),
            pltpu.VMEM((adapt, width), BF),
            pltpu.VMEM((rows, width), BF),
            pltpu.VMEM((width, 2 * adapt + PAIR), BF),
            pltpu.SemaphoreType.DMA((5,)),
        ],
        2 * rows * width * (4 * hidden + 6 * adapt),
        8 * width * hidden,
        lens, nrm1, att, late, cot, late, late, down, db, up, ub, norms,
    )


def cross_backward(lens, gtwo, late, cq, mk, mv, parts):
    rows, width = cq.shape
    steps = width // GROUP
    places = mk.shape[0]
    seqs = lens.shape[0]
    sent = (parts, seqs, places // seqs // parts, width)
    return call(
        cross_backward_kernel,
        (steps,),
        [
            whole((rows, width)),
            rows_of(GROUP, width, OUT_AT),
            columns(rows, GROUP),
            columns(places, GROUP),
            columns(places, GROUP),
            columns(width, GROUP, KV_AT // GROUP),
            columns(width, GROUP, KV_AT // GROUP + steps),
        ],
        [columns(rows, GROUP), whole(sent)],
        [shaped((rows, width), BF), shaped(sent, BF)],
        [
            pltpu.VMEM((rows, width), BF),
            pltpu.VMEM((places, width), F32),
            pltpu.VMEM((places, GROUP), BF),
            pltpu.VMEM((places, GROUP), BF),
        ],
        2 * width * width * (rows + 2 * places),
        14 * width * width,
        lens, gtwo, late, cq, mk, mv, late, late,
    )


def self_backward(lens, gtwo, cdq, late, nrm1, inv1, norms, q, k, v, pk, pv):
    rows, width = q.shape
    steps = width // GROUP
    return call(
        self_backward_kernel,
        (steps,),
        [
            whole((rows, width)),
            whole((rows, width)),
            square(width, CQ_AT),
            whole((rows, width)),
            whole((rows, 1)),
            whole(norms.shape),
            rows_of(GROUP, width, SOUT_AT),
            columns(rows, GROUP),
            columns(rows, GROUP),
            columns(rows, GROUP),
            columns(PREFIX_PAD, GROUP),
            columns(PREFIX_PAD, GROUP),
        ],
        [whole((rows, width))]
        + [columns(rows, GROUP)] * 3
        + [pl.BlockSpec((GROUP, PAIR), lambda i, *_: (i, 0))],
        [shaped((rows, width), F32)]
        + [shaped((rows, width), BF)] * 3
        + [shaped((width, PAIR), F32)],
        [pltpu.VMEM((rows, width), BF)],
        2 * rows * width * width * 4,
        20 * width * width,
        lens, gtwo, cdq, late, nrm1, inv1, norms, late, q, k, v, pk, pv,
    )


def input_gradient(gone, dq, dk, dv, early):
    rows, width = gone.shape

    def part(index):
        return pl.BlockSpec((GROUP, width), lambda i: (i, index))

    return pl.pallas_call(
        input_grad_kernel,
        grid=(width // GROUP,),
        in_specs=[pl.BlockSpec((rows, GROUP), lambda i: (0, i))]
        + [whole((rows, width))] * 3
        + [part(0), part(1), part(2)],
        out_specs=pl.BlockSpec((rows, GROUP), lambda i: (0, i)),
        out_shape=shaped((rows, width), BF),
        compiler_params=pltpu.CompilerParams(
            vmem_limit_bytes=VMEM_BYTES, dimension_semantics=("arbitrary",)
        ),
        cost_estimate=pl.CostEstimate(
            flops=6 * rows * width * width, bytes_accessed=12 * width * width, transcendentals=0
        ),
    )(gone, dq, dk, dv, early, early, early)


def around(count, by):
    return [(i, (i + by) % count) for i in range(count)]


def ring_gather(shard, other):
    rows = shard.shape[0]
    half = rows // 2
    count = lax.axis_size("dp_0")
    x, core = lax.axis_index("dp_0"), lax.axis_index("dp_1")
    below = lax.ppermute(shard, "dp_0", around(count, 1))
    above = lax.ppermute(shard, "dp_0", around(count, -1))
    filled = jnp.zeros((count * 2 * rows, shard.shape[1]), shard.dtype)
    filled, other = lax.optimization_barrier((filled, other))
    far_low = lax.ppermute(below[:half], "dp_0", around(count, 1))
    far_high = lax.ppermute(above[half:], "dp_0", around(count, -1))
    for piece, offset, start in (
        (shard, 0, 0), (below, -1, 0), (above, 1, 0), (far_low, 2, 0), (far_high, 2, half),
    ):
        swapped = lax.ppermute(piece, "dp_1", around(2, 1))
        chip = (x + offset + count) % count
        for part, place in ((piece, core), (swapped, 1 - core)):
            at = (chip * 2 + place) * rows + start
            filled = lax.dynamic_update_slice_in_dim(filled, part, at, 0)
    return filled, other


def scatter_sum(blocks):
    count = lax.axis_size("dp_0")
    x, core = lax.axis_index("dp_0"), lax.axis_index("dp_1")
    by_core = blocks.reshape(count, 2, *blocks.shape[1:])
    kept = lax.dynamic_index_in_dim(by_core, core, 1, keepdims=False)
    given = lax.dynamic_index_in_dim(by_core, 1 - core, 1, keepdims=False)
    paired = kept + lax.ppermute(given, "dp_1", around(2, 1))
    total = lax.dynamic_index_in_dim(paired, x, 0, keepdims=False)
    for by in range(1, count):
        sent = lax.dynamic_index_in_dim(paired, (x + by) % count, 0, keepdims=False)
        total = total + lax.ppermute(sent, "dp_0", around(count, by))
    return total


def local(
    tokens, memory, cotangent, tgt_len, src_len,
    self_qkv, self_out, cross_q, cross_kv, cross_out, ffn_in, ffn_out,
    first_gain, first_bias, second_gain, second_bias, third_gain, third_bias,
    prefix_key, prefix_value, down_weight, down_bias, up_weight, up_bias,
):
    mem_groups = lax.axis_size(MEM)
    mem_place = lax.axis_index(MEM)
    seqs, tgt, width = tokens.shape
    src_block = memory.shape[1]
    prefix = prefix_key.shape[0]

    high = cross_out.shape[0] // mem_groups
    mine = functools.partial(
        lax.dynamic_slice_in_dim, start_index=mem_place * high, slice_size=high
    )
    spread = mine(ffn_out.reshape(SPREAD, -1, width), axis=1)
    late = lax.all_gather(
        jnp.concatenate(
            [jnp.moveaxis(spread, 0, 1).reshape(high, SPREAD * width)]
            + [mine(w, axis=0) for w in (ffn_in, cross_out, self_out, cross_q, cross_kv)],
            axis=1,
        ),
        DP_MEM, axis=0, tiled=True,
    )
    early, memory = ring_gather(self_qkv, memory)
    mem_rows = lax.all_to_all(memory, MEM, split_axis=0, concat_axis=1, tiled=True)
    mem_rows = mem_rows.reshape(-1, width)
    own_src = lax.dynamic_slice_in_dim(src_len, mem_place * seqs, seqs, 0)

    tok = tokens.reshape(seqs * tgt, width)
    cot = cotangent.reshape(seqs * tgt, width)
    pk = jnp.pad(prefix_key, ((0, PREFIX_PAD - prefix), (0, 0)))
    pv = jnp.pad(prefix_value, ((0, PREFIX_PAD - prefix), (0, 0)))

    q, k, v, att = self_forward(tgt_len, tok, early, pk, pv)
    vectors = jnp.stack(
        [first_gain, first_bias, second_gain, second_bias, third_gain, third_bias]
        + [third_bias] * 2
    )
    vectors, att = lax.optimization_barrier((vectors, att))
    norms = lax.all_gather(vectors, DP, axis=1, tiled=True).astype(F32)
    mk, mv, cq, nrm1, inv1, cross = cross_forward(own_src, mem_rows, late, tok, att, norms)
    output, gtwo, adapter = ffn(
        tgt_len, nrm1, cross, cot, late,
        down_weight, down_bias.astype(F32)[None], up_weight, up_bias.astype(F32)[None], norms,
    )
    adapter = lax.psum_scatter(adapter, DP, scatter_dimension=0, tiled=True)

    def summed(x, axes):
        arrived = lax.all_to_all(x, axes, split_axis=0, concat_axis=0, tiled=True)
        return jnp.sum(arrived.astype(F32), axis=0)

    cdq, dmem = cross_backward(own_src, gtwo, late, cq, mk, mv, mem_groups)
    memory_grad = lax.all_to_all(dmem, MEM, split_axis=0, concat_axis=0, tiled=True)
    gone, dq, dk, dv, small = self_backward(
        tgt_len, gtwo, cdq, late, nrm1, inv1, norms, q, k, v, pk, pv
    )
    small = scatter_sum(small.reshape(lax.axis_size(DP), -1, PAIR))
    dq, small, memory_grad = lax.optimization_barrier((dq, small, memory_grad))
    din = input_gradient(gone, dq, dk, dv, early)
    adapt = down_weight.shape[1]
    tail = (adapter[:, 2 * adapt :].astype(F32) + small).astype(BF)
    joined = jnp.concatenate([adapter[:, : 2 * adapt], tail], axis=1)
    total = summed(joined.reshape(mem_groups, -1, joined.shape[1]), MEM)
    last = total[:, 2 * adapt :]
    return (
        output.reshape(tokens.shape),
        din.reshape(tokens.shape),
        memory_grad.reshape(memory.shape),
        last[:, :prefix].T,
        last[:, PREFIX_PAD : PREFIX_PAD + prefix].T,
        total[:, :adapt],
        last[:BIAS_ROWS, 2 * PREFIX_PAD + 1],
        total[:, adapt : 2 * adapt].T,
        last[:, 2 * PREFIX_PAD],
    )


def solution(mesh):
    torus = Mesh(mesh.devices.reshape(4, 2, 4, 4), ("dp_0", "dp_1", "mem_0", "mem_1"))
    by_dp = P(DP, None)
    copied = P(None)
    return jax.shard_map(
        local,
        mesh=torus,
        in_specs=(
            P(DP_MEM, None, None), P(DP, MEM, None), P(DP_MEM, None, None), P(DP_MEM), P(DP),
            by_dp, by_dp, by_dp, by_dp, by_dp, by_dp, by_dp,
            P(DP), P(DP), P(DP), P(DP), P(DP), P(DP),
            copied, copied, copied, copied, copied, copied,
        ),
        out_specs=(
            P(DP_MEM, None, None),
            P(DP_MEM, None, None),
            P(DP, MEM, None),
            P(None, DP_MEM),
            P(None, DP_MEM),
            P(DP_MEM, None),
            P(DP_MEM),
            P(None, DP_MEM),
            P(DP_MEM),
        ),
        check_vma=False,
    )
```

```python
import functools

import jax
import jax.numpy as jnp
from jax import lax
from jax.experimental import pallas as pl
from jax.experimental.pallas import tpu as pltpu
from jax.sharding import Mesh
from jax.sharding import PartitionSpec as P

HEAD_DIM = 64
PAIR = 128
GROUP = 256
PREFIX = 30
PREFIX_PAD = 32
BIAS_ROWS = 4
MEM = ("mem_0", "mem_1")
DP = ("dp_0", "dp_1")
DP_MEM = ("dp_0", "dp_1", "mem_0", "mem_1")

NEGATIVE = -1e30
EPSILON = 1e-05
SCALE = HEAD_DIM ** (-0.5)
BF = jnp.bfloat16
F32 = jnp.float32
SPREAD = 4
STRIP = 128
FFN_BLOCK = 1024
FF_AT = 0
IN_AT = 4096
OUT_AT = 8192
SOUT_AT = 9216
CQ_AT = 10240
KV_AT = 11264
VMEM_BYTES = 60 * 1024 * 1024


def dot_nn(left, right):
    return lax.dot_general(left, right, (((1,), (0,)), ((), ())), preferred_element_type=F32)


def dot_nt(left, right):
    return lax.dot_general(left, right, (((1,), (1,)), ((), ())), preferred_element_type=F32)


def dot_tn(left, right):
    return lax.dot_general(left, right, (((0,), (0,)), ((), ())), preferred_element_type=F32)


def per_head(x):
    lane = lax.broadcasted_iota(jnp.int32, (1, GROUP), 1)
    return [
        x * jnp.where(lane // HEAD_DIM == h, 1.0, 0.0).astype(BF)
        for h in range(GROUP // HEAD_DIM)
    ]


def stacked(parts):
    return jnp.concatenate(parts, axis=0)


def beside(parts):
    return jnp.concatenate(parts, axis=1)


def cut(x, count, axis):
    size = x.shape[axis] // count
    return [lax.slice_in_dim(x, i * size, (i + 1) * size, axis=axis) for i in range(count)]


def norm_stats(hidden):
    centred = hidden - jnp.mean(hidden, axis=-1, keepdims=True)
    inverse = lax.rsqrt(jnp.mean(centred * centred, axis=-1, keepdims=True) + EPSILON)
    return centred * inverse, inverse


def norm_back(grad_in, normed, inverse, gain):
    scaled = grad_in * gain
    return inverse * (
        scaled
        - jnp.mean(scaled, axis=-1, keepdims=True)
        - normed * jnp.mean(scaled * normed, axis=-1, keepdims=True)
    )


def gelu_both(pre):
    cdf = 0.5 * (1.0 + lax.erf(pre * (0.5**0.5)))
    density = jnp.exp(-0.5 * pre * pre) * 0.3989422804014327
    return pre * cdf, cdf + pre * density


def self_forward_kernel(
    len_ref, tok_ref, wq_ref, wk_ref, wv_ref, pk_ref, pv_ref,
    q_ref, k_ref, v_ref, att_ref,
):
    seqs = len_ref.shape[0]
    rows_all = tok_ref.shape[0]
    tgt = rows_all // seqs
    projected = dot_nn(tok_ref[...], beside([wq_ref[...], wk_ref[...], wv_ref[...]])).astype(BF)
    q_ref[...] = projected[:, :GROUP]
    k_ref[...] = projected[:, GROUP : 2 * GROUP]
    v_ref[...] = projected[:, 2 * GROUP :]
    heads = GROUP // HEAD_DIM
    row = lax.broadcasted_iota(jnp.int32, (tgt, tgt), 0)
    col = lax.broadcasted_iota(jnp.int32, (tgt, tgt), 1)
    prefix_bias = jnp.where(
        lax.broadcasted_iota(jnp.int32, (1, PREFIX_PAD), 1) < PREFIX, 0.0, NEGATIVE
    )
    pk = per_head(pk_ref[...])
    pv = per_head(pv_ref[...])
    ones = stacked(
        per_head(jnp.ones((PREFIX_PAD, GROUP), BF)) + per_head(jnp.ones((tgt, GROUP), BF))
    )
    scores = []
    for s in range(seqs):
        here = pl.ds(s * tgt, tgt)
        scores.append(dot_nt(q_ref[here, :] * SCALE, stacked(pk + per_head(k_ref[here, :]))))
    for s in range(seqs):
        here = pl.ds(s * tgt, tgt)
        bias = jnp.where((col <= row) & (col < len_ref[s]), 0.0, NEGATIVE)
        pre = cut(scores[s][:, : heads * PREFIX_PAD], heads, 1)
        own = cut(scores[s][:, heads * PREFIX_PAD :], heads, 1)
        own_probs, pre_probs = [], []
        for x, y in zip(own, pre):
            x = x + bias
            y = y + prefix_bias
            top = jnp.maximum(jnp.max(x, axis=1, keepdims=True), jnp.max(y, axis=1, keepdims=True))
            own_probs.append(jnp.exp(x - top).astype(BF))
            pre_probs.append(jnp.exp(y - top).astype(BF))
        probs = beside(pre_probs + own_probs)
        total = dot_nn(probs, stacked(pv + per_head(v_ref[here, :])))
        att_ref[here, :] = (total / dot_nn(probs, ones)).astype(BF)


def cross_forward_kernel(
    len_ref, mem_ref, wk_ref, wv_ref, tok_ref, self_ref, wo_ref, wcq_ref, norm_ref,
    mk_ref, mv_ref, cq_ref, nrm1_ref, inv1_ref, att_ref,
):
    step = pl.program_id(0)
    seqs = len_ref.shape[0]
    tgt = tok_ref.shape[0] // seqs
    src = mem_ref.shape[0] // seqs

    @pl.when(step == 0)
    def _():
        for s in range(seqs):
            r = pl.ds(s * tgt, tgt)
            nrm, inv = norm_stats(
                tok_ref[r, :].astype(F32) + dot_nn(self_ref[r, :], wo_ref[...])
            )
            nrm1_ref[r, :] = nrm
            inv1_ref[r, :] = inv
            first = nrm * norm_ref[0:1, :] + norm_ref[1:2, :]
            cq_ref[r, :] = dot_nn(first.astype(BF), wcq_ref[...]).astype(BF)

    mem = mem_ref[...]
    projected = dot_nn(mem, beside([wk_ref[...], wv_ref[...]])).astype(BF)
    mk_ref[...] = projected[:, :GROUP]
    mv_ref[...] = projected[:, GROUP:]
    heads = GROUP // HEAD_DIM
    lanes = pl.ds(pl.multiple_of(step * GROUP, GROUP), GROUP)
    slot = lax.broadcasted_iota(jnp.int32, (1, src), 1)
    ones = stacked(per_head(jnp.ones((src, GROUP), BF)))
    scores = []
    for s in range(seqs):
        q = cq_ref[s * tgt : (s + 1) * tgt, lanes] * SCALE
        scores.append(dot_nt(q, stacked(per_head(mk_ref[s * src : (s + 1) * src, :]))))
    for s in range(seqs):
        bias = jnp.where(slot < len_ref[s], 0.0, NEGATIVE)
        probs = []
        for x in cut(scores[s], heads, 1):
            x = x + bias
            probs.append(jnp.exp(x - jnp.max(x, axis=1, keepdims=True)).astype(BF))
        probs = beside(probs)
        total = dot_nn(probs, stacked(per_head(mv_ref[s * src : (s + 1) * src, :])))
        att_ref[s * tgt : (s + 1) * tgt, :] = (total / dot_nn(probs, ones)).astype(BF)


def ffn_kernel(
    len_ref, nrm1_ref, att_ref, wco_ref, cot_ref, win_ref, wff_ref, down_ref, db_ref, up_ref, ub_ref,
    norm_ref,
    out_ref, gtwo_ref, adapt_ref,
    nrm2_ref, inv2_ref, acc_ref, low_ref, slope_ref, aact_ref, aslope_ref, g_ref,
    cot_here, down_here, up_here, out_here, adapt_here, sems,
):
    phase = pl.program_id(0)
    j = pl.program_id(1)
    last = pl.num_programs(1) - 1
    seqs = len_ref.shape[0]
    rows_all = nrm1_ref.shape[0]
    tgt = rows_all // seqs
    half = rows_all // 2
    width = nrm1_ref.shape[1]
    strip = wff_ref.shape[0] // (win_ref.shape[1] // (SPREAD * STRIP))
    wff = stacked(
        [
            wff_ref[c : c + strip, b * width : (b + 1) * width]
            for c in range(0, wff_ref.shape[0], strip)
            for b in range(SPREAD)
        ]
    )

    cot_in = pltpu.make_async_copy(cot_ref, cot_here, sems.at[0])
    down_in = pltpu.make_async_copy(down_ref, down_here, sems.at[1])
    up_in = pltpu.make_async_copy(up_ref, up_here, sems.at[2])
    out_back = pltpu.make_async_copy(out_here, out_ref, sems.at[3])
    adapt_back = pltpu.make_async_copy(adapt_here, adapt_ref, sems.at[4])

    @pl.when((phase == 0) & (j == 0))
    def _():
        down_in.start()
        up_in.start()
        cot_in.start()
        for b in range(2):
            r = pl.ds(b * half, half)
            first = nrm1_ref[r, :] * norm_ref[0:1, :] + norm_ref[1:2, :]
            nrm, inv = norm_stats(first + dot_nn(att_ref[r, :], wco_ref[...]))
            nrm2_ref[r, :] = nrm
            inv2_ref[r, :] = inv
            second = nrm * norm_ref[2:3, :] + norm_ref[3:4, :]
            low_ref[r, :] = second.astype(BF)
            acc_ref[r, :] = second

    @pl.when(phase == 0)
    def _():
        act, slope = gelu_both(dot_nn(low_ref[...], win_ref[...]))
        slope_ref[j] = slope.astype(BF)
        acc_ref[...] += dot_nn(act.astype(BF), wff)

    @pl.when((phase == 1) & (j == 0))
    def _():
        down_in.wait()
        up_in.wait()
        cot_in.wait()
        act, slope = gelu_both(dot_nn(low_ref[...], down_here[...]) + db_ref[...])
        aact_ref[...] = act.astype(BF)
        aslope_ref[...] = slope.astype(BF)
        for s in range(seqs):
            r = pl.ds(s * tgt, tgt)
            adapted = dot_nn(aact_ref[r, :], up_here[...]) + ub_ref[...]
            nrm, inv = norm_stats(acc_ref[r, :] + 4.0 * adapted)
            out_here[r, :] = (nrm * norm_ref[4:5, :] + norm_ref[5:6, :]).astype(BF)
            live = lax.broadcasted_iota(jnp.int32, (tgt, 1), 0) < len_ref[s]
            go = jnp.where(live, cot_here[r, :].astype(F32), 0.0)
            gthree = norm_back(go, nrm, inv, norm_ref[4:5, :])
            g_ref[r, :] = gthree.astype(BF)
            acc_ref[r, :] = gthree
        out_back.start()
        agrad = g_ref[...] * 4.0
        adapt = aact_ref.shape[1]
        apg = (dot_nt(agrad, up_here[...]) * aslope_ref[...].astype(F32)).astype(BF)
        adapt_here[:, :adapt] = dot_tn(low_ref[...], apg).astype(BF)
        adapt_here[:, adapt : 2 * adapt] = dot_tn(agrad, aact_ref[...]).astype(BF)
        ones = jnp.ones((rows_all, PAIR), BF)
        down_sum = dot_tn(apg, ones).astype(BF)
        high = width // adapt
        row = lax.broadcasted_iota(jnp.int32, (width, adapt), 0)
        col = lax.broadcasted_iota(jnp.int32, (width, adapt), 1)
        block = BIAS_ROWS * high
        entry = lax.div(row, block) * BIAS_ROWS + lax.rem(row, block)
        chosen = (entry == col) & (lax.rem(row, block) < BIAS_ROWS)
        placed = dot_nn(jnp.where(chosen, 1.0, 0.0).astype(BF), down_sum)
        lane = lax.broadcasted_iota(jnp.int32, (width, PAIR), 1)
        sums = jnp.where(lane == 2 * PREFIX_PAD, dot_tn(agrad, ones), placed)
        sums = jnp.where((lane >= 2 * PREFIX_PAD) & (lane < 2 * PREFIX_PAD + 2), sums, 0.0)
        adapt_here[:, 2 * adapt :] = sums.astype(BF)
        adapt_back.start()
        acc_ref[...] += dot_nt(apg, down_here[...])

    @pl.when(phase == 1)
    def _():
        grad = (dot_nt(g_ref[...], wff) * slope_ref[j].astype(F32)).astype(BF)
        acc_ref[...] += dot_nt(grad, win_ref[...])

    @pl.when((phase == 1) & (j == last))
    def _():
        gtwo_ref[...] = norm_back(acc_ref[...], nrm2_ref[...], inv2_ref[...], norm_ref[2:3, :])
        out_back.wait()
        adapt_back.wait()


def cross_backward_kernel(
    len_ref, gtwo_ref, wco_ref, cq_ref, mk_ref, mv_ref, wk_ref, wv_ref, late_ref, nrm1_ref,
    inv1_ref, norm_ref,
    dmem_ref, gone_ref, gone_low_ref,
    low_ref, acc_ref, dk_ref, dv_ref, dq_ref, wcq_here, nrm1_here, sems,
):
    step = pl.program_id(0)
    seqs = len_ref.shape[0]
    tgt = cq_ref.shape[0] // seqs
    src = mk_ref.shape[0] // seqs
    width = gtwo_ref.shape[1]
    copies = [
        pltpu.make_async_copy(late_ref.at[:, pl.ds(CQ_AT, width)], wcq_here, sems.at[0]),
        pltpu.make_async_copy(nrm1_ref, nrm1_here, sems.at[1]),
    ]

    @pl.when(step == 0)
    def _():
        for copy in copies:
            copy.start()
        low_ref[...] = gtwo_ref[...].astype(BF)
        acc_ref[...] = jnp.zeros_like(acc_ref)

    mg_all = dot_nt(low_ref[...], wco_ref[...]).astype(BF)
    heads = GROUP // HEAD_DIM
    slot = lax.broadcasted_iota(jnp.int32, (src, tgt), 0)
    for s in range(seqs):
        bias = jnp.where(slot < len_ref[s], 0.0, NEGATIVE)
        here = pl.ds(s * tgt, tgt)
        there = pl.ds(s * src, src)
        q = cq_ref[here, :] * SCALE
        mg = mg_all[s * tgt : (s + 1) * tgt]
        k = mk_ref[there, :]
        scores = cut(dot_nt(stacked(per_head(k)), q), heads, 0)
        dprobs = cut(dot_nt(stacked(per_head(mv_ref[there, :])), mg), heads, 0)
        probs, grads = [], []
        for x, d in zip(scores, dprobs):
            x = x + bias
            x = jnp.exp(x - jnp.max(x, axis=0, keepdims=True))
            x = x * (1.0 / jnp.sum(x, axis=0, keepdims=True))
            grads.append((x * (d - jnp.sum(x * d, axis=0, keepdims=True))).astype(BF))
            probs.append(x.astype(BF))
        dq = dot_tn(stacked(grads), stacked(per_head(k)))
        lanes = pl.ds(pl.multiple_of(step * GROUP, GROUP), GROUP)
        dq_ref[here, lanes] = (dq * SCALE).astype(BF)
        dk_ref[there, :] = dot_nn(beside(grads), stacked(per_head(q))).astype(BF)
        dv_ref[there, :] = dot_nn(beside(probs), stacked(per_head(mg))).astype(BF)
    acc_ref[...] += dot_nt(
        beside([dk_ref[...], dv_ref[...]]), beside([wk_ref[...], wv_ref[...]])
    )

    @pl.when(step == pl.num_programs(0) - 1)
    def _():
        parts, _, high, width = dmem_ref.shape
        for s in range(seqs):
            block = acc_ref[s * src : (s + 1) * src, :]
            dmem_ref[:, s] = block.reshape(parts, high, width).astype(BF)
        for copy in copies:
            copy.wait()
        grad_first = gtwo_ref[...] + dot_nt(dq_ref[...], wcq_here[...])
        grad_one = norm_back(grad_first, nrm1_here[...], inv1_ref[...], norm_ref[0:1, :])
        gone_ref[...] = grad_one
        gone_low_ref[...] = grad_one.astype(BF)


def self_backward_kernel(
    len_ref, low_ref, wo_ref, q_ref, k_ref, v_ref, pk_ref, pv_ref,
    dq_ref, dk_ref, dv_ref, small_ref,
):
    seqs = len_ref.shape[0]
    tgt = low_ref.shape[0] // seqs
    ag_all = dot_nt(low_ref[...], wo_ref[...]).astype(BF)
    heads = GROUP // HEAD_DIM
    row = lax.broadcasted_iota(jnp.int32, (tgt, tgt), 1)
    col = lax.broadcasted_iota(jnp.int32, (tgt, tgt), 0)
    prefix_bias = jnp.where(
        lax.broadcasted_iota(jnp.int32, (PREFIX_PAD, tgt), 0) < PREFIX, 0.0, NEGATIVE
    )
    pk = per_head(pk_ref[...])
    pv = per_head(pv_ref[...])
    dpk = jnp.zeros((PREFIX_PAD, GROUP), F32)
    dpv = jnp.zeros((PREFIX_PAD, GROUP), F32)
    split = heads * PREFIX_PAD
    for s in range(seqs):
        bias = jnp.where((col <= row) & (col < len_ref[s]), 0.0, NEGATIVE)
        here = pl.ds(s * tgt, tgt)
        q = q_ref[here, :] * SCALE
        ag = ag_all[s * tgt : (s + 1) * tgt]
        keys = stacked(pk + per_head(k_ref[here, :]))
        scores = dot_nt(keys, q)
        dprobs = dot_nt(stacked(pv + per_head(v_ref[here, :])), ag)
        probs, grads = [], []
        for x, d, y, e in zip(
            cut(scores[split:], heads, 0),
            cut(dprobs[split:], heads, 0),
            cut(scores[:split], heads, 0),
            cut(dprobs[:split], heads, 0),
        ):
            x = x + bias
            y = y + prefix_bias
            top = jnp.maximum(jnp.max(x, axis=0, keepdims=True), jnp.max(y, axis=0, keepdims=True))
            x = jnp.exp(x - top)
            y = jnp.exp(y - top)
            inv = 1.0 / (jnp.sum(x, axis=0, keepdims=True) + jnp.sum(y, axis=0, keepdims=True))
            x = x * inv
            y = y * inv
            delta = jnp.sum(x * d, axis=0, keepdims=True) + jnp.sum(y * e, axis=0, keepdims=True)
            grads.append([(y * (e - delta)).astype(BF), (x * (d - delta)).astype(BF)])
            probs.append(stacked([y.astype(BF), x.astype(BF)]))
        dq = dot_tn(stacked([g[0] for g in grads] + [g[1] for g in grads]), keys)
        dk = dot_nn(beside([stacked(g) for g in grads]), stacked(per_head(q)))
        dv = dot_nn(beside(probs), stacked(per_head(ag)))
        dq_ref[here, :] = (dq * SCALE).astype(BF)
        dk_ref[here, :] = dk[PREFIX_PAD:].astype(BF)
        dv_ref[here, :] = dv[PREFIX_PAD:].astype(BF)
        dpk = dpk + dk[:PREFIX_PAD]
        dpv = dpv + dv[:PREFIX_PAD]
    for p in range(GROUP // PAIR):
        at = slice(p * PAIR, (p + 1) * PAIR)
        both = stacked(
            [dpk[:, at], dpv[:, at], jnp.zeros((PAIR - 2 * PREFIX_PAD, PAIR), F32)]
        )
        small_ref[at, :] = both.T


def input_grad_kernel(
    gone_ref, dq_ref, dk_ref, dv_ref, wq_ref, wk_ref, wv_ref, arrived_ref, din_ref, given_ref, sem
):
    handed_on = pltpu.make_async_copy(arrived_ref, given_ref, sem.at[0])

    @pl.when(pl.program_id(0) == 0)
    def _():
        handed_on.start()

    din_ref[...] = (
        gone_ref[...]
        + dot_nt(
            beside([dq_ref[...], dk_ref[...], dv_ref[...]]),
            beside([wq_ref[...], wk_ref[...], wv_ref[...]]),
        )
    ).astype(BF)

    @pl.when(pl.program_id(0) == pl.num_programs(0) - 1)
    def _():
        handed_on.wait()


ANYWHERE = pl.BlockSpec(memory_space=pl.ANY)


def square(width, at):
    return pl.BlockSpec((width, width), lambda *_: (0, at // width))


def whole(shape):
    return pl.BlockSpec(shape, lambda *_: (0,) * len(shape))


def columns(rows, width, offset=0):
    return pl.BlockSpec((rows, width), lambda i, *_: (0, i + offset))


def rows_of(height, width, at):
    return pl.BlockSpec((height, width), lambda i, *_: (i, at // width))


def shaped(shape, dtype):
    return jax.ShapeDtypeStruct(shape, dtype)


def call(kernel, grid, in_specs, out_specs, outs, scratch, flops, moved, *args):
    return pl.pallas_call(
        kernel,
        grid_spec=pltpu.PrefetchScalarGridSpec(
            num_scalar_prefetch=1,
            grid=grid,
            in_specs=in_specs,
            out_specs=out_specs,
            scratch_shapes=scratch,
        ),
        out_shape=outs,
        compiler_params=pltpu.CompilerParams(
            vmem_limit_bytes=VMEM_BYTES,
            dimension_semantics=("arbitrary",) * len(grid),
        ),
        cost_estimate=pl.CostEstimate(flops=flops, bytes_accessed=moved, transcendentals=0),
    )(*args)


def self_forward(lens, tok, early, pk, pv):
    rows, width = tok.shape
    steps = width // GROUP
    return call(
        self_forward_kernel,
        (steps,),
        [
            whole((rows, width)),
            columns(width, GROUP),
            columns(width, GROUP, steps),
            columns(width, GROUP, 2 * steps),
            columns(PREFIX_PAD, GROUP),
            columns(PREFIX_PAD, GROUP),
        ],
        [columns(rows, GROUP)] * 4,
        [shaped((rows, width), BF)] * 4,
        [],
        2 * rows * width * width * 3,
        14 * width * width,
        lens, tok, early, early, early, pk, pv,
    )


def cross_forward(lens, mem, late, tok, att, norms):
    rows, width = tok.shape
    steps = width // GROUP
    places = mem.shape[0]
    return call(
        cross_forward_kernel,
        (steps,),
        [
            whole((places, width)),
            columns(width, GROUP, KV_AT // GROUP),
            columns(width, GROUP, KV_AT // GROUP + steps),
            whole((rows, width)),
            whole((rows, width)),
            square(width, SOUT_AT),
            square(width, CQ_AT),
            whole(norms.shape),
        ],
        [columns(places, GROUP)] * 2
        + [whole((rows, width)), whole((rows, width)), whole((rows, 1)), columns(rows, GROUP)],
        [shaped((places, width), BF)] * 2
        + [shaped((rows, width), BF), shaped((rows, width), F32), shaped((rows, 1), F32)]
        + [shaped((rows, width), BF)],
        [],
        2 * width * width * (2 * rows + 2 * places),
        16 * width * width,
        lens, mem, late, late, tok, att, late, late, norms,
    )


def ffn(lens, nrm1, att, cot, late, down, db, up, ub, norms):
    rows, width = nrm1.shape
    hidden = SPREAD * width
    adapt = down.shape[1]
    block = FFN_BLOCK
    steps = hidden // block
    return call(
        ffn_kernel,
        (2, steps),
        [
            whole((rows, width)),
            whole((rows, width)),
            square(width, OUT_AT),
            ANYWHERE,
            pl.BlockSpec((width, block), lambda p, j, *_: (0, j + IN_AT // block)),
            pl.BlockSpec((block // SPREAD, SPREAD * width), lambda p, j, *_: (j, FF_AT)),
            ANYWHERE,
            whole((1, adapt)),
            ANYWHERE,
            whole((1, width)),
            whole(norms.shape),
        ],
        [ANYWHERE, whole((rows, width)), ANYWHERE],
        [
            shaped((rows, width), BF),
            shaped((rows, width), F32),
            shaped((width, 2 * adapt + PAIR), BF),
        ],
        [
            pltpu.VMEM((rows, width), F32),
            pltpu.VMEM((rows, 1), F32),
            pltpu.VMEM((rows, width), F32),
            pltpu.VMEM((rows, width), BF),
            pltpu.VMEM((steps, rows, block), BF),
            pltpu.VMEM((rows, adapt), BF),
            pltpu.VMEM((rows, adapt), BF),
            pltpu.VMEM((rows, width), BF),
            pltpu.VMEM((rows, width), BF),
            pltpu.VMEM((width, adapt), BF),
            pltpu.VMEM((adapt, width), BF),
            pltpu.VMEM((rows, width), BF),
            pltpu.VMEM((width, 2 * adapt + PAIR), BF),
            pltpu.SemaphoreType.DMA((5,)),
        ],
        2 * rows * width * (4 * hidden + 6 * adapt),
        8 * width * hidden,
        lens, nrm1, att, late, cot, late, late, down, db, up, ub, norms,
    )


def cross_backward(lens, gtwo, late, cq, mk, mv, nrm1, inv1, norms, parts):
    rows, width = cq.shape
    steps = width // GROUP
    places = mk.shape[0]
    seqs = lens.shape[0]
    sent = (parts, seqs, places // seqs // parts, width)
    return call(
        cross_backward_kernel,
        (steps,),
        [
            whole((rows, width)),
            rows_of(GROUP, width, OUT_AT),
            columns(rows, GROUP),
            columns(places, GROUP),
            columns(places, GROUP),
            columns(width, GROUP, KV_AT // GROUP),
            columns(width, GROUP, KV_AT // GROUP + steps),
            ANYWHERE,
            ANYWHERE,
            whole((rows, 1)),
            whole(norms.shape),
        ],
        [whole(sent), whole((rows, width)), whole((rows, width))],
        [shaped(sent, BF), shaped((rows, width), F32), shaped((rows, width), BF)],
        [
            pltpu.VMEM((rows, width), BF),
            pltpu.VMEM((places, width), F32),
            pltpu.VMEM((places, GROUP), BF),
            pltpu.VMEM((places, GROUP), BF),
            pltpu.VMEM((rows, width), BF),
            pltpu.VMEM((width, width), BF),
            pltpu.VMEM((rows, width), F32),
            pltpu.SemaphoreType.DMA((2,)),
        ],
        2 * width * width * (rows + 2 * places),
        14 * width * width,
        lens, gtwo, late, cq, mk, mv, late, late, late, nrm1, inv1, norms,
    )


def self_backward(lens, gone_low, late, q, k, v, pk, pv):
    rows, width = q.shape
    steps = width // GROUP
    return call(
        self_backward_kernel,
        (steps,),
        [whole((rows, width)), rows_of(GROUP, width, SOUT_AT)]
        + [columns(rows, GROUP)] * 3
        + [columns(PREFIX_PAD, GROUP)] * 2,
        [columns(rows, GROUP)] * 3 + [pl.BlockSpec((GROUP, PAIR), lambda i, *_: (i, 0))],
        [shaped((rows, width), BF)] * 3 + [shaped((width, PAIR), F32)],
        [],
        2 * rows * width * width * 4,
        20 * width * width,
        lens, gone_low, late, q, k, v, pk, pv,
    )


def input_gradient(gone, dq, dk, dv, early, arrived):
    rows, width = gone.shape

    def part(index):
        return pl.BlockSpec((GROUP, width), lambda i: (i, index))

    return pl.pallas_call(
        input_grad_kernel,
        grid=(width // GROUP,),
        in_specs=[pl.BlockSpec((rows, GROUP), lambda i: (0, i))]
        + [whole((rows, width))] * 3
        + [part(0), part(1), part(2), ANYWHERE],
        out_specs=[pl.BlockSpec((rows, GROUP), lambda i: (0, i)), ANYWHERE],
        out_shape=[shaped((rows, width), BF), shaped(arrived.shape, arrived.dtype)],
        scratch_shapes=[pltpu.SemaphoreType.DMA((1,))],
        compiler_params=pltpu.CompilerParams(
            vmem_limit_bytes=VMEM_BYTES, dimension_semantics=("arbitrary",)
        ),
        cost_estimate=pl.CostEstimate(
            flops=6 * rows * width * width, bytes_accessed=12 * width * width, transcendentals=0
        ),
    )(gone, dq, dk, dv, early, early, early, arrived)


def around(count, by):
    return [(i, (i + by) % count) for i in range(count)]


def ring_gather(shard, other):
    rows = shard.shape[0]
    half = rows // 2
    count = lax.axis_size("dp_0")
    x, core = lax.axis_index("dp_0"), lax.axis_index("dp_1")
    below = lax.ppermute(shard, "dp_0", around(count, 1))
    above = lax.ppermute(shard, "dp_0", around(count, -1))
    filled = jnp.zeros((count * 2 * rows, shard.shape[1]), shard.dtype)
    filled, other = lax.optimization_barrier((filled, other))
    far_low = lax.ppermute(below[:half], "dp_0", around(count, 1))
    far_high = lax.ppermute(above[half:], "dp_0", around(count, -1))
    for piece, offset, start in (
        (shard, 0, 0), (below, -1, 0), (above, 1, 0), (far_low, 2, 0), (far_high, 2, half),
    ):
        swapped = lax.ppermute(piece, "dp_1", around(2, 1))
        chip = (x + offset + count) % count
        for part, place in ((piece, core), (swapped, 1 - core)):
            at = (chip * 2 + place) * rows + start
            filled = lax.dynamic_update_slice_in_dim(filled, part, at, 0)
    return filled, other


def scatter_sum(blocks):
    count = lax.axis_size("dp_0")
    x, core = lax.axis_index("dp_0"), lax.axis_index("dp_1")
    by_core = blocks.reshape(count, 2, *blocks.shape[1:])
    kept = lax.dynamic_index_in_dim(by_core, core, 1, keepdims=False)
    given = lax.dynamic_index_in_dim(by_core, 1 - core, 1, keepdims=False)
    paired = kept + lax.ppermute(given, "dp_1", around(2, 1))
    total = lax.dynamic_index_in_dim(paired, x, 0, keepdims=False)
    for by in range(1, count):
        sent = lax.dynamic_index_in_dim(paired, (x + by) % count, 0, keepdims=False)
        total = total + lax.ppermute(sent, "dp_0", around(count, by))
    return total


def local(
    tokens, memory, cotangent, tgt_len, src_len,
    self_qkv, self_out, cross_q, cross_kv, cross_out, ffn_in, ffn_out,
    first_gain, first_bias, second_gain, second_bias, third_gain, third_bias,
    prefix_key, prefix_value, down_weight, down_bias, up_weight, up_bias,
):
    mem_groups = lax.axis_size(MEM)
    mem_place = lax.axis_index(MEM)
    seqs, tgt, width = tokens.shape
    src_block = memory.shape[1]
    prefix = prefix_key.shape[0]

    high = cross_out.shape[0] // mem_groups
    mine = functools.partial(
        lax.dynamic_slice_in_dim, start_index=mem_place * high, slice_size=high
    )
    spread = mine(ffn_out.reshape(SPREAD, -1, width), axis=1)
    late = lax.all_gather(
        jnp.concatenate(
            [jnp.moveaxis(spread, 0, 1).reshape(high, SPREAD * width)]
            + [mine(w, axis=0) for w in (ffn_in, cross_out, self_out, cross_q, cross_kv)],
            axis=1,
        ),
        DP_MEM, axis=0, tiled=True,
    )
    early, memory = ring_gather(self_qkv, memory)
    mem_rows = lax.all_to_all(memory, MEM, split_axis=0, concat_axis=1, tiled=True)
    mem_rows = mem_rows.reshape(-1, width)
    own_src = lax.dynamic_slice_in_dim(src_len, mem_place * seqs, seqs, 0)

    tok = tokens.reshape(seqs * tgt, width)
    cot = cotangent.reshape(seqs * tgt, width)
    pk = jnp.pad(prefix_key, ((0, PREFIX_PAD - prefix), (0, 0)))
    pv = jnp.pad(prefix_value, ((0, PREFIX_PAD - prefix), (0, 0)))

    q, k, v, att = self_forward(tgt_len, tok, early, pk, pv)
    vectors = jnp.stack(
        [first_gain, first_bias, second_gain, second_bias, third_gain, third_bias]
        + [third_bias] * 2
    )
    vectors, att = lax.optimization_barrier((vectors, att))
    norms = lax.all_gather(vectors, DP, axis=1, tiled=True).astype(F32)
    mk, mv, cq, nrm1, inv1, cross = cross_forward(own_src, mem_rows, late, tok, att, norms)
    output, gtwo, adapter = ffn(
        tgt_len, nrm1, cross, cot, late,
        down_weight, down_bias.astype(F32)[None], up_weight, up_bias.astype(F32)[None], norms,
    )
    adapter = lax.psum_scatter(adapter, DP, scatter_dimension=0, tiled=True)

    dmem, gone, gone_low = cross_backward(
        own_src, gtwo, late, cq, mk, mv, nrm1, inv1, norms, mem_groups
    )
    memory_grad = lax.all_to_all(
        dmem.reshape(memory.shape), MEM, split_axis=0, concat_axis=0, tiled=True
    )
    dq, dk, dv, small = self_backward(tgt_len, gone_low, late, q, k, v, pk, pv)
    small = scatter_sum(small.reshape(lax.axis_size(DP), -1, PAIR))
    dq, small, memory_grad = lax.optimization_barrier((dq, small, memory_grad))
    din, memory_grad = input_gradient(gone, dq, dk, dv, early, memory_grad)
    adapt = down_weight.shape[1]
    joined = (adapter.astype(F32) + jnp.pad(small, ((0, 0), (2 * adapt, 0)))).astype(BF)
    arrived = lax.all_to_all(
        joined.reshape(mem_groups, -1, joined.shape[1]),
        MEM, split_axis=0, concat_axis=0, tiled=True,
    )
    down_grad, up_grad, last = (
        jnp.sum(arrived[..., a:b].astype(F32), axis=0)
        for a, b in ((0, adapt), (adapt, 2 * adapt), (2 * adapt, joined.shape[1]))
    )
    return (
        output.reshape(tokens.shape),
        din.reshape(tokens.shape),
        memory_grad,
        last[:, :prefix].T,
        last[:, PREFIX_PAD : PREFIX_PAD + prefix].T,
        down_grad,
        last[:BIAS_ROWS, 2 * PREFIX_PAD + 1],
        up_grad.T,
        last[:, 2 * PREFIX_PAD],
    )


def solution(mesh):
    torus = Mesh(mesh.devices.reshape(4, 2, 4, 4), ("dp_0", "dp_1", "mem_0", "mem_1"))
    by_dp = P(DP, None)
    copied = P(None)
    return jax.shard_map(
        local,
        mesh=torus,
        in_specs=(
            P(DP_MEM, None, None), P(DP, MEM, None), P(DP_MEM, None, None), P(DP_MEM), P(DP),
            by_dp, by_dp, by_dp, by_dp, by_dp, by_dp, by_dp,
            P(DP), P(DP), P(DP), P(DP), P(DP), P(DP),
            copied, copied, copied, copied, copied, copied,
        ),
        out_specs=(
            P(DP_MEM, None, None),
            P(DP_MEM, None, None),
            P(DP, MEM, None),
            P(None, DP_MEM),
            P(None, DP_MEM),
            P(DP_MEM, None),
            P(DP_MEM),
            P(None, DP_MEM),
            P(DP_MEM),
        ),
        check_vma=False,
    )
```

```python
import functools

import jax
import jax.numpy as jnp
from jax import lax
from jax.experimental import pallas as pl
from jax.experimental.pallas import tpu as pltpu
from jax.sharding import Mesh
from jax.sharding import PartitionSpec as P

HEAD_DIM = 64
PAIR = 128
GROUP = 256
PREFIX = 30
PREFIX_PAD = 32
BIAS_ROWS = 4
MEM = ("mem_0", "mem_1")
DP = ("dp_0", "dp_1")
DP_MEM = ("dp_0", "dp_1", "mem_0", "mem_1")

NEGATIVE = -1e30
EPSILON = 1e-05
SCALE = HEAD_DIM ** (-0.5)
BF = jnp.bfloat16
F32 = jnp.float32
SPREAD = 4
STRIP = 128
FFN_BLOCK = 1024
FF_AT = 0
IN_AT = 4096
OUT_AT = 8192
SOUT_AT = 9216
CQ_AT = 10240
KV_AT = 11264
VMEM_BYTES = 60 * 1024 * 1024


def dot_nn(left, right):
    return lax.dot_general(left, right, (((1,), (0,)), ((), ())), preferred_element_type=F32)


def dot_nt(left, right):
    return lax.dot_general(left, right, (((1,), (1,)), ((), ())), preferred_element_type=F32)


def dot_tn(left, right):
    return lax.dot_general(left, right, (((0,), (0,)), ((), ())), preferred_element_type=F32)


def per_head(x):
    lane = lax.broadcasted_iota(jnp.int32, (1, GROUP), 1)
    return [
        x * jnp.where(lane // HEAD_DIM == h, 1.0, 0.0).astype(BF)
        for h in range(GROUP // HEAD_DIM)
    ]


def stacked(parts):
    return jnp.concatenate(parts, axis=0)


def beside(parts):
    return jnp.concatenate(parts, axis=1)


def cut(x, count, axis):
    size = x.shape[axis] // count
    return [lax.slice_in_dim(x, i * size, (i + 1) * size, axis=axis) for i in range(count)]


def norm_stats(hidden):
    centred = hidden - jnp.mean(hidden, axis=-1, keepdims=True)
    inverse = lax.rsqrt(jnp.mean(centred * centred, axis=-1, keepdims=True) + EPSILON)
    return centred * inverse, inverse


def norm_back(grad_in, normed, inverse, gain):
    scaled = grad_in * gain
    return inverse * (
        scaled
        - jnp.mean(scaled, axis=-1, keepdims=True)
        - normed * jnp.mean(scaled * normed, axis=-1, keepdims=True)
    )


def gelu_both(pre):
    cdf = 0.5 * (1.0 + lax.erf(pre * (0.5**0.5)))
    density = jnp.exp(-0.5 * pre * pre) * 0.3989422804014327
    return pre * cdf, cdf + pre * density


def self_forward_kernel(
    len_ref, tok_ref, wq_ref, wk_ref, wv_ref, pk_ref, pv_ref,
    q_ref, k_ref, v_ref, att_ref,
):
    seqs = len_ref.shape[0]
    rows_all = tok_ref.shape[0]
    tgt = rows_all // seqs
    projected = dot_nn(tok_ref[...], beside([wq_ref[...], wk_ref[...], wv_ref[...]])).astype(BF)
    q_ref[...] = projected[:, :GROUP]
    k_ref[...] = projected[:, GROUP : 2 * GROUP]
    v_ref[...] = projected[:, 2 * GROUP :]
    heads = GROUP // HEAD_DIM
    row = lax.broadcasted_iota(jnp.int32, (tgt, tgt), 0)
    col = lax.broadcasted_iota(jnp.int32, (tgt, tgt), 1)
    prefix_bias = jnp.where(
        lax.broadcasted_iota(jnp.int32, (1, PREFIX_PAD), 1) < PREFIX, 0.0, NEGATIVE
    )
    pk = per_head(pk_ref[...])
    pv = per_head(pv_ref[...])
    ones = stacked(
        per_head(jnp.ones((PREFIX_PAD, GROUP), BF)) + per_head(jnp.ones((tgt, GROUP), BF))
    )
    scores = []
    for s in range(seqs):
        here = pl.ds(s * tgt, tgt)
        scores.append(dot_nt(q_ref[here, :] * SCALE, stacked(pk + per_head(k_ref[here, :]))))
    for s in range(seqs):
        here = pl.ds(s * tgt, tgt)
        bias = jnp.where((col <= row) & (col < len_ref[s]), 0.0, NEGATIVE)
        pre = cut(scores[s][:, : heads * PREFIX_PAD], heads, 1)
        own = cut(scores[s][:, heads * PREFIX_PAD :], heads, 1)
        own_probs, pre_probs = [], []
        for x, y in zip(own, pre):
            x = x + bias
            y = y + prefix_bias
            top = jnp.maximum(jnp.max(x, axis=1, keepdims=True), jnp.max(y, axis=1, keepdims=True))
            own_probs.append(jnp.exp(x - top).astype(BF))
            pre_probs.append(jnp.exp(y - top).astype(BF))
        probs = beside(pre_probs + own_probs)
        total = dot_nn(probs, stacked(pv + per_head(v_ref[here, :])))
        att_ref[here, :] = (total / dot_nn(probs, ones)).astype(BF)


def cross_forward_kernel(
    len_ref, mem_ref, wk_ref, wv_ref, tok_ref, self_ref, wo_ref, wcq_ref, norm_ref,
    mk_ref, mv_ref, cq_ref, nrm1_ref, inv1_ref, att_ref,
):
    step = pl.program_id(0)
    seqs = len_ref.shape[0]
    tgt = tok_ref.shape[0] // seqs
    src = mem_ref.shape[0] // seqs

    @pl.when(step == 0)
    def _():
        for s in range(seqs):
            r = pl.ds(s * tgt, tgt)
            nrm, inv = norm_stats(
                tok_ref[r, :].astype(F32) + dot_nn(self_ref[r, :], wo_ref[...])
            )
            nrm1_ref[r, :] = nrm
            inv1_ref[r, :] = inv
            first = nrm * norm_ref[0:1, :] + norm_ref[1:2, :]
            cq_ref[r, :] = dot_nn(first.astype(BF), wcq_ref[...]).astype(BF)

    mem = mem_ref[...]
    projected = dot_nn(mem, beside([wk_ref[...], wv_ref[...]])).astype(BF)
    mk_ref[...] = projected[:, :GROUP]
    mv_ref[...] = projected[:, GROUP:]
    heads = GROUP // HEAD_DIM
    lanes = pl.ds(pl.multiple_of(step * GROUP, GROUP), GROUP)
    slot = lax.broadcasted_iota(jnp.int32, (1, src), 1)
    ones = stacked(per_head(jnp.ones((src, GROUP), BF)))
    scores = []
    for s in range(seqs):
        q = cq_ref[s * tgt : (s + 1) * tgt, lanes] * SCALE
        scores.append(dot_nt(q, stacked(per_head(mk_ref[s * src : (s + 1) * src, :]))))
    for s in range(seqs):
        bias = jnp.where(slot < len_ref[s], 0.0, NEGATIVE)
        probs = []
        for x in cut(scores[s], heads, 1):
            x = x + bias
            probs.append(jnp.exp(x - jnp.max(x, axis=1, keepdims=True)).astype(BF))
        probs = beside(probs)
        total = dot_nn(probs, stacked(per_head(mv_ref[s * src : (s + 1) * src, :])))
        att_ref[s * tgt : (s + 1) * tgt, :] = (total / dot_nn(probs, ones)).astype(BF)


def ffn_kernel(
    len_ref, nrm1_ref, att_ref, wco_ref, cot_ref, win_ref, wff_ref, down_ref, db_ref, up_ref, ub_ref,
    norm_ref,
    out_ref, gtwo_ref, adapt_ref,
    nrm2_ref, inv2_ref, acc_ref, low_ref, slope_ref, aact_ref, aslope_ref, g_ref,
    cot_here, down_here, up_here, out_here, adapt_here, sems,
):
    phase = pl.program_id(0)
    j = pl.program_id(1)
    last = pl.num_programs(1) - 1
    seqs = len_ref.shape[0]
    rows_all = nrm1_ref.shape[0]
    tgt = rows_all // seqs
    half = rows_all // 2
    width = nrm1_ref.shape[1]
    strip = wff_ref.shape[0] // (win_ref.shape[1] // (SPREAD * STRIP))
    wff = stacked(
        [
            wff_ref[c : c + strip, b * width : (b + 1) * width]
            for c in range(0, wff_ref.shape[0], strip)
            for b in range(SPREAD)
        ]
    )

    cot_in = pltpu.make_async_copy(cot_ref, cot_here, sems.at[0])
    down_in = pltpu.make_async_copy(down_ref, down_here, sems.at[1])
    up_in = pltpu.make_async_copy(up_ref, up_here, sems.at[2])
    out_back = pltpu.make_async_copy(out_here, out_ref, sems.at[3])
    adapt_back = pltpu.make_async_copy(adapt_here, adapt_ref, sems.at[4])

    @pl.when((phase == 0) & (j == 0))
    def _():
        down_in.start()
        up_in.start()
        cot_in.start()
        for b in range(2):
            r = pl.ds(b * half, half)
            first = nrm1_ref[r, :] * norm_ref[0:1, :] + norm_ref[1:2, :]
            nrm, inv = norm_stats(first + dot_nn(att_ref[r, :], wco_ref[...]))
            nrm2_ref[r, :] = nrm
            inv2_ref[r, :] = inv
            second = nrm * norm_ref[2:3, :] + norm_ref[3:4, :]
            low_ref[r, :] = second.astype(BF)
            acc_ref[r, :] = second

    @pl.when(phase == 0)
    def _():
        act, slope = gelu_both(dot_nn(low_ref[...], win_ref[...]))
        slope_ref[j] = slope.astype(BF)
        acc_ref[...] += dot_nn(act.astype(BF), wff)

    @pl.when((phase == 1) & (j == 0))
    def _():
        down_in.wait()
        up_in.wait()
        cot_in.wait()
        act, slope = gelu_both(dot_nn(low_ref[...], down_here[...]) + db_ref[...])
        aact_ref[...] = act.astype(BF)
        aslope_ref[...] = slope.astype(BF)
        for s in range(seqs):
            r = pl.ds(s * tgt, tgt)
            adapted = dot_nn(aact_ref[r, :], up_here[...]) + ub_ref[...]
            nrm, inv = norm_stats(acc_ref[r, :] + 4.0 * adapted)
            out_here[r, :] = (nrm * norm_ref[4:5, :] + norm_ref[5:6, :]).astype(BF)
            live = lax.broadcasted_iota(jnp.int32, (tgt, 1), 0) < len_ref[s]
            go = jnp.where(live, cot_here[r, :].astype(F32), 0.0)
            gthree = norm_back(go, nrm, inv, norm_ref[4:5, :])
            g_ref[r, :] = gthree.astype(BF)
            acc_ref[r, :] = gthree
        out_back.start()
        agrad = g_ref[...] * 4.0
        adapt = aact_ref.shape[1]
        apg = (dot_nt(agrad, up_here[...]) * aslope_ref[...].astype(F32)).astype(BF)
        adapt_here[:, :adapt] = dot_tn(low_ref[...], apg).astype(BF)
        adapt_here[:, adapt : 2 * adapt] = dot_tn(agrad, aact_ref[...]).astype(BF)
        ones = jnp.ones((rows_all, PAIR), BF)
        down_sum = dot_tn(apg, ones).astype(BF)
        high = width // adapt
        row = lax.broadcasted_iota(jnp.int32, (width, adapt), 0)
        col = lax.broadcasted_iota(jnp.int32, (width, adapt), 1)
        block = BIAS_ROWS * high
        entry = lax.div(row, block) * BIAS_ROWS + lax.rem(row, block)
        chosen = (entry == col) & (lax.rem(row, block) < BIAS_ROWS)
        placed = dot_nn(jnp.where(chosen, 1.0, 0.0).astype(BF), down_sum)
        lane = lax.broadcasted_iota(jnp.int32, (width, PAIR), 1)
        sums = jnp.where(lane == 2 * PREFIX_PAD, dot_tn(agrad, ones), placed)
        sums = jnp.where((lane >= 2 * PREFIX_PAD) & (lane < 2 * PREFIX_PAD + 2), sums, 0.0)
        adapt_here[:, 2 * adapt :] = sums.astype(BF)
        adapt_back.start()
        acc_ref[...] += dot_nt(apg, down_here[...])

    @pl.when(phase == 1)
    def _():
        grad = (dot_nt(g_ref[...], wff) * slope_ref[j].astype(F32)).astype(BF)
        acc_ref[...] += dot_nt(grad, win_ref[...])

    @pl.when((phase == 1) & (j == last))
    def _():
        gtwo_ref[...] = norm_back(acc_ref[...], nrm2_ref[...], inv2_ref[...], norm_ref[2:3, :])
        out_back.wait()
        adapt_back.wait()


def cross_backward_kernel(
    len_ref, gtwo_ref, wco_ref, cq_ref, mk_ref, mv_ref, wk_ref, wv_ref, late_ref, nrm1_ref,
    inv1_ref, norm_ref,
    dmem_ref, gone_ref, gone_low_ref,
    low_ref, acc_ref, dk_ref, dv_ref, dq_ref, wcq_here, nrm1_here, sems,
):
    step = pl.program_id(0)
    seqs = len_ref.shape[0]
    tgt = cq_ref.shape[0] // seqs
    src = mk_ref.shape[0] // seqs
    width = gtwo_ref.shape[1]
    copies = [
        pltpu.make_async_copy(late_ref.at[:, pl.ds(CQ_AT, width)], wcq_here, sems.at[0]),
        pltpu.make_async_copy(nrm1_ref, nrm1_here, sems.at[1]),
    ]

    @pl.when(step == 0)
    def _():
        for copy in copies:
            copy.start()
        low_ref[...] = gtwo_ref[...].astype(BF)
        acc_ref[...] = jnp.zeros_like(acc_ref)

    mg_all = dot_nt(low_ref[...], wco_ref[...]).astype(BF)
    heads = GROUP // HEAD_DIM
    slot = lax.broadcasted_iota(jnp.int32, (src, tgt), 0)
    for s in range(seqs):
        bias = jnp.where(slot < len_ref[s], 0.0, NEGATIVE)
        here = pl.ds(s * tgt, tgt)
        there = pl.ds(s * src, src)
        q = cq_ref[here, :] * SCALE
        mg = mg_all[s * tgt : (s + 1) * tgt]
        k = mk_ref[there, :]
        scores = cut(dot_nt(stacked(per_head(k)), q), heads, 0)
        dprobs = cut(dot_nt(stacked(per_head(mv_ref[there, :])), mg), heads, 0)
        probs, grads = [], []
        for x, d in zip(scores, dprobs):
            x = x + bias
            x = jnp.exp(x - jnp.max(x, axis=0, keepdims=True))
            x = x * (1.0 / jnp.sum(x, axis=0, keepdims=True))
            grads.append((x * (d - jnp.sum(x * d, axis=0, keepdims=True))).astype(BF))
            probs.append(x.astype(BF))
        dq = dot_tn(stacked(grads), stacked(per_head(k)))
        lanes = pl.ds(pl.multiple_of(step * GROUP, GROUP), GROUP)
        dq_ref[here, lanes] = (dq * SCALE).astype(BF)
        dk_ref[there, :] = dot_nn(beside(grads), stacked(per_head(q))).astype(BF)
        dv_ref[there, :] = dot_nn(beside(probs), stacked(per_head(mg))).astype(BF)
    acc_ref[...] += dot_nt(
        beside([dk_ref[...], dv_ref[...]]), beside([wk_ref[...], wv_ref[...]])
    )

    @pl.when(step == pl.num_programs(0) - 1)
    def _():
        parts, _, high, width = dmem_ref.shape
        for s in range(seqs):
            block = acc_ref[s * src : (s + 1) * src, :]
            dmem_ref[:, s] = block.reshape(parts, high, width).astype(BF)
        for copy in copies:
            copy.wait()
        grad_first = gtwo_ref[...] + dot_nt(dq_ref[...], wcq_here[...])
        grad_one = norm_back(grad_first, nrm1_here[...], inv1_ref[...], norm_ref[0:1, :])
        gone_ref[...] = grad_one
        gone_low_ref[...] = grad_one.astype(BF)


def self_backward_kernel(
    len_ref, low_ref, wo_ref, q_ref, k_ref, v_ref, pk_ref, pv_ref,
    dq_ref, dk_ref, dv_ref, small_ref,
):
    seqs = len_ref.shape[0]
    tgt = low_ref.shape[0] // seqs
    ag_all = dot_nt(low_ref[...], wo_ref[...]).astype(BF)
    heads = GROUP // HEAD_DIM
    row = lax.broadcasted_iota(jnp.int32, (tgt, tgt), 1)
    col = lax.broadcasted_iota(jnp.int32, (tgt, tgt), 0)
    prefix_bias = jnp.where(
        lax.broadcasted_iota(jnp.int32, (PREFIX_PAD, tgt), 0) < PREFIX, 0.0, NEGATIVE
    )
    pk = per_head(pk_ref[...])
    pv = per_head(pv_ref[...])
    dpk = jnp.zeros((PREFIX_PAD, GROUP), F32)
    dpv = jnp.zeros((PREFIX_PAD, GROUP), F32)
    split = heads * PREFIX_PAD
    for s in range(seqs):
        bias = jnp.where((col <= row) & (col < len_ref[s]), 0.0, NEGATIVE)
        here = pl.ds(s * tgt, tgt)
        q = q_ref[here, :] * SCALE
        ag = ag_all[s * tgt : (s + 1) * tgt]
        keys = stacked(pk + per_head(k_ref[here, :]))
        scores = dot_nt(keys, q)
        dprobs = dot_nt(stacked(pv + per_head(v_ref[here, :])), ag)
        probs, grads = [], []
        for x, d, y, e in zip(
            cut(scores[split:], heads, 0),
            cut(dprobs[split:], heads, 0),
            cut(scores[:split], heads, 0),
            cut(dprobs[:split], heads, 0),
        ):
            x = x + bias
            y = y + prefix_bias
            top = jnp.maximum(jnp.max(x, axis=0, keepdims=True), jnp.max(y, axis=0, keepdims=True))
            x = jnp.exp(x - top)
            y = jnp.exp(y - top)
            inv = 1.0 / (jnp.sum(x, axis=0, keepdims=True) + jnp.sum(y, axis=0, keepdims=True))
            x = x * inv
            y = y * inv
            delta = jnp.sum(x * d, axis=0, keepdims=True) + jnp.sum(y * e, axis=0, keepdims=True)
            grads.append([(y * (e - delta)).astype(BF), (x * (d - delta)).astype(BF)])
            probs.append(stacked([y.astype(BF), x.astype(BF)]))
        dq = dot_tn(stacked([g[0] for g in grads] + [g[1] for g in grads]), keys)
        dk = dot_nn(beside([stacked(g) for g in grads]), stacked(per_head(q)))
        dv = dot_nn(beside(probs), stacked(per_head(ag)))
        dq_ref[here, :] = (dq * SCALE).astype(BF)
        dk_ref[here, :] = dk[PREFIX_PAD:].astype(BF)
        dv_ref[here, :] = dv[PREFIX_PAD:].astype(BF)
        dpk = dpk + dk[:PREFIX_PAD]
        dpv = dpv + dv[:PREFIX_PAD]
    for p in range(GROUP // PAIR):
        at = slice(p * PAIR, (p + 1) * PAIR)
        both = stacked(
            [dpk[:, at], dpv[:, at], jnp.zeros((PAIR - 2 * PREFIX_PAD, PAIR), F32)]
        )
        small_ref[at, :] = both.T


def input_grad_kernel(gone_ref, dq_ref, dk_ref, dv_ref, wq_ref, wk_ref, wv_ref, din_ref):
    din_ref[...] = (
        gone_ref[...]
        + dot_nt(
            beside([dq_ref[...], dk_ref[...], dv_ref[...]]),
            beside([wq_ref[...], wk_ref[...], wv_ref[...]]),
        )
    ).astype(BF)


ANYWHERE = pl.BlockSpec(memory_space=pl.ANY)


def square(width, at):
    return pl.BlockSpec((width, width), lambda *_: (0, at // width))


def whole(shape):
    return pl.BlockSpec(shape, lambda *_: (0,) * len(shape))


def columns(rows, width, offset=0):
    return pl.BlockSpec((rows, width), lambda i, *_: (0, i + offset))


def rows_of(height, width, at):
    return pl.BlockSpec((height, width), lambda i, *_: (i, at // width))


def shaped(shape, dtype):
    return jax.ShapeDtypeStruct(shape, dtype)


def call(kernel, grid, in_specs, out_specs, outs, scratch, flops, moved, *args):
    return pl.pallas_call(
        kernel,
        grid_spec=pltpu.PrefetchScalarGridSpec(
            num_scalar_prefetch=1,
            grid=grid,
            in_specs=in_specs,
            out_specs=out_specs,
            scratch_shapes=scratch,
        ),
        out_shape=outs,
        compiler_params=pltpu.CompilerParams(
            vmem_limit_bytes=VMEM_BYTES,
            dimension_semantics=("arbitrary",) * len(grid),
        ),
        cost_estimate=pl.CostEstimate(flops=flops, bytes_accessed=moved, transcendentals=0),
    )(*args)


def self_forward(lens, tok, early, pk, pv):
    rows, width = tok.shape
    steps = width // GROUP
    return call(
        self_forward_kernel,
        (steps,),
        [
            whole((rows, width)),
            columns(width, GROUP),
            columns(width, GROUP, steps),
            columns(width, GROUP, 2 * steps),
            columns(PREFIX_PAD, GROUP),
            columns(PREFIX_PAD, GROUP),
        ],
        [columns(rows, GROUP)] * 4,
        [shaped((rows, width), BF)] * 4,
        [],
        2 * rows * width * width * 3,
        14 * width * width,
        lens, tok, early, early, early, pk, pv,
    )


def cross_forward(lens, mem, late, tok, att, norms):
    rows, width = tok.shape
    steps = width // GROUP
    places = mem.shape[0]
    return call(
        cross_forward_kernel,
        (steps,),
        [
            whole((places, width)),
            columns(width, GROUP, KV_AT // GROUP),
            columns(width, GROUP, KV_AT // GROUP + steps),
            whole((rows, width)),
            whole((rows, width)),
            square(width, SOUT_AT),
            square(width, CQ_AT),
            whole(norms.shape),
        ],
        [columns(places, GROUP)] * 2
        + [whole((rows, width)), whole((rows, width)), whole((rows, 1)), columns(rows, GROUP)],
        [shaped((places, width), BF)] * 2
        + [shaped((rows, width), BF), shaped((rows, width), F32), shaped((rows, 1), F32)]
        + [shaped((rows, width), BF)],
        [],
        2 * width * width * (2 * rows + 2 * places),
        16 * width * width,
        lens, mem, late, late, tok, att, late, late, norms,
    )


def ffn(lens, nrm1, att, cot, late, down, db, up, ub, norms):
    rows, width = nrm1.shape
    hidden = SPREAD * width
    adapt = down.shape[1]
    block = FFN_BLOCK
    steps = hidden // block
    return call(
        ffn_kernel,
        (2, steps),
        [
            whole((rows, width)),
            whole((rows, width)),
            square(width, OUT_AT),
            ANYWHERE,
            pl.BlockSpec((width, block), lambda p, j, *_: (0, j + IN_AT // block)),
            pl.BlockSpec((block // SPREAD, SPREAD * width), lambda p, j, *_: (j, FF_AT)),
            ANYWHERE,
            whole((1, adapt)),
            ANYWHERE,
            whole((1, width)),
            whole(norms.shape),
        ],
        [ANYWHERE, whole((rows, width)), ANYWHERE],
        [
            shaped((rows, width), BF),
            shaped((rows, width), F32),
            shaped((width, 2 * adapt + PAIR), BF),
        ],
        [
            pltpu.VMEM((rows, width), F32),
            pltpu.VMEM((rows, 1), F32),
            pltpu.VMEM((rows, width), F32),
            pltpu.VMEM((rows, width), BF),
            pltpu.VMEM((steps, rows, block), BF),
            pltpu.VMEM((rows, adapt), BF),
            pltpu.VMEM((rows, adapt), BF),
            pltpu.VMEM((rows, width), BF),
            pltpu.VMEM((rows, width), BF),
            pltpu.VMEM((width, adapt), BF),
            pltpu.VMEM((adapt, width), BF),
            pltpu.VMEM((rows, width), BF),
            pltpu.VMEM((width, 2 * adapt + PAIR), BF),
            pltpu.SemaphoreType.DMA((5,)),
        ],
        2 * rows * width * (4 * hidden + 6 * adapt),
        8 * width * hidden,
        lens, nrm1, att, late, cot, late, late, down, db, up, ub, norms,
    )


def cross_backward(lens, gtwo, late, cq, mk, mv, nrm1, inv1, norms, parts):
    rows, width = cq.shape
    steps = width // GROUP
    places = mk.shape[0]
    seqs = lens.shape[0]
    sent = (parts, seqs, places // seqs // parts, width)
    return call(
        cross_backward_kernel,
        (steps,),
        [
            whole((rows, width)),
            rows_of(GROUP, width, OUT_AT),
            columns(rows, GROUP),
            columns(places, GROUP),
            columns(places, GROUP),
            columns(width, GROUP, KV_AT // GROUP),
            columns(width, GROUP, KV_AT // GROUP + steps),
            ANYWHERE,
            ANYWHERE,
            whole((rows, 1)),
            whole(norms.shape),
        ],
        [whole(sent), whole((rows, width)), whole((rows, width))],
        [shaped(sent, BF), shaped((rows, width), F32), shaped((rows, width), BF)],
        [
            pltpu.VMEM((rows, width), BF),
            pltpu.VMEM((places, width), F32),
            pltpu.VMEM((places, GROUP), BF),
            pltpu.VMEM((places, GROUP), BF),
            pltpu.VMEM((rows, width), BF),
            pltpu.VMEM((width, width), BF),
            pltpu.VMEM((rows, width), F32),
            pltpu.SemaphoreType.DMA((2,)),
        ],
        2 * width * width * (rows + 2 * places),
        14 * width * width,
        lens, gtwo, late, cq, mk, mv, late, late, late, nrm1, inv1, norms,
    )


def self_backward(lens, gone_low, late, q, k, v, pk, pv):
    rows, width = q.shape
    steps = width // GROUP
    return call(
        self_backward_kernel,
        (steps,),
        [whole((rows, width)), rows_of(GROUP, width, SOUT_AT)]
        + [columns(rows, GROUP)] * 3
        + [columns(PREFIX_PAD, GROUP)] * 2,
        [columns(rows, GROUP)] * 3 + [pl.BlockSpec((GROUP, PAIR), lambda i, *_: (i, 0))],
        [shaped((rows, width), BF)] * 3 + [shaped((width, PAIR), F32)],
        [],
        2 * rows * width * width * 4,
        20 * width * width,
        lens, gone_low, late, q, k, v, pk, pv,
    )


def input_gradient(gone, dq, dk, dv, early):
    rows, width = gone.shape

    def part(index):
        return pl.BlockSpec((GROUP, width), lambda i: (i, index))

    return pl.pallas_call(
        input_grad_kernel,
        grid=(width // GROUP,),
        in_specs=[pl.BlockSpec((rows, GROUP), lambda i: (0, i))]
        + [whole((rows, width))] * 3
        + [part(0), part(1), part(2)],
        out_specs=pl.BlockSpec((rows, GROUP), lambda i: (0, i)),
        out_shape=shaped((rows, width), BF),
        compiler_params=pltpu.CompilerParams(
            vmem_limit_bytes=VMEM_BYTES, dimension_semantics=("arbitrary",)
        ),
        cost_estimate=pl.CostEstimate(
            flops=6 * rows * width * width, bytes_accessed=12 * width * width, transcendentals=0
        ),
    )(gone, dq, dk, dv, early, early, early)


def around(count, by):
    return [(i, (i + by) % count) for i in range(count)]


def ring_gather(shard, other):
    rows = shard.shape[0]
    half = rows // 2
    count = lax.axis_size("dp_0")
    x, core = lax.axis_index("dp_0"), lax.axis_index("dp_1")
    below = lax.ppermute(shard, "dp_0", around(count, 1))
    above = lax.ppermute(shard, "dp_0", around(count, -1))
    filled = jnp.zeros((count * 2 * rows, shard.shape[1]), shard.dtype)
    filled, other = lax.optimization_barrier((filled, other))
    far_low = lax.ppermute(below[:half], "dp_0", around(count, 1))
    far_high = lax.ppermute(above[half:], "dp_0", around(count, -1))
    for piece, offset, start in (
        (shard, 0, 0), (below, -1, 0), (above, 1, 0), (far_low, 2, 0), (far_high, 2, half),
    ):
        swapped = lax.ppermute(piece, "dp_1", around(2, 1))
        chip = (x + offset + count) % count
        for part, place in ((piece, core), (swapped, 1 - core)):
            at = (chip * 2 + place) * rows + start
            filled = lax.dynamic_update_slice_in_dim(filled, part, at, 0)
    return filled, other


def scatter_sum(blocks):
    count = lax.axis_size("dp_0")
    x, core = lax.axis_index("dp_0"), lax.axis_index("dp_1")
    by_core = blocks.reshape(count, 2, *blocks.shape[1:])
    kept = lax.dynamic_index_in_dim(by_core, core, 1, keepdims=False)
    given = lax.dynamic_index_in_dim(by_core, 1 - core, 1, keepdims=False)
    paired = kept + lax.ppermute(given, "dp_1", around(2, 1))
    total = lax.dynamic_index_in_dim(paired, x, 0, keepdims=False)
    for by in range(1, count):
        sent = lax.dynamic_index_in_dim(paired, (x + by) % count, 0, keepdims=False)
        total = total + lax.ppermute(sent, "dp_0", around(count, by))
    return total


def local(
    tokens, memory, cotangent, tgt_len, src_len,
    self_qkv, self_out, cross_q, cross_kv, cross_out, ffn_in, ffn_out,
    first_gain, first_bias, second_gain, second_bias, third_gain, third_bias,
    prefix_key, prefix_value, down_weight, down_bias, up_weight, up_bias,
):
    mem_groups = lax.axis_size(MEM)
    mem_place = lax.axis_index(MEM)
    seqs, tgt, width = tokens.shape
    src_block = memory.shape[1]
    prefix = prefix_key.shape[0]

    high = cross_out.shape[0] // mem_groups
    mine = functools.partial(
        lax.dynamic_slice_in_dim, start_index=mem_place * high, slice_size=high
    )
    spread = mine(ffn_out.reshape(SPREAD, -1, width), axis=1)
    late = lax.all_gather(
        jnp.concatenate(
            [jnp.moveaxis(spread, 0, 1).reshape(high, SPREAD * width)]
            + [mine(w, axis=0) for w in (ffn_in, cross_out, self_out, cross_q, cross_kv)],
            axis=1,
        ),
        DP_MEM, axis=0, tiled=True,
    )
    early, memory = ring_gather(self_qkv, memory)
    mem_rows = lax.all_to_all(memory, MEM, split_axis=0, concat_axis=1, tiled=True)
    mem_rows = mem_rows.reshape(-1, width)
    own_src = lax.dynamic_slice_in_dim(src_len, mem_place * seqs, seqs, 0)

    tok = tokens.reshape(seqs * tgt, width)
    cot = cotangent.reshape(seqs * tgt, width)
    pk = jnp.pad(prefix_key, ((0, PREFIX_PAD - prefix), (0, 0)))
    pv = jnp.pad(prefix_value, ((0, PREFIX_PAD - prefix), (0, 0)))

    q, k, v, att = self_forward(tgt_len, tok, early, pk, pv)
    vectors = jnp.stack(
        [first_gain, first_bias, second_gain, second_bias, third_gain, third_bias]
        + [third_bias] * 2
    )
    vectors, att = lax.optimization_barrier((vectors, att))
    norms = lax.all_gather(vectors, DP, axis=1, tiled=True).astype(F32)
    mk, mv, cq, nrm1, inv1, cross = cross_forward(own_src, mem_rows, late, tok, att, norms)
    output, gtwo, adapter = ffn(
        tgt_len, nrm1, cross, cot, late,
        down_weight, down_bias.astype(F32)[None], up_weight, up_bias.astype(F32)[None], norms,
    )
    adapter = lax.psum_scatter(adapter, DP, scatter_dimension=0, tiled=True)

    dmem, gone, gone_low = cross_backward(
        own_src, gtwo, late, cq, mk, mv, nrm1, inv1, norms, mem_groups
    )
    memory_grad = lax.all_to_all(dmem, MEM, split_axis=0, concat_axis=0, tiled=True)
    dq, dk, dv, small = self_backward(tgt_len, gone_low, late, q, k, v, pk, pv)
    small = scatter_sum(small.reshape(lax.axis_size(DP), -1, PAIR))
    dq, small, memory_grad = lax.optimization_barrier((dq, small, memory_grad))
    din = input_gradient(gone, dq, dk, dv, early)
    adapt = down_weight.shape[1]
    joined = (adapter.astype(F32) + jnp.pad(small, ((0, 0), (2 * adapt, 0)))).astype(BF)
    arrived = lax.all_to_all(
        joined.reshape(mem_groups, -1, joined.shape[1]),
        MEM, split_axis=0, concat_axis=0, tiled=True,
    )
    down_grad, up_grad, last = (
        jnp.sum(arrived[..., a:b].astype(F32), axis=0)
        for a, b in ((0, adapt), (adapt, 2 * adapt), (2 * adapt, joined.shape[1]))
    )
    return (
        output.reshape(tokens.shape),
        din.reshape(tokens.shape),
        memory_grad.reshape(memory.shape),
        last[:, :prefix].T,
        last[:, PREFIX_PAD : PREFIX_PAD + prefix].T,
        down_grad,
        last[:BIAS_ROWS, 2 * PREFIX_PAD + 1],
        up_grad.T,
        last[:, 2 * PREFIX_PAD],
    )


def solution(mesh):
    torus = Mesh(mesh.devices.reshape(4, 2, 4, 4), ("dp_0", "dp_1", "mem_0", "mem_1"))
    by_dp = P(DP, None)
    copied = P(None)
    return jax.shard_map(
        local,
        mesh=torus,
        in_specs=(
            P(DP_MEM, None, None), P(DP, MEM, None), P(DP_MEM, None, None), P(DP_MEM), P(DP),
            by_dp, by_dp, by_dp, by_dp, by_dp, by_dp, by_dp,
            P(DP), P(DP), P(DP), P(DP), P(DP), P(DP),
            copied, copied, copied, copied, copied, copied,
        ),
        out_specs=(
            P(DP_MEM, None, None),
            P(DP_MEM, None, None),
            P(DP, MEM, None),
            P(None, DP_MEM),
            P(None, DP_MEM),
            P(DP_MEM, None),
            P(DP_MEM),
            P(None, DP_MEM),
            P(DP_MEM),
        ),
        check_vma=False,
    )
```

```python
import functools

import jax
import jax.numpy as jnp
from jax import lax
from jax.experimental import pallas as pl
from jax.experimental.pallas import tpu as pltpu
from jax.sharding import Mesh
from jax.sharding import PartitionSpec as P

HEAD_DIM = 64
PAIR = 128
GROUP = 256
PREFIX = 30
PREFIX_PAD = 32
BIAS_ROWS = 4
MEM = ("mem_0", "mem_1")
DP = ("dp_0", "dp_1")
DP_MEM = ("dp_0", "dp_1", "mem_0", "mem_1")

NEGATIVE = -1e30
EPSILON = 1e-05
SCALE = HEAD_DIM ** (-0.5)
BF = jnp.bfloat16
F32 = jnp.float32
SPREAD = 4
STRIP = 128
FFN_BLOCK = 1024
FF_AT = 0
IN_AT = 4096
OUT_AT = 8192
SOUT_AT = 9216
CQ_AT = 10240
KV_AT = 11264
VMEM_BYTES = 60 * 1024 * 1024


def dot_nn(left, right):
    return lax.dot_general(left, right, (((1,), (0,)), ((), ())), preferred_element_type=F32)


def dot_nt(left, right):
    return lax.dot_general(left, right, (((1,), (1,)), ((), ())), preferred_element_type=F32)


def dot_tn(left, right):
    return lax.dot_general(left, right, (((0,), (0,)), ((), ())), preferred_element_type=F32)


def per_head(x):
    lane = lax.broadcasted_iota(jnp.int32, (1, GROUP), 1)
    return [
        x * jnp.where(lane // HEAD_DIM == h, 1.0, 0.0).astype(BF)
        for h in range(GROUP // HEAD_DIM)
    ]


def stacked(parts):
    return jnp.concatenate(parts, axis=0)


def beside(parts):
    return jnp.concatenate(parts, axis=1)


def cut(x, count, axis):
    size = x.shape[axis] // count
    return [lax.slice_in_dim(x, i * size, (i + 1) * size, axis=axis) for i in range(count)]


def norm_stats(hidden):
    centred = hidden - jnp.mean(hidden, axis=-1, keepdims=True)
    inverse = lax.rsqrt(jnp.mean(centred * centred, axis=-1, keepdims=True) + EPSILON)
    return centred * inverse, inverse


def norm_back(grad_in, normed, inverse, gain):
    scaled = grad_in * gain
    return inverse * (
        scaled
        - jnp.mean(scaled, axis=-1, keepdims=True)
        - normed * jnp.mean(scaled * normed, axis=-1, keepdims=True)
    )


def gelu_both(pre):
    cdf = 0.5 * (1.0 + lax.erf(pre * (0.5**0.5)))
    density = jnp.exp(-0.5 * pre * pre) * 0.3989422804014327
    return pre * cdf, cdf + pre * density


def self_forward_kernel(
    len_ref, tok_ref, wq_ref, wk_ref, wv_ref, pk_ref, pv_ref,
    q_ref, k_ref, v_ref, att_ref,
):
    seqs = len_ref.shape[0]
    rows_all = tok_ref.shape[0]
    tgt = rows_all // seqs
    projected = dot_nn(tok_ref[...], beside([wq_ref[...], wk_ref[...], wv_ref[...]])).astype(BF)
    q_ref[...] = projected[:, :GROUP]
    k_ref[...] = projected[:, GROUP : 2 * GROUP]
    v_ref[...] = projected[:, 2 * GROUP :]
    heads = GROUP // HEAD_DIM
    row = lax.broadcasted_iota(jnp.int32, (tgt, tgt), 0)
    col = lax.broadcasted_iota(jnp.int32, (tgt, tgt), 1)
    prefix_bias = jnp.where(
        lax.broadcasted_iota(jnp.int32, (1, PREFIX_PAD), 1) < PREFIX, 0.0, NEGATIVE
    )
    pk = per_head(pk_ref[...])
    pv = per_head(pv_ref[...])
    ones = stacked(
        per_head(jnp.ones((PREFIX_PAD, GROUP), BF)) + per_head(jnp.ones((tgt, GROUP), BF))
    )
    scores = []
    for s in range(seqs):
        here = pl.ds(s * tgt, tgt)
        scores.append(dot_nt(q_ref[here, :] * SCALE, stacked(pk + per_head(k_ref[here, :]))))
    for s in range(seqs):
        here = pl.ds(s * tgt, tgt)
        bias = jnp.where((col <= row) & (col < len_ref[s]), 0.0, NEGATIVE)
        pre = cut(scores[s][:, : heads * PREFIX_PAD], heads, 1)
        own = cut(scores[s][:, heads * PREFIX_PAD :], heads, 1)
        own_probs, pre_probs = [], []
        for x, y in zip(own, pre):
            x = x + bias
            y = y + prefix_bias
            top = jnp.maximum(jnp.max(x, axis=1, keepdims=True), jnp.max(y, axis=1, keepdims=True))
            own_probs.append(jnp.exp(x - top).astype(BF))
            pre_probs.append(jnp.exp(y - top).astype(BF))
        probs = beside(pre_probs + own_probs)
        total = dot_nn(probs, stacked(pv + per_head(v_ref[here, :])))
        att_ref[here, :] = (total / dot_nn(probs, ones)).astype(BF)


def cross_forward_kernel(
    len_ref, mem_ref, wk_ref, wv_ref, tok_ref, self_ref, wo_ref, wcq_ref, norm_ref,
    mk_ref, mv_ref, cq_ref, nrm1_ref, inv1_ref, att_ref,
):
    step = pl.program_id(0)
    seqs = len_ref.shape[0]
    tgt = tok_ref.shape[0] // seqs
    src = mem_ref.shape[0] // seqs

    @pl.when(step == 0)
    def _():
        for s in range(seqs):
            r = pl.ds(s * tgt, tgt)
            nrm, inv = norm_stats(
                tok_ref[r, :].astype(F32) + dot_nn(self_ref[r, :], wo_ref[...])
            )
            nrm1_ref[r, :] = nrm
            inv1_ref[r, :] = inv
            first = nrm * norm_ref[0:1, :] + norm_ref[1:2, :]
            cq_ref[r, :] = dot_nn(first.astype(BF), wcq_ref[...]).astype(BF)

    mem = mem_ref[...]
    projected = dot_nn(mem, beside([wk_ref[...], wv_ref[...]])).astype(BF)
    mk_ref[...] = projected[:, :GROUP]
    mv_ref[...] = projected[:, GROUP:]
    heads = GROUP // HEAD_DIM
    lanes = pl.ds(pl.multiple_of(step * GROUP, GROUP), GROUP)
    slot = lax.broadcasted_iota(jnp.int32, (1, src), 1)
    ones = stacked(per_head(jnp.ones((src, GROUP), BF)))
    scores = []
    for s in range(seqs):
        q = cq_ref[s * tgt : (s + 1) * tgt, lanes] * SCALE
        scores.append(dot_nt(q, stacked(per_head(mk_ref[s * src : (s + 1) * src, :]))))
    for s in range(seqs):
        bias = jnp.where(slot < len_ref[s], 0.0, NEGATIVE)
        probs = []
        for x in cut(scores[s], heads, 1):
            x = x + bias
            probs.append(jnp.exp(x - jnp.max(x, axis=1, keepdims=True)).astype(BF))
        probs = beside(probs)
        total = dot_nn(probs, stacked(per_head(mv_ref[s * src : (s + 1) * src, :])))
        att_ref[s * tgt : (s + 1) * tgt, :] = (total / dot_nn(probs, ones)).astype(BF)


def ffn_kernel(
    len_ref, nrm1_ref, att_ref, wco_ref, cot_ref, win_ref, wff_ref, down_ref, db_ref, up_ref, ub_ref,
    norm_ref,
    out_ref, gtwo_ref, adapt_ref,
    nrm2_ref, inv2_ref, acc_ref, low_ref, slope_ref, aact_ref, aslope_ref, g_ref,
    cot_here, down_here, up_here, out_here, adapt_here, sems,
):
    phase = pl.program_id(0)
    j = pl.program_id(1)
    last = pl.num_programs(1) - 1
    seqs = len_ref.shape[0]
    rows_all = nrm1_ref.shape[0]
    tgt = rows_all // seqs
    half = rows_all // 2
    width = nrm1_ref.shape[1]
    strip = wff_ref.shape[0] // (win_ref.shape[1] // (SPREAD * STRIP))
    wff = stacked(
        [
            wff_ref[c : c + strip, b * width : (b + 1) * width]
            for c in range(0, wff_ref.shape[0], strip)
            for b in range(SPREAD)
        ]
    )

    cot_in = pltpu.make_async_copy(cot_ref, cot_here, sems.at[0])
    down_in = pltpu.make_async_copy(down_ref, down_here, sems.at[1])
    up_in = pltpu.make_async_copy(up_ref, up_here, sems.at[2])
    out_back = pltpu.make_async_copy(out_here, out_ref, sems.at[3])
    adapt_back = pltpu.make_async_copy(adapt_here, adapt_ref, sems.at[4])

    @pl.when((phase == 0) & (j == 0))
    def _():
        down_in.start()
        up_in.start()
        cot_in.start()
        for b in range(2):
            r = pl.ds(b * half, half)
            first = nrm1_ref[r, :] * norm_ref[0:1, :] + norm_ref[1:2, :]
            nrm, inv = norm_stats(first + dot_nn(att_ref[r, :], wco_ref[...]))
            nrm2_ref[r, :] = nrm
            inv2_ref[r, :] = inv
            second = nrm * norm_ref[2:3, :] + norm_ref[3:4, :]
            low_ref[r, :] = second.astype(BF)
            acc_ref[r, :] = second

    @pl.when(phase == 0)
    def _():
        act, slope = gelu_both(dot_nn(low_ref[...], win_ref[...]))
        slope_ref[j] = slope.astype(BF)
        acc_ref[...] += dot_nn(act.astype(BF), wff)

    @pl.when((phase == 1) & (j == 0))
    def _():
        down_in.wait()
        up_in.wait()
        cot_in.wait()
        act, slope = gelu_both(dot_nn(low_ref[...], down_here[...]) + db_ref[...])
        aact_ref[...] = act.astype(BF)
        aslope_ref[...] = slope.astype(BF)
        for s in range(seqs):
            r = pl.ds(s * tgt, tgt)
            adapted = dot_nn(aact_ref[r, :], up_here[...]) + ub_ref[...]
            nrm, inv = norm_stats(acc_ref[r, :] + 4.0 * adapted)
            out_here[r, :] = (nrm * norm_ref[4:5, :] + norm_ref[5:6, :]).astype(BF)
            live = lax.broadcasted_iota(jnp.int32, (tgt, 1), 0) < len_ref[s]
            go = jnp.where(live, cot_here[r, :].astype(F32), 0.0)
            gthree = norm_back(go, nrm, inv, norm_ref[4:5, :])
            g_ref[r, :] = gthree.astype(BF)
            acc_ref[r, :] = gthree
        out_back.start()
        agrad = g_ref[...] * 4.0
        adapt = aact_ref.shape[1]
        apg = (dot_nt(agrad, up_here[...]) * aslope_ref[...].astype(F32)).astype(BF)
        adapt_here[:, :adapt] = dot_tn(low_ref[...], apg).astype(BF)
        adapt_here[:, adapt : 2 * adapt] = dot_tn(agrad, aact_ref[...]).astype(BF)
        ones = jnp.ones((rows_all, PAIR), BF)
        down_sum = dot_tn(apg, ones).astype(BF)
        high = width // adapt
        row = lax.broadcasted_iota(jnp.int32, (width, adapt), 0)
        col = lax.broadcasted_iota(jnp.int32, (width, adapt), 1)
        block = BIAS_ROWS * high
        entry = lax.div(row, block) * BIAS_ROWS + lax.rem(row, block)
        chosen = (entry == col) & (lax.rem(row, block) < BIAS_ROWS)
        placed = dot_nn(jnp.where(chosen, 1.0, 0.0).astype(BF), down_sum)
        lane = lax.broadcasted_iota(jnp.int32, (width, PAIR), 1)
        sums = jnp.where(lane == 2 * PREFIX_PAD, dot_tn(agrad, ones), placed)
        sums = jnp.where((lane >= 2 * PREFIX_PAD) & (lane < 2 * PREFIX_PAD + 2), sums, 0.0)
        adapt_here[:, 2 * adapt :] = sums.astype(BF)
        adapt_back.start()
        acc_ref[...] += dot_nt(apg, down_here[...])

    @pl.when(phase == 1)
    def _():
        grad = (dot_nt(g_ref[...], wff) * slope_ref[j].astype(F32)).astype(BF)
        acc_ref[...] += dot_nt(grad, win_ref[...])

    @pl.when((phase == 1) & (j == last))
    def _():
        gtwo_ref[...] = norm_back(acc_ref[...], nrm2_ref[...], inv2_ref[...], norm_ref[2:3, :])
        out_back.wait()
        adapt_back.wait()


def cross_backward_kernel(
    len_ref, gtwo_ref, wco_ref, cq_ref, mk_ref, mv_ref, wk_ref, wv_ref, late_ref, nrm1_ref,
    inv1_ref, norm_ref,
    dmem_ref, gone_ref, gone_low_ref,
    low_ref, acc_ref, dk_ref, dv_ref, dq_ref, wcq_here, nrm1_here, sems,
):
    step = pl.program_id(0)
    seqs = len_ref.shape[0]
    tgt = cq_ref.shape[0] // seqs
    src = mk_ref.shape[0] // seqs
    width = gtwo_ref.shape[1]
    copies = [
        pltpu.make_async_copy(late_ref.at[:, pl.ds(CQ_AT, width)], wcq_here, sems.at[0]),
        pltpu.make_async_copy(nrm1_ref, nrm1_here, sems.at[1]),
    ]

    @pl.when(step == 0)
    def _():
        for copy in copies:
            copy.start()
        low_ref[...] = gtwo_ref[...].astype(BF)
        acc_ref[...] = jnp.zeros_like(acc_ref)

    mg_all = dot_nt(low_ref[...], wco_ref[...]).astype(BF)
    heads = GROUP // HEAD_DIM
    slot = lax.broadcasted_iota(jnp.int32, (src, tgt), 0)
    raw = []
    for s in range(seqs):
        q = cq_ref[s * tgt : (s + 1) * tgt, :] * SCALE
        mg = mg_all[s * tgt : (s + 1) * tgt]
        there = pl.ds(s * src, src)
        raw.append(
            (
                dot_nt(stacked(per_head(mk_ref[there, :])), q),
                dot_nt(stacked(per_head(mv_ref[there, :])), mg),
            )
        )
    for s in range(seqs):
        bias = jnp.where(slot < len_ref[s], 0.0, NEGATIVE)
        here = pl.ds(s * tgt, tgt)
        there = pl.ds(s * src, src)
        probs, grads = [], []
        for x, d in zip(cut(raw[s][0], heads, 0), cut(raw[s][1], heads, 0)):
            x = x + bias
            x = jnp.exp(x - jnp.max(x, axis=0, keepdims=True))
            x = x * (1.0 / jnp.sum(x, axis=0, keepdims=True))
            grads.append((x * (d - jnp.sum(x * d, axis=0, keepdims=True))).astype(BF))
            probs.append(x.astype(BF))
        q = cq_ref[here, :] * SCALE
        mg = mg_all[s * tgt : (s + 1) * tgt]
        dv_ref[there, :] = dot_nn(beside(probs), stacked(per_head(mg))).astype(BF)
        dk_ref[there, :] = dot_nn(beside(grads), stacked(per_head(q))).astype(BF)
        dq = dot_tn(stacked(grads), stacked(per_head(mk_ref[there, :])))
        lanes = pl.ds(pl.multiple_of(step * GROUP, GROUP), GROUP)
        dq_ref[here, lanes] = (dq * SCALE).astype(BF)
    acc_ref[...] += dot_nt(
        beside([dk_ref[...], dv_ref[...]]), beside([wk_ref[...], wv_ref[...]])
    )

    @pl.when(step == pl.num_programs(0) - 1)
    def _():
        parts, _, high, width = dmem_ref.shape
        for s in range(seqs):
            block = acc_ref[s * src : (s + 1) * src, :]
            dmem_ref[:, s] = block.reshape(parts, high, width).astype(BF)
        for copy in copies:
            copy.wait()
        grad_first = gtwo_ref[...] + dot_nt(dq_ref[...], wcq_here[...])
        grad_one = norm_back(grad_first, nrm1_here[...], inv1_ref[...], norm_ref[0:1, :])
        gone_ref[...] = grad_one
        gone_low_ref[...] = grad_one.astype(BF)


def self_backward_kernel(
    len_ref, low_ref, wo_ref, q_ref, k_ref, v_ref, pk_ref, pv_ref,
    dq_ref, dk_ref, dv_ref, small_ref,
):
    seqs = len_ref.shape[0]
    tgt = low_ref.shape[0] // seqs
    ag_all = dot_nt(low_ref[...], wo_ref[...]).astype(BF)
    heads = GROUP // HEAD_DIM
    row = lax.broadcasted_iota(jnp.int32, (tgt, tgt), 1)
    col = lax.broadcasted_iota(jnp.int32, (tgt, tgt), 0)
    prefix_bias = jnp.where(
        lax.broadcasted_iota(jnp.int32, (PREFIX_PAD, tgt), 0) < PREFIX, 0.0, NEGATIVE
    )
    pk = per_head(pk_ref[...])
    pv = per_head(pv_ref[...])
    dpk = jnp.zeros((PREFIX_PAD, GROUP), F32)
    dpv = jnp.zeros((PREFIX_PAD, GROUP), F32)
    split = heads * PREFIX_PAD
    raw = []
    for s in range(seqs):
        here = pl.ds(s * tgt, tgt)
        raw.append(
            (
                dot_nt(stacked(pk + per_head(k_ref[here, :])), q_ref[here, :] * SCALE),
                dot_nt(stacked(pv + per_head(v_ref[here, :])), ag_all[s * tgt : (s + 1) * tgt]),
            )
        )
    for s in range(seqs):
        bias = jnp.where((col <= row) & (col < len_ref[s]), 0.0, NEGATIVE)
        here = pl.ds(s * tgt, tgt)
        q = q_ref[here, :] * SCALE
        ag = ag_all[s * tgt : (s + 1) * tgt]
        keys = stacked(pk + per_head(k_ref[here, :]))
        scores, dprobs = raw[s]
        probs, grads = [], []
        for x, d, y, e in zip(
            cut(scores[split:], heads, 0),
            cut(dprobs[split:], heads, 0),
            cut(scores[:split], heads, 0),
            cut(dprobs[:split], heads, 0),
        ):
            x = x + bias
            y = y + prefix_bias
            top = jnp.maximum(jnp.max(x, axis=0, keepdims=True), jnp.max(y, axis=0, keepdims=True))
            x = jnp.exp(x - top)
            y = jnp.exp(y - top)
            inv = 1.0 / (jnp.sum(x, axis=0, keepdims=True) + jnp.sum(y, axis=0, keepdims=True))
            x = x * inv
            y = y * inv
            delta = jnp.sum(x * d, axis=0, keepdims=True) + jnp.sum(y * e, axis=0, keepdims=True)
            grads.append([(y * (e - delta)).astype(BF), (x * (d - delta)).astype(BF)])
            probs.append(stacked([y.astype(BF), x.astype(BF)]))
        dq = dot_tn(stacked([g[0] for g in grads] + [g[1] for g in grads]), keys)
        dk = dot_nn(beside([stacked(g) for g in grads]), stacked(per_head(q)))
        dv = dot_nn(beside(probs), stacked(per_head(ag)))
        dq_ref[here, :] = (dq * SCALE).astype(BF)
        dk_ref[here, :] = dk[PREFIX_PAD:].astype(BF)
        dv_ref[here, :] = dv[PREFIX_PAD:].astype(BF)
        dpk = dpk + dk[:PREFIX_PAD]
        dpv = dpv + dv[:PREFIX_PAD]
    for p in range(GROUP // PAIR):
        at = slice(p * PAIR, (p + 1) * PAIR)
        both = stacked(
            [dpk[:, at], dpv[:, at], jnp.zeros((PAIR - 2 * PREFIX_PAD, PAIR), F32)]
        )
        small_ref[at, :] = both.T


def input_grad_kernel(gone_ref, dq_ref, dk_ref, dv_ref, wq_ref, wk_ref, wv_ref, din_ref):
    din_ref[...] = (
        gone_ref[...]
        + dot_nt(
            beside([dq_ref[...], dk_ref[...], dv_ref[...]]),
            beside([wq_ref[...], wk_ref[...], wv_ref[...]]),
        )
    ).astype(BF)


ANYWHERE = pl.BlockSpec(memory_space=pl.ANY)


def square(width, at):
    return pl.BlockSpec((width, width), lambda *_: (0, at // width))


def whole(shape):
    return pl.BlockSpec(shape, lambda *_: (0,) * len(shape))


def columns(rows, width, offset=0):
    return pl.BlockSpec((rows, width), lambda i, *_: (0, i + offset))


def rows_of(height, width, at):
    return pl.BlockSpec((height, width), lambda i, *_: (i, at // width))


def shaped(shape, dtype):
    return jax.ShapeDtypeStruct(shape, dtype)


def call(kernel, grid, in_specs, out_specs, outs, scratch, flops, moved, *args):
    return pl.pallas_call(
        kernel,
        grid_spec=pltpu.PrefetchScalarGridSpec(
            num_scalar_prefetch=1,
            grid=grid,
            in_specs=in_specs,
            out_specs=out_specs,
            scratch_shapes=scratch,
        ),
        out_shape=outs,
        compiler_params=pltpu.CompilerParams(
            vmem_limit_bytes=VMEM_BYTES,
            dimension_semantics=("arbitrary",) * len(grid),
        ),
        cost_estimate=pl.CostEstimate(flops=flops, bytes_accessed=moved, transcendentals=0),
    )(*args)


def self_forward(lens, tok, early, pk, pv):
    rows, width = tok.shape
    steps = width // GROUP
    return call(
        self_forward_kernel,
        (steps,),
        [
            whole((rows, width)),
            columns(width, GROUP),
            columns(width, GROUP, steps),
            columns(width, GROUP, 2 * steps),
            columns(PREFIX_PAD, GROUP),
            columns(PREFIX_PAD, GROUP),
        ],
        [columns(rows, GROUP)] * 4,
        [shaped((rows, width), BF)] * 4,
        [],
        2 * rows * width * width * 3,
        14 * width * width,
        lens, tok, early, early, early, pk, pv,
    )


def cross_forward(lens, mem, late, tok, att, norms):
    rows, width = tok.shape
    steps = width // GROUP
    places = mem.shape[0]
    return call(
        cross_forward_kernel,
        (steps,),
        [
            whole((places, width)),
            columns(width, GROUP, KV_AT // GROUP),
            columns(width, GROUP, KV_AT // GROUP + steps),
            whole((rows, width)),
            whole((rows, width)),
            square(width, SOUT_AT),
            square(width, CQ_AT),
            whole(norms.shape),
        ],
        [columns(places, GROUP)] * 2
        + [whole((rows, width)), whole((rows, width)), whole((rows, 1)), columns(rows, GROUP)],
        [shaped((places, width), BF)] * 2
        + [shaped((rows, width), BF), shaped((rows, width), F32), shaped((rows, 1), F32)]
        + [shaped((rows, width), BF)],
        [],
        2 * width * width * (2 * rows + 2 * places),
        16 * width * width,
        lens, mem, late, late, tok, att, late, late, norms,
    )


def ffn(lens, nrm1, att, cot, late, down, db, up, ub, norms):
    rows, width = nrm1.shape
    hidden = SPREAD * width
    adapt = down.shape[1]
    block = FFN_BLOCK
    steps = hidden // block
    return call(
        ffn_kernel,
        (2, steps),
        [
            whole((rows, width)),
            whole((rows, width)),
            square(width, OUT_AT),
            ANYWHERE,
            pl.BlockSpec((width, block), lambda p, j, *_: (0, j + IN_AT // block)),
            pl.BlockSpec((block // SPREAD, SPREAD * width), lambda p, j, *_: (j, FF_AT)),
            ANYWHERE,
            whole((1, adapt)),
            ANYWHERE,
            whole((1, width)),
            whole(norms.shape),
        ],
        [ANYWHERE, whole((rows, width)), ANYWHERE],
        [
            shaped((rows, width), BF),
            shaped((rows, width), F32),
            shaped((width, 2 * adapt + PAIR), BF),
        ],
        [
            pltpu.VMEM((rows, width), F32),
            pltpu.VMEM((rows, 1), F32),
            pltpu.VMEM((rows, width), F32),
            pltpu.VMEM((rows, width), BF),
            pltpu.VMEM((steps, rows, block), BF),
            pltpu.VMEM((rows, adapt), BF),
            pltpu.VMEM((rows, adapt), BF),
            pltpu.VMEM((rows, width), BF),
            pltpu.VMEM((rows, width), BF),
            pltpu.VMEM((width, adapt), BF),
            pltpu.VMEM((adapt, width), BF),
            pltpu.VMEM((rows, width), BF),
            pltpu.VMEM((width, 2 * adapt + PAIR), BF),
            pltpu.SemaphoreType.DMA((5,)),
        ],
        2 * rows * width * (4 * hidden + 6 * adapt),
        8 * width * hidden,
        lens, nrm1, att, late, cot, late, late, down, db, up, ub, norms,
    )


def cross_backward(lens, gtwo, late, cq, mk, mv, nrm1, inv1, norms, parts):
    rows, width = cq.shape
    steps = width // GROUP
    places = mk.shape[0]
    seqs = lens.shape[0]
    sent = (parts, seqs, places // seqs // parts, width)
    return call(
        cross_backward_kernel,
        (steps,),
        [
            whole((rows, width)),
            rows_of(GROUP, width, OUT_AT),
            columns(rows, GROUP),
            columns(places, GROUP),
            columns(places, GROUP),
            columns(width, GROUP, KV_AT // GROUP),
            columns(width, GROUP, KV_AT // GROUP + steps),
            ANYWHERE,
            ANYWHERE,
            whole((rows, 1)),
            whole(norms.shape),
        ],
        [whole(sent), whole((rows, width)), whole((rows, width))],
        [shaped(sent, BF), shaped((rows, width), F32), shaped((rows, width), BF)],
        [
            pltpu.VMEM((rows, width), BF),
            pltpu.VMEM((places, width), F32),
            pltpu.VMEM((places, GROUP), BF),
            pltpu.VMEM((places, GROUP), BF),
            pltpu.VMEM((rows, width), BF),
            pltpu.VMEM((width, width), BF),
            pltpu.VMEM((rows, width), F32),
            pltpu.SemaphoreType.DMA((2,)),
        ],
        2 * width * width * (rows + 2 * places),
        14 * width * width,
        lens, gtwo, late, cq, mk, mv, late, late, late, nrm1, inv1, norms,
    )


def self_backward(lens, gone_low, late, q, k, v, pk, pv):
    rows, width = q.shape
    steps = width // GROUP
    return call(
        self_backward_kernel,
        (steps,),
        [whole((rows, width)), rows_of(GROUP, width, SOUT_AT)]
        + [columns(rows, GROUP)] * 3
        + [columns(PREFIX_PAD, GROUP)] * 2,
        [columns(rows, GROUP)] * 3 + [pl.BlockSpec((GROUP, PAIR), lambda i, *_: (i, 0))],
        [shaped((rows, width), BF)] * 3 + [shaped((width, PAIR), F32)],
        [],
        2 * rows * width * width * 4,
        20 * width * width,
        lens, gone_low, late, q, k, v, pk, pv,
    )


def input_gradient(gone, dq, dk, dv, early):
    rows, width = gone.shape

    def part(index):
        return pl.BlockSpec((GROUP, width), lambda i: (i, index))

    return pl.pallas_call(
        input_grad_kernel,
        grid=(width // GROUP,),
        in_specs=[pl.BlockSpec((rows, GROUP), lambda i: (0, i))]
        + [whole((rows, width))] * 3
        + [part(0), part(1), part(2)],
        out_specs=pl.BlockSpec((rows, GROUP), lambda i: (0, i)),
        out_shape=shaped((rows, width), BF),
        compiler_params=pltpu.CompilerParams(
            vmem_limit_bytes=VMEM_BYTES, dimension_semantics=("arbitrary",)
        ),
        cost_estimate=pl.CostEstimate(
            flops=6 * rows * width * width, bytes_accessed=12 * width * width, transcendentals=0
        ),
    )(gone, dq, dk, dv, early, early, early)


def around(count, by):
    return [(i, (i + by) % count) for i in range(count)]


def ring_gather(shard, other):
    rows = shard.shape[0]
    half = rows // 2
    count = lax.axis_size("dp_0")
    x, core = lax.axis_index("dp_0"), lax.axis_index("dp_1")
    below = lax.ppermute(shard, "dp_0", around(count, 1))
    above = lax.ppermute(shard, "dp_0", around(count, -1))
    filled = jnp.zeros((count * 2 * rows, shard.shape[1]), shard.dtype)
    filled, other = lax.optimization_barrier((filled, other))
    far_low = lax.ppermute(below[:half], "dp_0", around(count, 1))
    far_high = lax.ppermute(above[half:], "dp_0", around(count, -1))
    for piece, offset, start in (
        (shard, 0, 0), (below, -1, 0), (above, 1, 0), (far_low, 2, 0), (far_high, 2, half),
    ):
        swapped = lax.ppermute(piece, "dp_1", around(2, 1))
        chip = (x + offset + count) % count
        for part, place in ((piece, core), (swapped, 1 - core)):
            at = (chip * 2 + place) * rows + start
            filled = lax.dynamic_update_slice_in_dim(filled, part, at, 0)
    return filled, other


def scatter_sum(blocks):
    count = lax.axis_size("dp_0")
    x, core = lax.axis_index("dp_0"), lax.axis_index("dp_1")
    by_core = blocks.reshape(count, 2, *blocks.shape[1:])
    kept = lax.dynamic_index_in_dim(by_core, core, 1, keepdims=False)
    given = lax.dynamic_index_in_dim(by_core, 1 - core, 1, keepdims=False)
    paired = kept + lax.ppermute(given, "dp_1", around(2, 1))
    total = lax.dynamic_index_in_dim(paired, x, 0, keepdims=False)
    for by in range(1, count):
        sent = lax.dynamic_index_in_dim(paired, (x + by) % count, 0, keepdims=False)
        total = total + lax.ppermute(sent, "dp_0", around(count, by))
    return total


def local(
    tokens, memory, cotangent, tgt_len, src_len,
    self_qkv, self_out, cross_q, cross_kv, cross_out, ffn_in, ffn_out,
    first_gain, first_bias, second_gain, second_bias, third_gain, third_bias,
    prefix_key, prefix_value, down_weight, down_bias, up_weight, up_bias,
):
    mem_groups = lax.axis_size(MEM)
    mem_place = lax.axis_index(MEM)
    seqs, tgt, width = tokens.shape
    src_block = memory.shape[1]
    prefix = prefix_key.shape[0]

    high = cross_out.shape[0] // mem_groups
    mine = functools.partial(
        lax.dynamic_slice_in_dim, start_index=mem_place * high, slice_size=high
    )
    spread = mine(ffn_out.reshape(SPREAD, -1, width), axis=1)
    late = lax.all_gather(
        jnp.concatenate(
            [jnp.moveaxis(spread, 0, 1).reshape(high, SPREAD * width)]
            + [mine(w, axis=0) for w in (ffn_in, cross_out, self_out, cross_q, cross_kv)],
            axis=1,
        ),
        DP_MEM, axis=0, tiled=True,
    )
    early, memory = ring_gather(self_qkv, memory)
    mem_rows = lax.all_to_all(memory, MEM, split_axis=0, concat_axis=1, tiled=True)
    mem_rows = mem_rows.reshape(-1, width)
    own_src = lax.dynamic_slice_in_dim(src_len, mem_place * seqs, seqs, 0)

    tok = tokens.reshape(seqs * tgt, width)
    cot = cotangent.reshape(seqs * tgt, width)
    pk = jnp.pad(prefix_key, ((0, PREFIX_PAD - prefix), (0, 0)))
    pv = jnp.pad(prefix_value, ((0, PREFIX_PAD - prefix), (0, 0)))

    q, k, v, att = self_forward(tgt_len, tok, early, pk, pv)
    vectors = jnp.stack(
        [first_gain, first_bias, second_gain, second_bias, third_gain, third_bias]
        + [third_bias] * 2
    )
    vectors, att = lax.optimization_barrier((vectors, att))
    norms = lax.all_gather(vectors, DP, axis=1, tiled=True).astype(F32)
    mk, mv, cq, nrm1, inv1, cross = cross_forward(own_src, mem_rows, late, tok, att, norms)
    output, gtwo, adapter = ffn(
        tgt_len, nrm1, cross, cot, late,
        down_weight, down_bias.astype(F32)[None], up_weight, up_bias.astype(F32)[None], norms,
    )
    adapter = lax.psum_scatter(adapter, DP, scatter_dimension=0, tiled=True)

    dmem, gone, gone_low = cross_backward(
        own_src, gtwo, late, cq, mk, mv, nrm1, inv1, norms, mem_groups
    )
    memory_grad = lax.all_to_all(dmem, MEM, split_axis=0, concat_axis=0, tiled=True)
    dq, dk, dv, small = self_backward(tgt_len, gone_low, late, q, k, v, pk, pv)
    small = scatter_sum(small.reshape(lax.axis_size(DP), -1, PAIR))
    dq, small, memory_grad = lax.optimization_barrier((dq, small, memory_grad))
    din = input_gradient(gone, dq, dk, dv, early)
    adapt = down_weight.shape[1]
    joined = (adapter.astype(F32) + jnp.pad(small, ((0, 0), (2 * adapt, 0)))).astype(BF)
    arrived = lax.all_to_all(
        joined.reshape(mem_groups, -1, joined.shape[1]),
        MEM, split_axis=0, concat_axis=0, tiled=True,
    )
    down_grad, up_grad, last = (
        jnp.sum(arrived[..., a:b].astype(F32), axis=0)
        for a, b in ((0, adapt), (adapt, 2 * adapt), (2 * adapt, joined.shape[1]))
    )
    return (
        output.reshape(tokens.shape),
        din.reshape(tokens.shape),
        memory_grad.reshape(memory.shape),
        last[:, :prefix].T,
        last[:, PREFIX_PAD : PREFIX_PAD + prefix].T,
        down_grad,
        last[:BIAS_ROWS, 2 * PREFIX_PAD + 1],
        up_grad.T,
        last[:, 2 * PREFIX_PAD],
    )


def solution(mesh):
    torus = Mesh(mesh.devices.reshape(4, 2, 4, 4), ("dp_0", "dp_1", "mem_0", "mem_1"))
    by_dp = P(DP, None)
    copied = P(None)
    return jax.shard_map(
        local,
        mesh=torus,
        in_specs=(
            P(DP_MEM, None, None), P(DP, MEM, None), P(DP_MEM, None, None), P(DP_MEM), P(DP),
            by_dp, by_dp, by_dp, by_dp, by_dp, by_dp, by_dp,
            P(DP), P(DP), P(DP), P(DP), P(DP), P(DP),
            copied, copied, copied, copied, copied, copied,
        ),
        out_specs=(
            P(DP_MEM, None, None),
            P(DP_MEM, None, None),
            P(DP, MEM, None),
            P(None, DP_MEM),
            P(None, DP_MEM),
            P(DP_MEM, None),
            P(DP_MEM),
            P(None, DP_MEM),
            P(DP_MEM),
        ),
        check_vma=False,
    )
```

```python
import functools

import jax
import jax.numpy as jnp
from jax import lax
from jax.experimental import pallas as pl
from jax.experimental.pallas import tpu as pltpu
from jax.sharding import Mesh
from jax.sharding import PartitionSpec as P

HEAD_DIM = 64
PAIR = 128
GROUP = 256
PREFIX = 30
PREFIX_PAD = 32
BIAS_ROWS = 4
MEM = ("mem_0", "mem_1")
DP = ("dp_0", "dp_1")
DP_MEM = ("dp_0", "dp_1", "mem_0", "mem_1")

NEGATIVE = -1e30
EPSILON = 1e-05
SCALE = HEAD_DIM ** (-0.5)
BF = jnp.bfloat16
F32 = jnp.float32
SPREAD = 4
STRIP = 128
FFN_BLOCK = 1024
FF_AT = 0
IN_AT = 4096
OUT_AT = 8192
SOUT_AT = 9216
CQ_AT = 10240
KV_AT = 11264
VMEM_BYTES = 60 * 1024 * 1024


def dot_nn(left, right):
    return lax.dot_general(left, right, (((1,), (0,)), ((), ())), preferred_element_type=F32)


def dot_nt(left, right):
    return lax.dot_general(left, right, (((1,), (1,)), ((), ())), preferred_element_type=F32)


def dot_tn(left, right):
    return lax.dot_general(left, right, (((0,), (0,)), ((), ())), preferred_element_type=F32)


def per_head(x):
    lane = lax.broadcasted_iota(jnp.int32, (1, GROUP), 1)
    return [
        x * jnp.where(lane // HEAD_DIM == h, 1.0, 0.0).astype(BF)
        for h in range(GROUP // HEAD_DIM)
    ]


def stacked(parts):
    return jnp.concatenate(parts, axis=0)


def beside(parts):
    return jnp.concatenate(parts, axis=1)


def cut(x, count, axis):
    size = x.shape[axis] // count
    return [lax.slice_in_dim(x, i * size, (i + 1) * size, axis=axis) for i in range(count)]


def norm_stats(hidden):
    centred = hidden - jnp.mean(hidden, axis=-1, keepdims=True)
    inverse = lax.rsqrt(jnp.mean(centred * centred, axis=-1, keepdims=True) + EPSILON)
    return centred * inverse, inverse


def norm_back(grad_in, normed, inverse, gain):
    scaled = grad_in * gain
    return inverse * (
        scaled
        - jnp.mean(scaled, axis=-1, keepdims=True)
        - normed * jnp.mean(scaled * normed, axis=-1, keepdims=True)
    )


def gelu_both(pre):
    cdf = 0.5 * (1.0 + lax.erf(pre * (0.5**0.5)))
    density = jnp.exp(-0.5 * pre * pre) * 0.3989422804014327
    return pre * cdf, cdf + pre * density


def self_forward_kernel(
    len_ref, tok_ref, wq_ref, wk_ref, wv_ref, pk_ref, pv_ref,
    q_ref, k_ref, v_ref, att_ref,
):
    seqs = len_ref.shape[0]
    rows_all = tok_ref.shape[0]
    tgt = rows_all // seqs
    projected = dot_nn(tok_ref[...], beside([wq_ref[...], wk_ref[...], wv_ref[...]])).astype(BF)
    q_ref[...] = projected[:, :GROUP]
    k_ref[...] = projected[:, GROUP : 2 * GROUP]
    v_ref[...] = projected[:, 2 * GROUP :]
    heads = GROUP // HEAD_DIM
    row = lax.broadcasted_iota(jnp.int32, (tgt, tgt), 0)
    col = lax.broadcasted_iota(jnp.int32, (tgt, tgt), 1)
    prefix_bias = jnp.where(
        lax.broadcasted_iota(jnp.int32, (1, PREFIX_PAD), 1) < PREFIX, 0.0, NEGATIVE
    )
    pk = per_head(pk_ref[...])
    pv = per_head(pv_ref[...])
    ones = stacked(
        per_head(jnp.ones((PREFIX_PAD, GROUP), BF)) + per_head(jnp.ones((tgt, GROUP), BF))
    )
    scores = []
    for s in range(seqs):
        here = pl.ds(s * tgt, tgt)
        scores.append(dot_nt(q_ref[here, :] * SCALE, stacked(pk + per_head(k_ref[here, :]))))
    for s in range(seqs):
        here = pl.ds(s * tgt, tgt)
        bias = jnp.where((col <= row) & (col < len_ref[s]), 0.0, NEGATIVE)
        pre = cut(scores[s][:, : heads * PREFIX_PAD], heads, 1)
        own = cut(scores[s][:, heads * PREFIX_PAD :], heads, 1)
        own_probs, pre_probs = [], []
        for x, y in zip(own, pre):
            x = x + bias
            y = y + prefix_bias
            top = jnp.maximum(jnp.max(x, axis=1, keepdims=True), jnp.max(y, axis=1, keepdims=True))
            own_probs.append(jnp.exp(x - top).astype(BF))
            pre_probs.append(jnp.exp(y - top).astype(BF))
        probs = beside(pre_probs + own_probs)
        total = dot_nn(probs, stacked(pv + per_head(v_ref[here, :])))
        att_ref[here, :] = (total / dot_nn(probs, ones)).astype(BF)


def cross_forward_kernel(
    len_ref, mem_ref, wk_ref, wv_ref, tok_ref, self_ref, wo_ref, wcq_ref, norm_ref,
    mk_ref, mv_ref, cq_ref, nrm1_ref, inv1_ref, att_ref,
):
    step = pl.program_id(0)
    seqs = len_ref.shape[0]
    tgt = tok_ref.shape[0] // seqs
    src = mem_ref.shape[0] // seqs

    @pl.when(step == 0)
    def _():
        for s in range(seqs):
            r = pl.ds(s * tgt, tgt)
            nrm, inv = norm_stats(
                tok_ref[r, :].astype(F32) + dot_nn(self_ref[r, :], wo_ref[...])
            )
            nrm1_ref[r, :] = nrm
            inv1_ref[r, :] = inv
            first = nrm * norm_ref[0:1, :] + norm_ref[1:2, :]
            cq_ref[r, :] = dot_nn(first.astype(BF), wcq_ref[...]).astype(BF)

    mem = mem_ref[...]
    projected = dot_nn(mem, beside([wk_ref[...], wv_ref[...]])).astype(BF)
    mk_ref[...] = projected[:, :GROUP]
    mv_ref[...] = projected[:, GROUP:]
    heads = GROUP // HEAD_DIM
    lanes = pl.ds(pl.multiple_of(step * GROUP, GROUP), GROUP)
    slot = lax.broadcasted_iota(jnp.int32, (1, src), 1)
    ones = stacked(per_head(jnp.ones((src, GROUP), BF)))
    scores = []
    for s in range(seqs):
        q = cq_ref[s * tgt : (s + 1) * tgt, lanes] * SCALE
        scores.append(dot_nt(q, stacked(per_head(mk_ref[s * src : (s + 1) * src, :]))))
    for s in range(seqs):
        bias = jnp.where(slot < len_ref[s], 0.0, NEGATIVE)
        probs = []
        for x in cut(scores[s], heads, 1):
            x = x + bias
            probs.append(jnp.exp(x - jnp.max(x, axis=1, keepdims=True)).astype(BF))
        probs = beside(probs)
        total = dot_nn(probs, stacked(per_head(mv_ref[s * src : (s + 1) * src, :])))
        att_ref[s * tgt : (s + 1) * tgt, :] = (total / dot_nn(probs, ones)).astype(BF)


def ffn_kernel(
    len_ref, nrm1_ref, att_ref, wco_ref, cot_ref, win_ref, wff_ref, down_ref, db_ref, up_ref, ub_ref,
    norm_ref,
    out_ref, gtwo_ref, adapt_ref,
    nrm2_ref, inv2_ref, acc_ref, low_ref, slope_ref, aact_ref, aslope_ref, g_ref,
    cot_here, down_here, up_here, out_here, adapt_here, sems,
):
    phase = pl.program_id(0)
    j = pl.program_id(1)
    last = pl.num_programs(1) - 1
    seqs = len_ref.shape[0]
    rows_all = nrm1_ref.shape[0]
    tgt = rows_all // seqs
    half = rows_all // 2
    width = nrm1_ref.shape[1]
    strip = wff_ref.shape[0] // (win_ref.shape[1] // (SPREAD * STRIP))
    wff = stacked(
        [
            wff_ref[c : c + strip, b * width : (b + 1) * width]
            for c in range(0, wff_ref.shape[0], strip)
            for b in range(SPREAD)
        ]
    )

    cot_in = pltpu.make_async_copy(cot_ref, cot_here, sems.at[0])
    down_in = pltpu.make_async_copy(down_ref, down_here, sems.at[1])
    up_in = pltpu.make_async_copy(up_ref, up_here, sems.at[2])
    out_back = pltpu.make_async_copy(out_here, out_ref, sems.at[3])
    adapt_back = pltpu.make_async_copy(adapt_here, adapt_ref, sems.at[4])

    @pl.when((phase == 0) & (j == 0))
    def _():
        down_in.start()
        up_in.start()
        cot_in.start()
        for b in range(2):
            r = pl.ds(b * half, half)
            first = nrm1_ref[r, :] * norm_ref[0:1, :] + norm_ref[1:2, :]
            nrm, inv = norm_stats(first + dot_nn(att_ref[r, :], wco_ref[...]))
            nrm2_ref[r, :] = nrm
            inv2_ref[r, :] = inv
            second = nrm * norm_ref[2:3, :] + norm_ref[3:4, :]
            low_ref[r, :] = second.astype(BF)
            acc_ref[r, :] = second

    @pl.when(phase == 0)
    def _():
        act, slope = gelu_both(dot_nn(low_ref[...], win_ref[...]))
        slope_ref[j] = slope.astype(BF)
        acc_ref[...] += dot_nn(act.astype(BF), wff)

    @pl.when((phase == 1) & (j == 0))
    def _():
        down_in.wait()
        up_in.wait()
        cot_in.wait()
        act, slope = gelu_both(dot_nn(low_ref[...], down_here[...]) + db_ref[...])
        aact_ref[...] = act.astype(BF)
        aslope_ref[...] = slope.astype(BF)
        for s in range(seqs):
            r = pl.ds(s * tgt, tgt)
            adapted = dot_nn(aact_ref[r, :], up_here[...]) + ub_ref[...]
            nrm, inv = norm_stats(acc_ref[r, :] + 4.0 * adapted)
            out_here[r, :] = (nrm * norm_ref[4:5, :] + norm_ref[5:6, :]).astype(BF)
            live = lax.broadcasted_iota(jnp.int32, (tgt, 1), 0) < len_ref[s]
            go = jnp.where(live, cot_here[r, :].astype(F32), 0.0)
            gthree = norm_back(go, nrm, inv, norm_ref[4:5, :])
            g_ref[r, :] = gthree.astype(BF)
            acc_ref[r, :] = gthree
        out_back.start()
        agrad = g_ref[...] * 4.0
        adapt = aact_ref.shape[1]
        apg = (dot_nt(agrad, up_here[...]) * aslope_ref[...].astype(F32)).astype(BF)
        adapt_here[:, :adapt] = dot_tn(low_ref[...], apg).astype(BF)
        adapt_here[:, adapt : 2 * adapt] = dot_tn(agrad, aact_ref[...]).astype(BF)
        ones = jnp.ones((rows_all, PAIR), BF)
        down_sum = dot_tn(apg, ones).astype(BF)
        high = width // adapt
        row = lax.broadcasted_iota(jnp.int32, (width, adapt), 0)
        col = lax.broadcasted_iota(jnp.int32, (width, adapt), 1)
        block = BIAS_ROWS * high
        entry = lax.div(row, block) * BIAS_ROWS + lax.rem(row, block)
        chosen = (entry == col) & (lax.rem(row, block) < BIAS_ROWS)
        placed = dot_nn(jnp.where(chosen, 1.0, 0.0).astype(BF), down_sum)
        lane = lax.broadcasted_iota(jnp.int32, (width, PAIR), 1)
        sums = jnp.where(lane == 2 * PREFIX_PAD, dot_tn(agrad, ones), placed)
        sums = jnp.where((lane >= 2 * PREFIX_PAD) & (lane < 2 * PREFIX_PAD + 2), sums, 0.0)
        adapt_here[:, 2 * adapt :] = sums.astype(BF)
        adapt_back.start()
        acc_ref[...] += dot_nt(apg, down_here[...])

    @pl.when(phase == 1)
    def _():
        grad = (dot_nt(g_ref[...], wff) * slope_ref[j].astype(F32)).astype(BF)
        acc_ref[...] += dot_nt(grad, win_ref[...])

    @pl.when((phase == 1) & (j == last))
    def _():
        gtwo_ref[...] = norm_back(acc_ref[...], nrm2_ref[...], inv2_ref[...], norm_ref[2:3, :])
        out_back.wait()
        adapt_back.wait()


def cross_backward_kernel(
    len_ref, gtwo_ref, wco_ref, cq_ref, mk_ref, mv_ref, wk_ref, wv_ref, late_ref, nrm1_ref,
    inv1_ref, norm_ref,
    dmem_ref, gone_ref, gone_low_ref,
    low_ref, acc_ref, dk_ref, dv_ref, dq_ref, wcq_here, nrm1_here, sems,
):
    step = pl.program_id(0)
    seqs = len_ref.shape[0]
    tgt = cq_ref.shape[0] // seqs
    src = mk_ref.shape[0] // seqs
    width = gtwo_ref.shape[1]
    copies = [
        pltpu.make_async_copy(late_ref.at[:, pl.ds(CQ_AT, width)], wcq_here, sems.at[0]),
        pltpu.make_async_copy(nrm1_ref, nrm1_here, sems.at[1]),
    ]

    @pl.when(step == 0)
    def _():
        for copy in copies:
            copy.start()
        low_ref[...] = gtwo_ref[...].astype(BF)
        acc_ref[...] = jnp.zeros_like(acc_ref)

    mg_all = dot_nt(low_ref[...], wco_ref[...]).astype(BF)
    heads = GROUP // HEAD_DIM
    slot = lax.broadcasted_iota(jnp.int32, (src, tgt), 0)
    raw = []
    for s in range(seqs):
        q = cq_ref[s * tgt : (s + 1) * tgt, :] * SCALE
        mg = mg_all[s * tgt : (s + 1) * tgt]
        there = pl.ds(s * src, src)
        raw.append(
            (
                dot_nt(stacked(per_head(mk_ref[there, :])), q),
                dot_nt(stacked(per_head(mv_ref[there, :])), mg),
            )
        )
    for s in range(seqs):
        bias = jnp.where(slot < len_ref[s], 0.0, NEGATIVE)
        here = pl.ds(s * tgt, tgt)
        there = pl.ds(s * src, src)
        probs, grads = [], []
        for x, d in zip(cut(raw[s][0], heads, 0), cut(raw[s][1], heads, 0)):
            x = x + bias
            x = jnp.exp(x - jnp.max(x, axis=0, keepdims=True))
            x = x * (1.0 / jnp.sum(x, axis=0, keepdims=True))
            grads.append((x * (d - jnp.sum(x * d, axis=0, keepdims=True))).astype(BF))
            probs.append(x.astype(BF))
        q = cq_ref[here, :] * SCALE
        mg = mg_all[s * tgt : (s + 1) * tgt]
        dv_ref[there, :] = dot_nn(beside(probs), stacked(per_head(mg))).astype(BF)
        dk_ref[there, :] = dot_nn(beside(grads), stacked(per_head(q))).astype(BF)
        dq = dot_tn(stacked(grads), stacked(per_head(mk_ref[there, :])))
        lanes = pl.ds(pl.multiple_of(step * GROUP, GROUP), GROUP)
        dq_ref[here, lanes] = (dq * SCALE).astype(BF)
    acc_ref[...] += dot_nt(
        beside([dk_ref[...], dv_ref[...]]), beside([wk_ref[...], wv_ref[...]])
    )

    @pl.when(step == pl.num_programs(0) - 1)
    def _():
        parts, _, high, width = dmem_ref.shape
        for s in range(seqs):
            block = acc_ref[s * src : (s + 1) * src, :]
            dmem_ref[:, s] = block.reshape(parts, high, width).astype(BF)
        for copy in copies:
            copy.wait()
        grad_first = gtwo_ref[...] + dot_nt(dq_ref[...], wcq_here[...])
        grad_one = norm_back(grad_first, nrm1_here[...], inv1_ref[...], norm_ref[0:1, :])
        gone_ref[...] = grad_one
        gone_low_ref[...] = grad_one.astype(BF)


def self_backward_kernel(
    len_ref, low_ref, wo_ref, q_ref, k_ref, v_ref, pk_ref, pv_ref,
    dq_ref, dk_ref, dv_ref, small_ref,
):
    seqs = len_ref.shape[0]
    tgt = low_ref.shape[0] // seqs
    ag_all = dot_nt(low_ref[...], wo_ref[...]).astype(BF)
    heads = GROUP // HEAD_DIM
    row = lax.broadcasted_iota(jnp.int32, (tgt, tgt), 1)
    col = lax.broadcasted_iota(jnp.int32, (tgt, tgt), 0)
    prefix_bias = jnp.where(
        lax.broadcasted_iota(jnp.int32, (PREFIX_PAD, tgt), 0) < PREFIX, 0.0, NEGATIVE
    )
    pk = per_head(pk_ref[...])
    pv = per_head(pv_ref[...])
    dpk = jnp.zeros((PREFIX_PAD, GROUP), F32)
    dpv = jnp.zeros((PREFIX_PAD, GROUP), F32)
    split = heads * PREFIX_PAD
    raw = []
    for s in range(seqs):
        here = pl.ds(s * tgt, tgt)
        raw.append(
            (
                dot_nt(stacked(pk + per_head(k_ref[here, :])), q_ref[here, :] * SCALE),
                dot_nt(stacked(pv + per_head(v_ref[here, :])), ag_all[s * tgt : (s + 1) * tgt]),
            )
        )
    for s in range(seqs):
        bias = jnp.where((col <= row) & (col < len_ref[s]), 0.0, NEGATIVE)
        here = pl.ds(s * tgt, tgt)
        q = q_ref[here, :] * SCALE
        ag = ag_all[s * tgt : (s + 1) * tgt]
        keys = stacked(pk + per_head(k_ref[here, :]))
        scores, dprobs = raw[s]
        probs, grads = [], []
        for x, d, y, e in zip(
            cut(scores[split:], heads, 0),
            cut(dprobs[split:], heads, 0),
            cut(scores[:split], heads, 0),
            cut(dprobs[:split], heads, 0),
        ):
            x = x + bias
            y = y + prefix_bias
            top = jnp.maximum(jnp.max(x, axis=0, keepdims=True), jnp.max(y, axis=0, keepdims=True))
            x = jnp.exp(x - top)
            y = jnp.exp(y - top)
            inv = 1.0 / (jnp.sum(x, axis=0, keepdims=True) + jnp.sum(y, axis=0, keepdims=True))
            x = x * inv
            y = y * inv
            delta = jnp.sum(x * d, axis=0, keepdims=True) + jnp.sum(y * e, axis=0, keepdims=True)
            grads.append([(y * (e - delta)).astype(BF), (x * (d - delta)).astype(BF)])
            probs.append(stacked([y.astype(BF), x.astype(BF)]))
        dq = dot_tn(stacked([g[0] for g in grads] + [g[1] for g in grads]), keys)
        dk = dot_nn(beside([stacked(g) for g in grads]), stacked(per_head(q)))
        dv = dot_nn(beside(probs), stacked(per_head(ag)))
        dq_ref[here, :] = (dq * SCALE).astype(BF)
        dk_ref[here, :] = dk[PREFIX_PAD:].astype(BF)
        dv_ref[here, :] = dv[PREFIX_PAD:].astype(BF)
        dpk = dpk + dk[:PREFIX_PAD]
        dpv = dpv + dv[:PREFIX_PAD]
    for p in range(GROUP // PAIR):
        at = slice(p * PAIR, (p + 1) * PAIR)
        both = stacked(
            [dpk[:, at], dpv[:, at], jnp.zeros((PAIR - 2 * PREFIX_PAD, PAIR), F32)]
        )
        small_ref[at, :] = both.T


def input_grad_kernel(
    gone_ref, dq_ref, dk_ref, dv_ref, wq_ref, wk_ref, wv_ref, arrived_ref, din_ref, given_ref, sem
):
    handed_on = pltpu.make_async_copy(arrived_ref, given_ref, sem.at[0])

    @pl.when(pl.program_id(0) == 0)
    def _():
        handed_on.start()

    din_ref[...] = (
        gone_ref[...]
        + dot_nt(
            beside([dq_ref[...], dk_ref[...], dv_ref[...]]),
            beside([wq_ref[...], wk_ref[...], wv_ref[...]]),
        )
    ).astype(BF)

    @pl.when(pl.program_id(0) == pl.num_programs(0) - 1)
    def _():
        handed_on.wait()


ANYWHERE = pl.BlockSpec(memory_space=pl.ANY)


def square(width, at):
    return pl.BlockSpec((width, width), lambda *_: (0, at // width))


def whole(shape):
    return pl.BlockSpec(shape, lambda *_: (0,) * len(shape))


def columns(rows, width, offset=0):
    return pl.BlockSpec((rows, width), lambda i, *_: (0, i + offset))


def rows_of(height, width, at):
    return pl.BlockSpec((height, width), lambda i, *_: (i, at // width))


def shaped(shape, dtype):
    return jax.ShapeDtypeStruct(shape, dtype)


def call(kernel, grid, in_specs, out_specs, outs, scratch, flops, moved, *args):
    return pl.pallas_call(
        kernel,
        grid_spec=pltpu.PrefetchScalarGridSpec(
            num_scalar_prefetch=1,
            grid=grid,
            in_specs=in_specs,
            out_specs=out_specs,
            scratch_shapes=scratch,
        ),
        out_shape=outs,
        compiler_params=pltpu.CompilerParams(
            vmem_limit_bytes=VMEM_BYTES,
            dimension_semantics=("arbitrary",) * len(grid),
        ),
        cost_estimate=pl.CostEstimate(flops=flops, bytes_accessed=moved, transcendentals=0),
    )(*args)


def self_forward(lens, tok, early, pk, pv):
    rows, width = tok.shape
    steps = width // GROUP
    return call(
        self_forward_kernel,
        (steps,),
        [
            whole((rows, width)),
            columns(width, GROUP),
            columns(width, GROUP, steps),
            columns(width, GROUP, 2 * steps),
            columns(PREFIX_PAD, GROUP),
            columns(PREFIX_PAD, GROUP),
        ],
        [columns(rows, GROUP)] * 4,
        [shaped((rows, width), BF)] * 4,
        [],
        2 * rows * width * width * 3,
        14 * width * width,
        lens, tok, early, early, early, pk, pv,
    )


def cross_forward(lens, mem, late, tok, att, norms):
    rows, width = tok.shape
    steps = width // GROUP
    places = mem.shape[0]
    return call(
        cross_forward_kernel,
        (steps,),
        [
            whole((places, width)),
            columns(width, GROUP, KV_AT // GROUP),
            columns(width, GROUP, KV_AT // GROUP + steps),
            whole((rows, width)),
            whole((rows, width)),
            square(width, SOUT_AT),
            square(width, CQ_AT),
            whole(norms.shape),
        ],
        [columns(places, GROUP)] * 2
        + [whole((rows, width)), whole((rows, width)), whole((rows, 1)), columns(rows, GROUP)],
        [shaped((places, width), BF)] * 2
        + [shaped((rows, width), BF), shaped((rows, width), F32), shaped((rows, 1), F32)]
        + [shaped((rows, width), BF)],
        [],
        2 * width * width * (2 * rows + 2 * places),
        16 * width * width,
        lens, mem, late, late, tok, att, late, late, norms,
    )


def ffn(lens, nrm1, att, cot, late, down, db, up, ub, norms):
    rows, width = nrm1.shape
    hidden = SPREAD * width
    adapt = down.shape[1]
    block = FFN_BLOCK
    steps = hidden // block
    return call(
        ffn_kernel,
        (2, steps),
        [
            whole((rows, width)),
            whole((rows, width)),
            square(width, OUT_AT),
            ANYWHERE,
            pl.BlockSpec((width, block), lambda p, j, *_: (0, j + IN_AT // block)),
            pl.BlockSpec((block // SPREAD, SPREAD * width), lambda p, j, *_: (j, FF_AT)),
            ANYWHERE,
            whole((1, adapt)),
            ANYWHERE,
            whole((1, width)),
            whole(norms.shape),
        ],
        [ANYWHERE, whole((rows, width)), ANYWHERE],
        [
            shaped((rows, width), BF),
            shaped((rows, width), F32),
            shaped((width, 2 * adapt + PAIR), BF),
        ],
        [
            pltpu.VMEM((rows, width), F32),
            pltpu.VMEM((rows, 1), F32),
            pltpu.VMEM((rows, width), F32),
            pltpu.VMEM((rows, width), BF),
            pltpu.VMEM((steps, rows, block), BF),
            pltpu.VMEM((rows, adapt), BF),
            pltpu.VMEM((rows, adapt), BF),
            pltpu.VMEM((rows, width), BF),
            pltpu.VMEM((rows, width), BF),
            pltpu.VMEM((width, adapt), BF),
            pltpu.VMEM((adapt, width), BF),
            pltpu.VMEM((rows, width), BF),
            pltpu.VMEM((width, 2 * adapt + PAIR), BF),
            pltpu.SemaphoreType.DMA((5,)),
        ],
        2 * rows * width * (4 * hidden + 6 * adapt),
        8 * width * hidden,
        lens, nrm1, att, late, cot, late, late, down, db, up, ub, norms,
    )


def cross_backward(lens, gtwo, late, cq, mk, mv, nrm1, inv1, norms, parts):
    rows, width = cq.shape
    steps = width // GROUP
    places = mk.shape[0]
    seqs = lens.shape[0]
    sent = (parts, seqs, places // seqs // parts, width)
    return call(
        cross_backward_kernel,
        (steps,),
        [
            whole((rows, width)),
            rows_of(GROUP, width, OUT_AT),
            columns(rows, GROUP),
            columns(places, GROUP),
            columns(places, GROUP),
            columns(width, GROUP, KV_AT // GROUP),
            columns(width, GROUP, KV_AT // GROUP + steps),
            ANYWHERE,
            ANYWHERE,
            whole((rows, 1)),
            whole(norms.shape),
        ],
        [whole(sent), whole((rows, width)), whole((rows, width))],
        [shaped(sent, BF), shaped((rows, width), F32), shaped((rows, width), BF)],
        [
            pltpu.VMEM((rows, width), BF),
            pltpu.VMEM((places, width), F32),
            pltpu.VMEM((places, GROUP), BF),
            pltpu.VMEM((places, GROUP), BF),
            pltpu.VMEM((rows, width), BF),
            pltpu.VMEM((width, width), BF),
            pltpu.VMEM((rows, width), F32),
            pltpu.SemaphoreType.DMA((2,)),
        ],
        2 * width * width * (rows + 2 * places),
        14 * width * width,
        lens, gtwo, late, cq, mk, mv, late, late, late, nrm1, inv1, norms,
    )


def self_backward(lens, gone_low, late, q, k, v, pk, pv):
    rows, width = q.shape
    steps = width // GROUP
    return call(
        self_backward_kernel,
        (steps,),
        [whole((rows, width)), rows_of(GROUP, width, SOUT_AT)]
        + [columns(rows, GROUP)] * 3
        + [columns(PREFIX_PAD, GROUP)] * 2,
        [columns(rows, GROUP)] * 3 + [pl.BlockSpec((GROUP, PAIR), lambda i, *_: (i, 0))],
        [shaped((rows, width), BF)] * 3 + [shaped((width, PAIR), F32)],
        [],
        2 * rows * width * width * 4,
        20 * width * width,
        lens, gone_low, late, q, k, v, pk, pv,
    )


def input_gradient(gone, dq, dk, dv, early, arrived):
    rows, width = gone.shape

    def part(index):
        return pl.BlockSpec((GROUP, width), lambda i: (i, index))

    return pl.pallas_call(
        input_grad_kernel,
        grid=(width // GROUP,),
        in_specs=[pl.BlockSpec((rows, GROUP), lambda i: (0, i))]
        + [whole((rows, width))] * 3
        + [part(0), part(1), part(2), pl.BlockSpec(memory_space=pltpu.VMEM)],
        out_specs=[pl.BlockSpec((rows, GROUP), lambda i: (0, i)), ANYWHERE],
        out_shape=[shaped((rows, width), BF), shaped(arrived.shape, arrived.dtype)],
        scratch_shapes=[pltpu.SemaphoreType.DMA((1,))],
        compiler_params=pltpu.CompilerParams(
            vmem_limit_bytes=VMEM_BYTES, dimension_semantics=("arbitrary",)
        ),
        cost_estimate=pl.CostEstimate(
            flops=6 * rows * width * width, bytes_accessed=12 * width * width, transcendentals=0
        ),
    )(gone, dq, dk, dv, early, early, early, arrived)


def around(count, by):
    return [(i, (i + by) % count) for i in range(count)]


def ring_gather(shard, other):
    rows = shard.shape[0]
    half = rows // 2
    count = lax.axis_size("dp_0")
    x, core = lax.axis_index("dp_0"), lax.axis_index("dp_1")
    below = lax.ppermute(shard, "dp_0", around(count, 1))
    above = lax.ppermute(shard, "dp_0", around(count, -1))
    filled = jnp.zeros((count * 2 * rows, shard.shape[1]), shard.dtype)
    filled, other = lax.optimization_barrier((filled, other))
    far_low = lax.ppermute(below[:half], "dp_0", around(count, 1))
    far_high = lax.ppermute(above[half:], "dp_0", around(count, -1))
    for piece, offset, start in (
        (shard, 0, 0), (below, -1, 0), (above, 1, 0), (far_low, 2, 0), (far_high, 2, half),
    ):
        swapped = lax.ppermute(piece, "dp_1", around(2, 1))
        chip = (x + offset + count) % count
        for part, place in ((piece, core), (swapped, 1 - core)):
            at = (chip * 2 + place) * rows + start
            filled = lax.dynamic_update_slice_in_dim(filled, part, at, 0)
    return filled, other


def scatter_sum(blocks):
    count = lax.axis_size("dp_0")
    x, core = lax.axis_index("dp_0"), lax.axis_index("dp_1")
    by_core = blocks.reshape(count, 2, *blocks.shape[1:])
    kept = lax.dynamic_index_in_dim(by_core, core, 1, keepdims=False)
    given = lax.dynamic_index_in_dim(by_core, 1 - core, 1, keepdims=False)
    paired = kept + lax.ppermute(given, "dp_1", around(2, 1))
    total = lax.dynamic_index_in_dim(paired, x, 0, keepdims=False)
    for by in range(1, count):
        sent = lax.dynamic_index_in_dim(paired, (x + by) % count, 0, keepdims=False)
        total = total + lax.ppermute(sent, "dp_0", around(count, by))
    return total


def local(
    tokens, memory, cotangent, tgt_len, src_len,
    self_qkv, self_out, cross_q, cross_kv, cross_out, ffn_in, ffn_out,
    first_gain, first_bias, second_gain, second_bias, third_gain, third_bias,
    prefix_key, prefix_value, down_weight, down_bias, up_weight, up_bias,
):
    mem_groups = lax.axis_size(MEM)
    mem_place = lax.axis_index(MEM)
    seqs, tgt, width = tokens.shape
    src_block = memory.shape[1]
    prefix = prefix_key.shape[0]

    high = cross_out.shape[0] // mem_groups
    mine = functools.partial(
        lax.dynamic_slice_in_dim, start_index=mem_place * high, slice_size=high
    )
    spread = mine(ffn_out.reshape(SPREAD, -1, width), axis=1)
    late = lax.all_gather(
        jnp.concatenate(
            [jnp.moveaxis(spread, 0, 1).reshape(high, SPREAD * width)]
            + [mine(w, axis=0) for w in (ffn_in, cross_out, self_out, cross_q, cross_kv)],
            axis=1,
        ),
        DP_MEM, axis=0, tiled=True,
    )
    early, memory = ring_gather(self_qkv, memory)
    mem_rows = lax.all_to_all(memory, MEM, split_axis=0, concat_axis=1, tiled=True)
    mem_rows = mem_rows.reshape(-1, width)
    own_src = lax.dynamic_slice_in_dim(src_len, mem_place * seqs, seqs, 0)

    tok = tokens.reshape(seqs * tgt, width)
    cot = cotangent.reshape(seqs * tgt, width)
    pk = jnp.pad(prefix_key, ((0, PREFIX_PAD - prefix), (0, 0)))
    pv = jnp.pad(prefix_value, ((0, PREFIX_PAD - prefix), (0, 0)))

    q, k, v, att = self_forward(tgt_len, tok, early, pk, pv)
    vectors = jnp.stack(
        [first_gain, first_bias, second_gain, second_bias, third_gain, third_bias]
        + [third_bias] * 2
    )
    vectors, att = lax.optimization_barrier((vectors, att))
    norms = lax.all_gather(vectors, DP, axis=1, tiled=True).astype(F32)
    mk, mv, cq, nrm1, inv1, cross = cross_forward(own_src, mem_rows, late, tok, att, norms)
    output, gtwo, adapter = ffn(
        tgt_len, nrm1, cross, cot, late,
        down_weight, down_bias.astype(F32)[None], up_weight, up_bias.astype(F32)[None], norms,
    )
    adapter = lax.psum_scatter(adapter, DP, scatter_dimension=0, tiled=True)

    dmem, gone, gone_low = cross_backward(
        own_src, gtwo, late, cq, mk, mv, nrm1, inv1, norms, mem_groups
    )
    memory_grad = lax.all_to_all(dmem, MEM, split_axis=0, concat_axis=0, tiled=True)
    dq, dk, dv, small = self_backward(tgt_len, gone_low, late, q, k, v, pk, pv)
    small = scatter_sum(small.reshape(lax.axis_size(DP), -1, PAIR))
    dq, small, memory_grad = lax.optimization_barrier((dq, small, memory_grad))
    memory_grad = memory_grad.reshape(memory.shape)
    din, memory_grad = input_gradient(gone, dq, dk, dv, early, memory_grad)
    adapt = down_weight.shape[1]
    joined = (adapter.astype(F32) + jnp.pad(small, ((0, 0), (2 * adapt, 0)))).astype(BF)
    arrived = lax.all_to_all(
        joined.reshape(mem_groups, -1, joined.shape[1]),
        MEM, split_axis=0, concat_axis=0, tiled=True,
    )
    down_grad, up_grad, last = (
        jnp.sum(arrived[..., a:b].astype(F32), axis=0)
        for a, b in ((0, adapt), (adapt, 2 * adapt), (2 * adapt, joined.shape[1]))
    )
    return (
        output.reshape(tokens.shape),
        din.reshape(tokens.shape),
        memory_grad,
        last[:, :prefix].T,
        last[:, PREFIX_PAD : PREFIX_PAD + prefix].T,
        down_grad,
        last[:BIAS_ROWS, 2 * PREFIX_PAD + 1],
        up_grad.T,
        last[:, 2 * PREFIX_PAD],
    )


def solution(mesh):
    torus = Mesh(mesh.devices.reshape(4, 2, 4, 4), ("dp_0", "dp_1", "mem_0", "mem_1"))
    by_dp = P(DP, None)
    copied = P(None)
    return jax.shard_map(
        local,
        mesh=torus,
        in_specs=(
            P(DP_MEM, None, None), P(DP, MEM, None), P(DP_MEM, None, None), P(DP_MEM), P(DP),
            by_dp, by_dp, by_dp, by_dp, by_dp, by_dp, by_dp,
            P(DP), P(DP), P(DP), P(DP), P(DP), P(DP),
            copied, copied, copied, copied, copied, copied,
        ),
        out_specs=(
            P(DP_MEM, None, None),
            P(DP_MEM, None, None),
            P(DP, MEM, None),
            P(None, DP_MEM),
            P(None, DP_MEM),
            P(DP_MEM, None),
            P(DP_MEM),
            P(None, DP_MEM),
            P(DP_MEM),
        ),
        check_vma=False,
    )
```
